32 devices in a mesh: rep: 4 (over x, core), fsdp: 8 (over z, y).
Axes of the slice: x: 2, y: 2, z: 4, core: 2. Of those that a mesh axis runs over, the one named last changes fastest.
Arguments:
- hidden: bfloat16 [17408, 768], P(('rep', 'fsdp')), may hold values from -6 to 6
- region_counts: int32 [64], P(('rep', 'fsdp')), may hold values from 10 to 100, as said below
- w_qkv: bfloat16 [2, 768, 2304], P(None, 'fsdp'), may hold values from -0.21875 to 0.21875
- w_out: bfloat16 [2, 768, 768], P(None, 'fsdp'), may hold values from -0.875 to 0.875
- w_up: bfloat16 [2, 768, 3072], P(None, 'fsdp'), may hold values from -0.21875 to 0.21875
- w_down: bfloat16 [2, 3072, 768], P(None, 'fsdp'), may hold values from -0.109375 to 0.109375
- bias_up: bfloat16 [2, 3072], P(None, 'fsdp'), may hold values from -1.1953125 to 1.1953125
- biases: bfloat16 [2, 6, 768], P(None, None, 'fsdp'), may hold values from -1.1953125 to 1.1953125
- norm_gains: bfloat16 [2, 2, 768], P(None, None, 'fsdp'), may hold values from 0.5 to 1.5
- cotangent: bfloat16 [17408, 768], P(('rep', 'fsdp')), may hold values from -6 to 6
Outputs:
- output: bfloat16 [17408, 768], P(('rep', 'fsdp'))
- grad_hidden: float32 [17408, 768], P(('rep', 'fsdp'))
- grad_w_qkv: float32 [2, 768, 2304], P(None, 'fsdp')
- grad_w_out: float32 [2, 768, 768], P(None, 'fsdp')
- grad_w_up: float32 [2, 768, 3072], P(None, 'fsdp')
- grad_w_down: float32 [2, 3072, 768], P(None, 'fsdp')
- grad_bias_up: float32 [2, 3072], P(None, 'fsdp')
- grad_biases: float32 [2, 6, 768], P(None, None, 'fsdp')
- grad_norm_gains: float32 [2, 2, 768], P(None, None, 'fsdp')
The draws below stay inside these ranges and needn't reach their ends.
Inputs may be any that keep to these rules, and one draw needn't show every extreme that they name: `region_counts`: each sequence's count of valid region slots; 10 and 100 are both reached in every draw, so region slots from 228 on are never valid.
All inputs are finite; a program needn't handle non-finite values.
Results may differ from the reference program's by a relative error of at most 0.023.
Values may be sent and summed in bfloat16 or wider, within the bound.
No kernel may reach another device: no remote copies, remote signals or barrier semaphores. Data moves between devices by JAX's collectives and lax.ppermute only.
A program may use at most 256 MiB of HBM per device.

```python
import jax
import jax.numpy as jnp
from jax import lax

D = 768
HEADS = 12
HEAD_DIM = 64
FF = 3072
LAYERS = 2
TEXT = 128
REGION_MOST = 100
REGION_LEAST = 10
SLOTS = 272
SEQS = 64
TOKENS = 17408


def draw_region_counts(key, part):
    key = jax.random.fold_in(key, 7)
    key_counts, key_top, key_bottom = jax.random.split(key, 3)
    counts = jax.random.randint(key_counts, (SEQS,), REGION_LEAST, REGION_MOST + 1)
    top_at = jax.random.randint(key_top, (), 0, SEQS)
    bottom_at = (top_at + jax.random.randint(key_bottom, (), 1, SEQS)) % SEQS
    positions = jnp.arange(SEQS)
    counts = jnp.where(positions == top_at, REGION_MOST, counts)
    counts = jnp.where(positions == bottom_at, REGION_LEAST, counts)
    return counts.astype(jnp.int32)


def steps_of(rng, dims, cuts, smallest, high):
    gain, own = 1.0, jax.random.fold_in(rng, 6)
    for axis_at, parts in cuts:
        draws = jnp.exp(jax.random.uniform(jax.random.fold_in(own, axis_at), (parts,), jnp.float32, smallest / len(cuts), high / len(cuts)))
        gain = gain * jnp.repeat(draws, dims[axis_at] // parts).reshape([-1 if axis == axis_at else 1 for axis in range(len(dims))])
    return gain


def bell_draw(own_key, dims, spread, limit, cuts=(), kind=jnp.bfloat16):
    level = steps_of(own_key, dims, cuts, -0.22, 0.18) if cuts else 1.0
    values = jax.random.normal(own_key, dims, jnp.float32) * spread * level
    return jnp.minimum(jnp.maximum(values, -limit), limit).astype(kind)


def setup_inputs(seed: int = 0) -> dict:
    splits = jax.random.split(jax.random.key(seed), 11)
    return {
        "hidden": bell_draw(splits[0], (TOKENS, D), 1.0, 6.0, ((0, 32),)),
        "region_counts": draw_region_counts(jax.random.fold_in(splits[10], 71), 0),
        "w_qkv": bell_draw(splits[2], (LAYERS, D, 3 * D), D ** -0.5, 0.21875, ((1, 8),)),
        "w_out": bell_draw(splits[3], (LAYERS, D, D), (D // 16) ** -0.5, 0.875, ((1, 8),)),
        "w_up": bell_draw(splits[4], (LAYERS, D, FF), D ** -0.5, 0.21875, ((1, 8),)),
        "w_down": bell_draw(splits[5], (LAYERS, FF, D), FF ** -0.5, 0.109375, ((1, 8),)),
        "bias_up": bell_draw(splits[6], (LAYERS, FF), 0.2, 1.1953125, ((1, 8),)),
        "biases": bell_draw(splits[7], (LAYERS, 6, D), 0.2, 1.1953125, ((2, 8),)),
        "norm_gains": jnp.clip(1.0 + 0.1 * jax.random.normal(splits[8], (LAYERS, 2, D), jnp.float32), 0.5, 1.5).astype(jnp.bfloat16),
        "cotangent": bell_draw(splits[9], (TOKENS, D), 1.0, 6.0, ((0, 32),)),
    }


@jax.custom_vjp
def low(v):
    return lax.optimization_barrier(v.astype(jnp.bfloat16)).astype(jnp.float32)

@jax.custom_vjp
def low_back(v):
    return v

def low_keep(v):
    return (low(v), None)

def low_pass(kept, grad):
    return (grad,)

def back_keep(v):
    return (v, None)

def back_low(kept, grad):
    return (low(grad),)
low.defvjp(low_keep, low_pass)
low_back.defvjp(back_keep, back_low)
HIGHEST = lax.Precision.HIGHEST
EPSILON = 1e-12
MASKED = -1000000000.0

def layer_norm(states, gain_row, shift_row):
    row_mean = lax.optimization_barrier(jnp.mean(states, axis=-1, keepdims=True))
    centered = states - row_mean
    variance = lax.optimization_barrier(jnp.mean(centered * centered, axis=-1, keepdims=True))
    return centered * lax.rsqrt(variance + EPSILON) * gain_row + shift_row

def one_layer(states, w_qkv, w_out, w_up, w_down, bias_up, biases, norm_gains, valid_keys):
    seq_count = valid_keys.shape[0]
    qkv_bias = jnp.concatenate([biases[0], jnp.zeros_like(biases[0]), biases[1]])
    projected = jnp.dot(low(states), w_qkv, precision=HIGHEST) + qkv_bias
    projected = low(low_back(projected))
    heads_view = projected.reshape(seq_count, SLOTS, 3, HEADS, HEAD_DIM)
    queries = heads_view[:, :, 0]
    key_rows = heads_view[:, :, 1]
    values = heads_view[:, :, 2]
    scores = jnp.einsum('sqhd,skhd->shqk', queries, key_rows, precision=HIGHEST) * HEAD_DIM ** (-0.5)
    scores = jnp.where(valid_keys[:, None, None, :], scores, MASKED)
    scores = low_back(scores)
    soft_weights = low(jax.nn.softmax(scores, axis=-1))
    context = jnp.einsum('shqk,skhd->sqhd', soft_weights, values, precision=HIGHEST)
    context = low(low_back(context.reshape(seq_count * SLOTS, D)))
    attended = low_back(jnp.dot(context, w_out, precision=HIGHEST) + biases[2])
    first = layer_norm(states + attended, norm_gains[0], biases[3])
    hidden_pre = low_back(jnp.dot(low(first), w_up, precision=HIGHEST) + bias_up)
    activated = low(jax.nn.gelu(hidden_pre, approximate=False))
    branch_out = low_back(jnp.dot(activated, w_down, precision=HIGHEST) + biases[4])
    return layer_norm(first + branch_out, norm_gains[1], biases[5])

def forward_layers(states, w_qkv, w_out, w_up, w_down, bias_up, biases, norm_gains, valid_keys):
    for layer_index in range(LAYERS):
        states = one_layer(states, w_qkv[layer_index], w_out[layer_index], w_up[layer_index], w_down[layer_index], bias_up[layer_index], biases[layer_index], norm_gains[layer_index], valid_keys)
    return states

def reference(hidden, region_counts, w_qkv, w_out, w_up, w_down, bias_up, biases, norm_gains, cotangent):
    group_size = max((size_try for size_try in range(1, 16) if SEQS % size_try == 0 and size_try * SLOTS <= 4096))
    group_count = SEQS // group_size
    params = tuple((weight.astype(jnp.float32) for weight in (w_qkv, w_out, w_up, w_down, bias_up, biases, norm_gains)))
    hidden_groups = hidden.reshape(group_count, group_size * SLOTS, D)
    cot_groups = cotangent.reshape(group_count, group_size * SLOTS, D)
    count_groups = region_counts.reshape(group_count, group_size)
    slot_index = jnp.arange(SLOTS)

    def group_step(totals, item):
        hidden_part, cot_part, count_part = item
        valid_keys = (slot_index[None, :] < TEXT) | (slot_index[None, :] - TEXT < count_part[:, None])

        def forward_group(states, *weights):
            return forward_layers(states, *weights, valid_keys)
        result, pull_back = jax.vjp(forward_group, hidden_part.astype(jnp.float32), *params)
        grads = pull_back(cot_part.astype(jnp.float32))
        totals = tuple((total + grad_part for total, grad_part in zip(totals, grads[1:])))
        return (totals, (result.astype(jnp.bfloat16), grads[0]))
    initial = tuple((jnp.zeros_like(weight) for weight in params))
    totals, (results, input_grads) = lax.scan(group_step, initial, (hidden_groups, cot_groups, count_groups))
    return (results.reshape(TOKENS, D), input_grads.reshape(TOKENS, D), totals[0], totals[1], totals[2], totals[3], totals[4], totals[5], totals[6])
```

```python
import functools

import jax
import jax.numpy as jnp
from jax import lax
from jax.experimental import pallas as pl
from jax.experimental.pallas import tpu as pltpu
from jax.sharding import PartitionSpec as P

HEADS = 12
HEAD_DIM = 64
LAYERS = 2
TEXT = 128
KEYS = 256
WIDE = 768
HALF = WIDE // 2
PAIR = 2 * HEAD_DIM
PAIRS = HEADS // 2
EPSILON = 1e-12
MASKED = -1000000000.0
AXES = ("rep", "fsdp")
VMEM_LIMIT = 60 * 1024 * 1024


def low(value):
    return value.astype(jnp.bfloat16)


def full(value):
    return value.astype(jnp.float32)


def mm(left, right):
    return jnp.dot(left, right, preferred_element_type=jnp.float32)


def mm_t(left, right):
    return lax.dot_general(
        left, right, (((1,), (1,)), ((), ())), preferred_element_type=jnp.float32
    )


def t_mm(left, right):
    return lax.dot_general(
        left, right, (((0,), (0,)), ((), ())), preferred_element_type=jnp.float32
    )


def flip(at, by):
    return 1 - at if by else at


class Place:
    def __init__(self, pos_ref, depth):
        self.core, self.side = pos_ref[0], pos_ref[1]
        self.row, self.level = pos_ref[2], pos_ref[3]
        self.depth = depth

    def shard(self, far_row, far_level):
        return lax.rem(self.level + self.depth - far_level, self.depth) * 2 + flip(
            self.row, far_row
        )

    def far_level(self, level):
        return lax.rem(self.level + self.depth - level, self.depth)


def half_lanes(at):
    return pl.ds(pl.multiple_of(at * HALF, HALF), HALF)


def load_unit(place, own, other, whole, sem, by_rows, side_first):
    for far_core, part in ((0, own), (1, other)):
        core = flip(place.core, far_core)
        for first in range(2):
            for second in range(2):
                far_side, far_row = (second, first) if side_first else (first, second)
                side = flip(place.side, far_side)
                for far_level in range(place.depth):
                    shard = place.shard(far_row, far_level)
                    blocks = pl.ds(side * 2, 2)
                    if by_rows:
                        target = whole.at[shard, blocks, :, half_lanes(core)]
                    else:
                        target = whole.at[blocks, shard, :, half_lanes(core)]
                    pltpu.make_async_copy(
                        part.at[first, second, far_level], target, sem
                    ).start()


def wait_all(ref, sem):
    pltpu.make_async_copy(ref, ref, sem).wait()


def store_columns(place, block, held, out, sem, side_first):
    far_side = place.side if block // 2 == 0 else 1 - place.side
    for far_core in range(2):
        core = flip(place.core, far_core)
        for far_row in range(2):
            for far_level in range(place.depth):
                shard = place.shard(far_row, far_level)
                at = (far_side, far_row) if side_first else (far_row, far_side)
                pltpu.make_async_copy(
                    held.at[shard, :, half_lanes(core)],
                    out.at[far_core, at[0], at[1], far_level, block % 2],
                    sem,
                ).start()


def store_rows(place, tile, held, out, sem, side_first):
    count = held.shape[0]
    for inner in range(count):
        shard = tile * count + inner
        far_row = place.row if shard % 2 == 0 else 1 - place.row
        far_level = place.far_level(shard // 2)
        for block in range(4):
            far_side = place.side if block // 2 == 0 else 1 - place.side
            at = (far_side, far_row) if side_first else (far_row, far_side)
            for half in range(2):
                far_core = place.core if half == 0 else 1 - place.core
                pltpu.make_async_copy(
                    held.at[inner, block, :, pl.ds(half * HALF, HALF)],
                    out.at[far_core, at[0], at[1], far_level, block % 2],
                    sem,
                ).start()


def chunks(rows):
    size = rows // 4 if rows % 64 == 0 or (rows // 4) % 8 == 0 else rows
    return [(start, size) for start in range(0, rows, size)]


def normalize(value):
    centered = value - jnp.mean(value, axis=-1, keepdims=True)
    scale = lax.rsqrt(jnp.mean(centered * centered, axis=-1, keepdims=True) + EPSILON)
    return centered * scale, scale


def norm_backward(grad, hat, scale, gain):
    direct = grad * gain
    return (
        direct
        - jnp.mean(direct, axis=-1, keepdims=True)
        - hat * jnp.mean(direct * hat, axis=-1, keepdims=True)
    ) * scale


def gelu_and_slope(value):
    size = jnp.abs(value) * 0.7071067811865476
    t = 1.0 / (1.0 + 0.3275911 * size)
    series = t * (
        0.127414796
        + t * (-0.142248368 + t * (0.7107068705 + t * (-0.7265760135 + t * 0.5307027145)))
    )
    bell = jnp.exp(-0.5 * value * value)
    tail = series * bell
    below = jnp.where(value >= 0, 1.0 - tail, tail)
    return value * below, below + value * bell * 0.3989422804014327


def attention_forward(
    depth, side_first, seqs, pos_ref, counts_ref, x_ref, own_ref, other_ref,
    qkv_bias_ref, out_bias_ref, gain_ref, shift_ref,
    first_ref, hat_ref, scale_ref, x_t_ref, ctx_t_ref, first_t_ref, qkv_ref, probs_ref,
    weight, ctx, held, weight_sem, held_sem,
):
    place = Place(pos_ref, depth)
    load_unit(place, own_ref, other_ref, weight, weight_sem, False, side_first)
    tokens = x_ref.shape[0]
    slots = tokens // seqs
    x_low = low(x_ref[...])
    x_t_ref[...] = x_low.T
    wait_all(weight, weight_sem)
    for block in range(3):
        out = mm(x_low, weight[block].reshape(WIDE, WIDE))
        out = low(out + qkv_bias_ref[:, block * WIDE : (block + 1) * WIDE])
        for pair in range(PAIRS):
            qkv_ref[block * PAIRS + pair] = out[:, pair * PAIR : (pair + 1) * PAIR]
    lane = lax.broadcasted_iota(jnp.int32, (KEYS, PAIR), 1)
    key = lax.broadcasted_iota(jnp.int32, (slots, KEYS), 1)
    for seq in range(seqs):
        valid = key < TEXT + counts_ref[seq]

        def pair_step(pair, carry, seq=seq, valid=valid):
            start = seq * slots
            slot = lax.rem(pair, 2)
            q = qkv_ref[pair, start : start + slots, :] * jnp.bfloat16(HEAD_DIM**-0.5)
            k = qkv_ref[PAIRS + pair, start : start + KEYS, :]
            v = qkv_ref[2 * PAIRS + pair, start : start + KEYS, :]
            none = jnp.zeros_like(k)
            k_both = jnp.concatenate(
                [jnp.where(lane < HEAD_DIM, k, none), jnp.where(lane < HEAD_DIM, none, k)], 0
            )
            v_both = jnp.concatenate(
                [jnp.where(lane < HEAD_DIM, v, none), jnp.where(lane < HEAD_DIM, none, v)], 0
            )
            scores = mm_t(q, k_both)
            halves = []
            for half in range(2):
                part = jnp.where(valid, scores[:, half * KEYS : (half + 1) * KEYS], MASKED)
                part = jnp.exp(part - jnp.max(part, axis=-1, keepdims=True))
                halves.append(low(part / jnp.sum(part, axis=-1, keepdims=True)))
            probs = jnp.concatenate(halves, 1)

            @pl.when(pair >= 2)
            def _():
                wait_all(held.at[slot], held_sem.at[slot])

            held[slot] = probs
            pltpu.make_async_copy(
                held.at[slot], probs_ref.at[seq, pair], held_sem.at[slot]
            ).start()
            ctx[pair, start : start + slots, :] = low(mm(probs, v_both))
            return carry

        lax.fori_loop(0, PAIRS, pair_step, 0)
        for slot in range(2):
            wait_all(held.at[slot], held_sem.at[slot])
    context = jnp.concatenate([ctx[pair] for pair in range(PAIRS)], 1)
    ctx_t_ref[...] = context.T
    first_ref[...] = mm(context, weight[3].reshape(WIDE, WIDE))
    for start, size in chunks(tokens):
        rows = pl.ds(start, size)
        hat, scale = normalize(full(x_ref[rows, :]) + (first_ref[rows, :] + out_bias_ref[...]))
        hat_ref[rows, :] = hat
        scale_ref[rows, :] = jnp.broadcast_to(scale, (size, 128))
        first_ref[rows, :] = hat * gain_ref[...] + shift_ref[...]
    first_t_ref[...] = low(first_ref[...]).T


def mlp_forward(
    depth, up_side_first, down_side_first, pos_ref, first_ref, up_own_ref, up_other_ref, down_own_ref, down_other_ref,
    up_bias_ref, down_bias_ref, gain_ref, shift_ref,
    out_ref, hat_ref, scale_ref, act_t_ref, slope_ref,
    up, down, pre, act, act_t, slope, up_sem, down_sem, act_sem, slope_sem,
):
    place = Place(pos_ref, depth)
    load_unit(place, up_own_ref, up_other_ref, up, up_sem, False, up_side_first)
    load_unit(place, down_own_ref, down_other_ref, down, down_sem, True, down_side_first)
    tokens = first_ref.shape[0]
    first_low = low(first_ref[...])
    shards = down.shape[0] // 4
    wait_all(up, up_sem)
    total = None
    for tile in range(4):
        slot = tile % 2
        pre[...] = mm(first_low, up[tile].reshape(WIDE, WIDE))
        if tile >= 2:
            wait_all(slope.at[slot], slope_sem.at[slot])
            wait_all(act_t.at[slot], act_sem.at[slot])

        def row_step(step, carry, tile=tile, slot=slot):
            rows = pl.ds(pl.multiple_of(step * 32, 32), 32)
            value = pre[rows, :] + up_bias_ref[:, tile * WIDE : (tile + 1) * WIDE]
            gelu, rise = gelu_and_slope(value)
            act[rows, :] = low(gelu)
            slope[slot, rows, :] = low(rise)
            return carry

        lax.fori_loop(0, tokens // 32, row_step, 0)
        pltpu.make_async_copy(slope.at[slot], slope_ref.at[tile], slope_sem.at[slot]).start()
        act_t[slot] = act[...].T
        pltpu.make_async_copy(act_t.at[slot], act_t_ref.at[tile], act_sem.at[slot]).start()
        if tile == 0:
            wait_all(down, down_sem)
        part = mm(act[...], down[tile * shards : (tile + 1) * shards].reshape(WIDE, WIDE))
        if tile == 0:
            out_ref[...] = part
        else:
            out_ref[...] += part
    for start, size in chunks(tokens):
        rows = pl.ds(start, size)
        hat, scale = normalize(first_ref[rows, :] + out_ref[rows, :] + down_bias_ref[...])
        hat_ref[rows, :] = hat
        scale_ref[rows, :] = jnp.broadcast_to(scale, (size, 128))
        out_ref[rows, :] = hat * gain_ref[...] + shift_ref[...]
    for slot in range(2):
        wait_all(slope.at[slot], slope_sem.at[slot])
        wait_all(act_t.at[slot], act_sem.at[slot])


def norm_step(grad_ref, hat_ref, scale_ref, gain_ref, out_ref, gain_grad_ref, shift_grad_ref, bias_grad_ref):
    sums = [0.0, 0.0, 0.0]
    for start, size in chunks(grad_ref.shape[0]):
        rows = pl.ds(start, size)
        grad, hat = full(grad_ref[rows, :]), hat_ref[rows, :]
        grad_in = norm_backward(grad, hat, scale_ref[rows, :][:, :1], gain_ref[...])
        out_ref[rows, :] = grad_in
        for at, value in enumerate((grad * hat, grad, full(low(grad_in)))):
            sums[at] += jnp.sum(value, axis=0, keepdims=True)
    gain_grad_ref[...], shift_grad_ref[...], bias_grad_ref[...] = sums


def down_backward(
    depth, side_first, pos_ref, grad_ref, hat_ref, scale_ref, gain_ref, act_t_ref,
    second_ref, gain_grad_ref, shift_grad_ref, bias_grad_ref, out_ref,
    act_t, held, act_sem, held_sem,
):
    place = Place(pos_ref, depth)
    pltpu.make_async_copy(act_t_ref, act_t, act_sem).start()
    norm_step(
        grad_ref, hat_ref, scale_ref, gain_ref, second_ref, gain_grad_ref, shift_grad_ref, bias_grad_ref
    )
    grad_low = low(second_ref[...])
    wait_all(act_t, act_sem)
    for tile in range(4):
        slot = tile % 2
        if tile >= 2:
            wait_all(held.at[slot], held_sem.at[slot])
        held[slot] = low(mm(act_t[tile], grad_low)).reshape(held.shape[1:])
        store_rows(place, tile, held.at[slot], out_ref, held_sem.at[slot], side_first)
    for slot in range(2):
        wait_all(held.at[slot], held_sem.at[slot])


def up_backward(
    depth, up_side_first, down_side_first, out_side_first, pos_ref, second_ref, up_own_ref, up_other_ref, down_own_ref,
    down_other_ref, slope_ref, first_t_ref, hat_ref, scale_ref, gain_ref,
    first_in_ref, gain_grad_ref, shift_grad_ref, bias_grad_ref, up_grad_ref, out_ref,
    up, down, slope, total, held, up_sem, down_sem, slope_sem, held_sem,
):
    place = Place(pos_ref, depth)
    load_unit(place, down_own_ref, down_other_ref, down, down_sem, True, down_side_first)
    load_unit(place, up_own_ref, up_other_ref, up, up_sem, False, up_side_first)
    pltpu.make_async_copy(slope_ref, slope, slope_sem).start()
    shards = down.shape[0] // 4
    grad_low = low(second_ref[...])
    first_t = first_t_ref[...]
    total[...] = second_ref[...]
    wait_all(down, down_sem)
    wait_all(slope, slope_sem)
    wait_all(up, up_sem)
    for tile in range(4):
        slot = tile % 2
        grad = mm_t(grad_low, down[tile * shards : (tile + 1) * shards].reshape(WIDE, WIDE))
        grad = low(grad * full(slope[tile]))
        up_grad_ref[:, tile * WIDE : (tile + 1) * WIDE] = jnp.sum(
            full(grad), axis=0, keepdims=True
        )
        if tile >= 2:
            wait_all(held.at[slot], held_sem.at[slot])
        held[slot] = low(mm(first_t, grad)).reshape(held.shape[1:])
        store_columns(place, tile, held.at[slot], out_ref, held_sem.at[slot], out_side_first)
        total[...] += mm_t(grad, up[tile].reshape(WIDE, WIDE))
    norm_step(
        total, hat_ref, scale_ref, gain_ref, first_in_ref, gain_grad_ref, shift_grad_ref, bias_grad_ref
    )
    for slot in range(2):
        wait_all(held.at[slot], held_sem.at[slot])


def attention_backward(
    depth, side_first, out_side_first, seqs, pos_ref, grad_ref, own_ref, other_ref, ctx_t_ref, x_t_ref, qkv_ref, probs_ref,
    x_grad_ref, qkv_grad_ref, out_ref,
    weight, probs, ctx_grad, grads, held, weight_sem, probs_sem, held_sem,
):
    place = Place(pos_ref, depth)
    load_unit(place, own_ref, other_ref, weight, weight_sem, False, side_first)
    pltpu.make_async_copy(probs_ref, probs, probs_sem).start()
    tokens = grad_ref.shape[0]
    slots = tokens // seqs
    grad_low = low(grad_ref[...])
    held[0] = low(mm(ctx_t_ref[...], grad_low)).reshape(held.shape[1:])
    store_columns(place, 3, held.at[0], out_ref, held_sem.at[0], out_side_first)
    wait_all(weight, weight_sem)
    from_out = low(mm_t(grad_low, weight[3].reshape(WIDE, WIDE)))
    for pair in range(PAIRS):
        ctx_grad[pair] = from_out[:, pair * PAIR : (pair + 1) * PAIR]
    wait_all(probs, probs_sem)
    lane = lax.broadcasted_iota(jnp.int32, (KEYS, PAIR), 1)
    for seq in range(seqs):

        def pair_step(pair, carry, seq=seq):
            start = seq * slots
            q = qkv_ref[pair, start : start + slots, :]
            k = qkv_ref[PAIRS + pair, start : start + KEYS, :]
            v = qkv_ref[2 * PAIRS + pair, start : start + KEYS, :]
            out_grad = ctx_grad[pair, start : start + slots, :]
            none = jnp.zeros_like(k)
            k_both = jnp.concatenate(
                [jnp.where(lane < HEAD_DIM, k, none), jnp.where(lane < HEAD_DIM, none, k)], 0
            )
            v_both = jnp.concatenate(
                [jnp.where(lane < HEAD_DIM, v, none), jnp.where(lane < HEAD_DIM, none, v)], 0
            )
            weights = probs[seq, pair]
            probs_grad = mm_t(out_grad, v_both)
            halves = []
            for half in range(2):
                lanes = slice(half * KEYS, (half + 1) * KEYS)
                weight_part, grad_part = full(weights[:, lanes]), probs_grad[:, lanes]
                dot = jnp.sum(weight_part * grad_part, axis=-1, keepdims=True)
                halves.append(low(weight_part * (grad_part - dot)))
            scores_grad = jnp.concatenate(halves, 1)
            q_grad = mm(scores_grad, k_both) * HEAD_DIM**-0.5
            grads[pair, start : start + slots, :] = low(q_grad)
            k_grad = t_mm(q, scores_grad) * HEAD_DIM**-0.5
            v_grad = t_mm(out_grad, weights)
            for at, value in ((PAIRS, k_grad), (2 * PAIRS, v_grad)):
                value = jnp.concatenate(
                    [value[:HEAD_DIM, :KEYS], value[HEAD_DIM:, KEYS:]], 0
                )
                grads[at + pair, start : start + KEYS, :] = low(value.T)
                grads[at + pair, start + KEYS : start + slots, :] = jnp.zeros(
                    (slots - KEYS, PAIR), jnp.bfloat16
                )
            return carry

        lax.fori_loop(0, PAIRS, pair_step, 0)
    x_t = x_t_ref[...]
    x_grad_ref[...] = grad_ref[...]
    for block in range(3):
        slot = (block + 1) % 2
        grad = jnp.concatenate([grads[block * PAIRS + pair] for pair in range(PAIRS)], 1)
        qkv_grad_ref[:, block * WIDE : (block + 1) * WIDE] = jnp.sum(
            full(grad), axis=0, keepdims=True
        )
        if block >= 1:
            wait_all(held.at[slot], held_sem.at[slot])
        held[slot] = low(mm(x_t, grad)).reshape(held.shape[1:])
        store_columns(place, block, held.at[slot], out_ref, held_sem.at[slot], out_side_first)
        x_grad_ref[...] += mm_t(grad, weight[block].reshape(WIDE, WIDE))
    for slot in range(2):
        wait_all(held.at[slot], held_sem.at[slot])


VMEM = pltpu.MemorySpace.VMEM
SMEM = pltpu.MemorySpace.SMEM
ANY = pl.ANY
F32 = jnp.float32
BF16 = jnp.bfloat16


def call(kernel, spaces, outs, scratch, flops):
    return pl.pallas_call(
        kernel,
        in_specs=[pl.BlockSpec(memory_space=space) for space in spaces],
        out_specs=[pl.BlockSpec(memory_space=space) for _, _, space in outs],
        out_shape=[jax.ShapeDtypeStruct(shape, dtype) for shape, dtype, _ in outs],
        scratch_shapes=scratch,
        compiler_params=pltpu.CompilerParams(vmem_limit_bytes=VMEM_LIMIT),
        cost_estimate=pl.CostEstimate(flops=flops, bytes_accessed=1 << 20, transcendentals=0),
    )


DMA = pltpu.SemaphoreType.DMA


class Sizes:
    def __init__(self, tokens, seqs, shards, rows):
        self.tokens, self.seqs, self.shards, self.rows = tokens, seqs, shards, rows
        self.depth = shards // 2
        self.slots = tokens // seqs

    def columns(self, count):
        return pltpu.VMEM((count, self.shards, self.rows, WIDE), BF16)

    def by_rows(self):
        return pltpu.VMEM((self.shards, 4, self.rows, WIDE), BF16)

    def unit_grad(self):
        return ((2, 2, 2, self.depth, 2, self.rows, HALF), BF16, ANY)


def run_attention_forward(z, pos, counts, x, unit, side_first, qkv_bias, out_bias, gain, shift):
    t = z.tokens
    return call(
        functools.partial(attention_forward, z.depth, side_first, z.seqs),
        [SMEM, SMEM, VMEM, ANY, ANY, VMEM, VMEM, VMEM, VMEM],
        [
            ((t, WIDE), F32, VMEM),
            ((t, WIDE), F32, VMEM),
            ((t, 128), F32, VMEM),
            ((WIDE, t), BF16, VMEM),
            ((WIDE, t), BF16, VMEM),
            ((WIDE, t), BF16, VMEM),
            ((3 * PAIRS, t, PAIR), BF16, VMEM),
            ((z.seqs, PAIRS, z.slots, 2 * KEYS), BF16, ANY),
        ],
        [
            z.columns(4),
            pltpu.VMEM((PAIRS, t, PAIR), BF16),
            pltpu.VMEM((2, z.slots, 2 * KEYS), BF16),
            DMA,
            DMA((2,)),
        ],
        12 * 10**9,
    )(pos, counts, x, unit[0], unit[1], qkv_bias, out_bias, gain, shift)


def run_mlp_forward(z, pos, first, up, up_side_first, down, down_side_first, up_bias, down_bias, gain, shift):
    t = z.tokens
    return call(
        functools.partial(mlp_forward, z.depth, up_side_first, down_side_first),
        [SMEM, VMEM, ANY, ANY, ANY, ANY, VMEM, VMEM, VMEM, VMEM],
        [
            ((t, WIDE), F32, VMEM),
            ((t, WIDE), F32, VMEM),
            ((t, 128), F32, VMEM),
            ((4, WIDE, t), BF16, ANY),
            ((4, t, WIDE), BF16, ANY),
        ],
        [
            z.columns(4),
            z.by_rows(),
            pltpu.VMEM((t, WIDE), F32),
            pltpu.VMEM((t, WIDE), BF16),
            pltpu.VMEM((2, WIDE, t), BF16),
            pltpu.VMEM((2, t, WIDE), BF16),
            DMA,
            DMA,
            DMA((2,)),
            DMA((2,)),
        ],
        16 * 10**9,
    )(pos, first, up[0], up[1], down[0], down[1], up_bias, down_bias, gain, shift)


def run_down_backward(z, pos, grad, hat, scale, gain, act_t, out_side_first):
    t = z.tokens
    return call(
        functools.partial(down_backward, z.depth, out_side_first),
        [SMEM, VMEM, VMEM, VMEM, VMEM, ANY],
        [
            ((t, WIDE), F32, VMEM),
            ((1, WIDE), F32, VMEM),
            ((1, WIDE), F32, VMEM),
            ((1, WIDE), F32, VMEM),
            z.unit_grad(),
        ],
        [
            pltpu.VMEM((4, WIDE, t), BF16),
            pltpu.VMEM((2, z.shards // 4, 4, z.rows, WIDE), BF16),
            DMA,
            DMA((2,)),
        ],
        8 * 10**9,
    )(pos, grad, hat, scale, gain, act_t)


def run_up_backward(z, pos, second, up, up_side_first, down, down_side_first, slope, first_t, hat, scale, gain, out_side_first):
    t = z.tokens
    return call(
        functools.partial(up_backward, z.depth, up_side_first, down_side_first, out_side_first),
        [SMEM, VMEM, ANY, ANY, ANY, ANY, ANY, VMEM, VMEM, VMEM, VMEM],
        [
            ((t, WIDE), F32, VMEM),
            ((1, WIDE), F32, VMEM),
            ((1, WIDE), F32, VMEM),
            ((1, WIDE), F32, VMEM),
            ((1, 4 * WIDE), F32, VMEM),
            z.unit_grad(),
        ],
        [
            z.columns(4),
            z.by_rows(),
            pltpu.VMEM((4, t, WIDE), BF16),
            pltpu.VMEM((t, WIDE), F32),
            pltpu.VMEM((2, z.shards, z.rows, WIDE), BF16),
            DMA,
            DMA,
            DMA,
            DMA((2,)),
        ],
        20 * 10**9,
    )(pos, second, up[0], up[1], down[0], down[1], slope, first_t, hat, scale, gain)


def run_attention_backward(z, pos, grad, unit, side_first, ctx_t, x_t, qkv, probs, out_side_first):
    t = z.tokens
    return call(
        functools.partial(attention_backward, z.depth, side_first, out_side_first, z.seqs),
        [SMEM, VMEM, ANY, ANY, VMEM, VMEM, VMEM, ANY],
        [
            ((t, WIDE), F32, VMEM),
            ((1, 3 * WIDE), F32, VMEM),
            z.unit_grad(),
        ],
        [
            z.columns(4),
            pltpu.VMEM((z.seqs, PAIRS, z.slots, 2 * KEYS), BF16),
            pltpu.VMEM((PAIRS, t, PAIR), BF16),
            pltpu.VMEM((3 * PAIRS, t, PAIR), BF16),
            pltpu.VMEM((2, z.shards, z.rows, WIDE), BF16),
            DMA,
            DMA,
            DMA((2,)),
        ],
        24 * 10**9,
    )(pos, grad, unit[0], unit[1], ctx_t, x_t, qkv, probs)


class Links:
    def __init__(self, rep_size, fsdp_size):
        self.rep_size, self.fsdp_size = rep_size, fsdp_size
        self.depth = fsdp_size // 2
        rep_at, fsdp_at = lax.axis_index("rep"), lax.axis_index("fsdp")
        self.core, self.side = rep_at % 2, (rep_at // 2) % 2
        self.row, self.level = fsdp_at % 2, fsdp_at // 2

    def permute(self, value, target):
        pairs = []
        for rep_at in range(self.rep_size):
            for fsdp_at in range(self.fsdp_size):
                to_rep, to_fsdp = target(rep_at, fsdp_at)
                pairs.append((rep_at * self.fsdp_size + fsdp_at, to_rep * self.fsdp_size + to_fsdp))
        return lax.ppermute(value, AXES, pairs)

    def other_core(self, value):
        return self.permute(value, lambda r, f: (r ^ 1, f))

    def other_side(self, value):
        return self.permute(value, lambda r, f: (r ^ 2, f))

    def other_row(self, value):
        return self.permute(value, lambda r, f: (r, f ^ 1))

    def level_up(self, value, step):
        return self.permute(value, lambda r, f: (r, ((f // 2 + step) % self.depth) * 2 + f % 2))


def own_quarter(links, columns=None, rows=None):
    if columns is not None:
        blocks = jnp.moveaxis(columns.reshape(columns.shape[0], 4, 2, HALF), 0, 2)
    else:
        blocks = jnp.moveaxis(rows.reshape(4, rows.shape[0] // 4, 2, HALF), 2, 1)
    picked = lax.dynamic_index_in_dim(blocks, links.core, 1, keepdims=False)
    return lax.dynamic_slice_in_dim(picked, links.side * 2, 2, 0)


def gather_unit(links, quarter, side_first):
    column = jnp.stack([quarter] + [links.level_up(quarter, step) for step in range(1, links.depth)])
    hops = (links.other_side, links.other_row) if side_first else (links.other_row, links.other_side)
    part = column
    for hop in hops:
        part = jnp.stack([part, hop(part)])
    return part, links.other_core(part)


def sum_unit(links, grad, side_first):
    hops = (links.other_side, links.other_row) if side_first else (links.other_row, links.other_side)
    total = full(grad[0]) + full(links.other_core(grad[1]))
    for hop in hops:
        total = total[0] + full(hop(low(total[1])))
    share = total[0]
    for step in range(1, links.depth):
        share = share + full(links.level_up(low(total[step]), links.depth - step))
    return low(share)


def sum_copies(links, share):
    if links.rep_size > 4:
        groups = [list(range(first, links.rep_size, 4)) for first in range(4)]
        share = lax.psum(share, "rep", axis_index_groups=groups)
    return share


def pair_up(own, other, at):
    return jnp.where(at == 0, jnp.stack([own, other]), jnp.stack([other, own]))


def join_quarters(links, shares):
    sides = pair_up(shares, links.other_side(shares), links.side)
    return pair_up(sides, links.other_core(sides), links.core)


def gather_small(links, shard):
    column = jnp.zeros((links.depth,) + shard.shape, shard.dtype)
    for step in range(links.depth):
        piece = shard if step == 0 else links.level_up(shard, step)
        at = (links.level - step) % links.depth
        column = lax.dynamic_update_index_in_dim(column, piece, at, 0)
    rows = pair_up(column, links.other_row(column), links.row)
    return jnp.moveaxis(rows, 0, 1).reshape((links.fsdp_size,) + shard.shape)


def sum_small(links, grad):
    total = full(low(grad)) + full(links.other_core(low(grad)))
    total = full(low(total)) + full(links.other_side(low(total)))
    parts = total.reshape((links.depth, 2) + total.shape[1:])
    total = lax.dynamic_index_in_dim(parts, links.row, 1, keepdims=False) + full(
        links.other_row(low(lax.dynamic_index_in_dim(parts, 1 - links.row, 1, keepdims=False)))
    )
    share = lax.dynamic_index_in_dim(total, links.level, 0, keepdims=False)
    for step in range(1, links.depth):
        at = (links.level + step) % links.depth
        piece = lax.dynamic_index_in_dim(total, at, 0, keepdims=False)
        share = share + full(links.level_up(low(piece), step))
    return low(share)


def join_small(bias_up, biases, gains, shard_count):
    return jnp.concatenate(
        [
            bias_up.reshape(shard_count, -1),
            jnp.moveaxis(biases.reshape(6, shard_count, -1), 1, 0).reshape(shard_count, -1),
            jnp.moveaxis(gains.reshape(2, shard_count, -1), 1, 0).reshape(shard_count, -1),
        ],
        axis=1,
    )


def split_small(joined, up_size, width):
    shard_count = joined.shape[0]
    bias_up = joined[:, :up_size].reshape(-1)
    biases = joined[:, up_size : up_size + 6 * width].reshape(shard_count, 6, width)
    gains = joined[:, up_size + 6 * width :].reshape(shard_count, 2, width)
    return (
        bias_up,
        jnp.moveaxis(biases, 0, 1).reshape(6, -1),
        jnp.moveaxis(gains, 0, 1).reshape(2, -1),
    )


SIDE_FIRST = ((False, True, False), (True, False, True))


def shards(
    rep_size, fsdp_size, hidden, region_counts, w_qkv, w_out, w_up, w_down, bias_up, biases, norm_gains, cotangent
):
    links = Links(rep_size, fsdp_size)
    z = Sizes(hidden.shape[0], region_counts.shape[0], fsdp_size, w_qkv.shape[1])
    up_size, width = bias_up.shape[1], biases.shape[2]
    pos = jnp.stack([links.core, links.side, links.row, links.level]).astype(jnp.int32)
    small = jnp.concatenate(
        [join_small(bias_up[l], biases[l], norm_gains[l], 1) for l in range(LAYERS)], axis=1
    )[0]
    small = gather_small(links, small).reshape(fsdp_size, LAYERS, -1)
    units, params = [], []
    for layer in range(LAYERS):
        sides = SIDE_FIRST[layer]
        first_part = jnp.concatenate([w_qkv[layer], w_out[layer]], axis=1)
        units.append(
            (
                gather_unit(links, own_quarter(links, columns=first_part), sides[0]),
                gather_unit(links, own_quarter(links, columns=w_up[layer]), sides[1]),
                gather_unit(links, own_quarter(links, rows=w_down[layer]), sides[2]),
            )
        )
        up_bias, rows, gains = (full(v) for v in split_small(small[:, layer], up_size, width))
        params.append((up_bias[None], rows[:, None], gains[:, None]))
    states = hidden
    kept = []
    for layer in range(LAYERS):
        sides = SIDE_FIRST[layer]
        first_unit, up, down = units[layer]
        up_bias, rows, gains = params[layer]
        qkv_bias = jnp.concatenate([rows[0], jnp.zeros_like(rows[0]), rows[1]], axis=1)
        first, hat_one, scale_one, x_t, ctx_t, first_t, qkv, probs = run_attention_forward(
            z, pos, region_counts, states, first_unit, sides[0], qkv_bias, rows[2], gains[0], rows[3]
        )
        states, hat_two, scale_two, act_t, slope = run_mlp_forward(
            z, pos, first, up, sides[1], down, sides[2], up_bias, rows[4], gains[1], rows[5]
        )
        kept.append((hat_one, scale_one, x_t, ctx_t, first_t, qkv, probs, hat_two, scale_two, act_t, slope))
    output = low(states)
    gradient = cotangent
    weight_grads = [None] * LAYERS
    small_grads = [None] * LAYERS
    for layer in reversed(range(LAYERS)):
        sides = SIDE_FIRST[layer]
        first_unit, up, down = units[layer]
        up_bias, rows, gains = params[layer]
        hat_one, scale_one, x_t, ctx_t, first_t, qkv, probs, hat_two, scale_two, act_t, slope = kept[layer]
        second, gain_two, shift_two, down_bias, down_grad = run_down_backward(
            z, pos, gradient, hat_two, scale_two, gains[1], act_t, sides[2]
        )
        first_in, gain_one, shift_one, out_bias, up_bias_grad, up_grad = run_up_backward(
            z, pos, second, up, sides[1], down, sides[2], slope, first_t, hat_one, scale_one, gains[0], sides[1]
        )
        gradient, qkv_sums, first_grad = run_attention_backward(
            z, pos, first_in, first_unit, sides[0], ctx_t, x_t, qkv, probs, sides[0]
        )
        shares = jnp.stack(
            [
                sum_unit(links, grad, side)
                for grad, side in ((first_grad, sides[0]), (up_grad, sides[1]), (down_grad, sides[2]))
            ]
        )
        weight_grads[layer] = full(join_quarters(links, sum_copies(links, shares)))
        bias_grads = jnp.concatenate(
            [qkv_sums[:, :WIDE], qkv_sums[:, 2 * WIDE :], out_bias, shift_one, down_bias, shift_two]
        )
        gain_grads = jnp.concatenate([gain_one, gain_two])
        small_sum = sum_small(links, join_small(up_bias_grad[0], bias_grads, gain_grads, fsdp_size))
        small_grads[layer] = full(sum_copies(links, small_sum))
    grads = jnp.stack(weight_grads)
    by_columns = jnp.transpose(grads[:, :, :, :2], (0, 3, 5, 2, 4, 1, 6)).reshape(LAYERS, 2, z.rows, 4 * WIDE)
    by_rows = jnp.transpose(grads[:, :, :, 2], (0, 2, 3, 4, 1, 5)).reshape(LAYERS, 4 * z.rows, WIDE)
    small = [split_small(value[None], up_size, width) for value in small_grads]
    return (
        output,
        gradient,
        by_columns[:, 0, :, : 3 * WIDE],
        by_columns[:, 0, :, 3 * WIDE :],
        by_columns[:, 1],
        by_rows,
    ) + tuple(jnp.stack([small[layer][member] for layer in range(LAYERS)]) for member in range(3))


def solution(mesh):
    in_specs = (
        P(("rep", "fsdp"), None),
        P(("rep", "fsdp")),
        P(None, "fsdp", None),
        P(None, "fsdp", None),
        P(None, "fsdp", None),
        P(None, "fsdp", None),
        P(None, "fsdp"),
        P(None, None, "fsdp"),
        P(None, None, "fsdp"),
        P(("rep", "fsdp"), None),
    )
    out_specs = (
        P(("rep", "fsdp"), None),
        P(("rep", "fsdp"), None),
        P(None, "fsdp", None),
        P(None, "fsdp", None),
        P(None, "fsdp", None),
        P(None, "fsdp", None),
        P(None, "fsdp"),
        P(None, None, "fsdp"),
        P(None, None, "fsdp"),
    )
    local = functools.partial(shards, mesh.shape["rep"], mesh.shape["fsdp"])
    return jax.shard_map(local, mesh=mesh, in_specs=in_specs, out_specs=out_specs, check_vma=False)
```

```python
import functools

import jax
import jax.numpy as jnp
from jax import lax
from jax.experimental import pallas as pl
from jax.experimental.pallas import tpu as pltpu
from jax.sharding import PartitionSpec as P

HEADS = 12
HEAD_DIM = 64
LAYERS = 2
TEXT = 128
KEYS = 256
WIDE = 768
HALF = WIDE // 2
PAIR = 2 * HEAD_DIM
PAIRS = HEADS // 2
EPSILON = 1e-12
MASKED = -1000000000.0
AXES = ("rep", "fsdp")
COST = 1.15e9
SMALL = 16
VMEM_LIMIT = 63 * 1024 * 1024
SMALL_LIMIT = 14 * 1024 * 1024


def low(value):
    return value.astype(jnp.bfloat16)


def full(value):
    return value.astype(jnp.float32)


def mm(left, right):
    return jnp.dot(left, right, preferred_element_type=jnp.float32)


def mm_t(left, right):
    return lax.dot_general(
        left, right, (((1,), (1,)), ((), ())), preferred_element_type=jnp.float32
    )


def t_mm(left, right):
    return lax.dot_general(
        left, right, (((0,), (0,)), ((), ())), preferred_element_type=jnp.float32
    )


def flip(at, by):
    return 1 - at if by else at


class Place:
    def __init__(self, pos_ref):
        self.core, self.side = pos_ref[0], pos_ref[1]
        self.row, self.level = pos_ref[2], pos_ref[3]

    def shard(self, level, far_row):
        return level * 2 + flip(self.row, far_row)


def half_lanes(at):
    return pl.ds(pl.multiple_of(at * HALF, HALF), HALF)


def part_of(arrays, path, far_core, far_side, far_row):
    last, first = (far_side, far_row) if path == 0 else (far_row, far_side)
    return arrays[path * 4 + far_core * 2 + last], first


def load_unit(place, depth, arrays, unit, whole, sem, by_rows):
    rows = pl.ds(0, whole.shape[2])
    for path in range(2):
        for far_core in range(2):
            lanes = half_lanes(flip(place.core, far_core))
            for far_side in range(2):
                block = flip(place.side, far_side) * 2 + path
                for far_row in range(2):
                    array, first = part_of(arrays, path, far_core, far_side, far_row)
                    for level in range(depth):
                        shard = place.shard(level, far_row)
                        at = (shard, block) if by_rows else (block, shard)
                        target = whole.at[at[0], at[1], :, lanes]
                        pltpu.make_async_copy(array.at[first, level, unit, rows], target, sem).start()


def load_block(place, depth, block, arrays, whole, sem):
    path = block % 2
    rows = pl.ds(0, whole.shape[1])
    needed_side = place.side if block // 2 == 0 else 1 - place.side
    for far_core in range(2):
        lanes = half_lanes(flip(place.core, far_core))
        for far_row in range(2):
            for far_side in range(2):

                @pl.when(needed_side == far_side)
                def _():
                    array, first = part_of(arrays, path, far_core, far_side, far_row)
                    for level in range(depth):
                        target = whole.at[place.shard(level, far_row), :, lanes]
                        pltpu.make_async_copy(array.at[first, level, 0, rows], target, sem).start()


def wait_all(ref, sem):
    pltpu.make_async_copy(ref, ref, sem).wait()


def sum_place(out, block, far_row, far_side, level):
    if block % 2:
        return out.at[1, far_side, far_row, level]
    return out.at[0, far_row, far_side, level]


def store_columns(place, block, held, outs, sem):
    rows = pl.ds(0, held.shape[1])
    far_side = place.side if block // 2 == 0 else 1 - place.side
    for far_core, out in enumerate(outs):
        core = flip(place.core, far_core)
        for far_row in range(2):
            for level in range(held.shape[0] // 2):
                source = held.at[place.shard(level, far_row), :, half_lanes(core)]
                target = sum_place(out, block, far_row, far_side, level).at[rows]
                pltpu.make_async_copy(source, target, sem).start()


def store_rows(place, tile, held, outs, sem):
    count = held.shape[0]
    for inner in range(count):
        shard = tile * count + inner
        far_row = place.row if shard % 2 == 0 else 1 - place.row
        for block in range(4):
            far_side = place.side if block // 2 == 0 else 1 - place.side
            for far_core, out in enumerate(outs):
                source = held.at[inner, block, :, half_lanes(flip(place.core, far_core))]
                target = sum_place(out, block, far_row, far_side, shard // 2)
                pltpu.make_async_copy(source, target, sem).start()


def chunks(rows):
    size = rows // 4 if rows % 64 == 0 or (rows // 4) % 8 == 0 else rows
    return [(start, size) for start in range(0, rows, size)]


def normalize(value):
    centered = value - jnp.mean(value, axis=-1, keepdims=True)
    scale = lax.rsqrt(jnp.mean(centered * centered, axis=-1, keepdims=True) + EPSILON)
    return centered * scale, scale


def norm_backward(grad, hat, scale, gain):
    direct = grad * gain
    return (
        direct
        - jnp.mean(direct, axis=-1, keepdims=True)
        - hat * jnp.mean(direct * hat, axis=-1, keepdims=True)
    ) * scale


def gelu_and_slope(value):
    size = jnp.abs(value) * 0.7071067811865476
    t = 1.0 / (1.0 + 0.3275911 * size)
    series = t * (
        0.127414796
        + t * (-0.142248368 + t * (0.7107068705 + t * (-0.7265760135 + t * 0.5307027145)))
    )
    bell = jnp.exp(-0.5 * value * value)
    tail = series * bell
    below = jnp.where(value >= 0, 1.0 - tail, tail)
    return value * below, below + value * bell * 0.3989422804014327


def attention_forward(
    depth, seqs, extra, pos_ref, counts_ref, x_ref, params_ref,
    *refs,
):
    parts, refs = refs[:8], refs[8 + extra :]
    first_ref, hat_ref, scale_ref, x_t_ref, ctx_t_ref, first_t_ref, qkv_ref, probs_ref = refs[:8]
    weight, ctx, held, weight_sem, held_sem = refs[8:]
    place = Place(pos_ref)
    load_unit(place, depth, parts, 0, weight, weight_sem, False)
    tokens = x_ref.shape[0]
    slots = tokens // seqs
    x_low = low(x_ref[...])
    x_t_ref[...] = x_low.T
    wait_all(weight, weight_sem)
    for block in range(3):
        out = mm(x_low, weight[block].reshape(WIDE, WIDE))
        if block != 1:
            out = out + params_ref[1 + block // 2 : 2 + block // 2, :WIDE]
        out = low(out)
        for pair in range(PAIRS):
            qkv_ref[block * PAIRS + pair] = out[:, pair * PAIR : (pair + 1) * PAIR]
    lane = lax.broadcasted_iota(jnp.int32, (KEYS, PAIR), 1)
    key = lax.broadcasted_iota(jnp.int32, (slots, KEYS), 1)
    for seq in range(seqs):
        valid = key < TEXT + counts_ref[seq]

        def pair_step(pair, carry, seq=seq, valid=valid):
            start = seq * slots
            slot = lax.rem(pair, 2)
            q = qkv_ref[pair, start : start + slots, :] * jnp.bfloat16(HEAD_DIM**-0.5)
            k = qkv_ref[PAIRS + pair, start : start + KEYS, :]
            v = qkv_ref[2 * PAIRS + pair, start : start + KEYS, :]
            none = jnp.zeros_like(k)
            k_both = jnp.concatenate(
                [jnp.where(lane < HEAD_DIM, k, none), jnp.where(lane < HEAD_DIM, none, k)], 0
            )
            v_both = jnp.concatenate(
                [jnp.where(lane < HEAD_DIM, v, none), jnp.where(lane < HEAD_DIM, none, v)], 0
            )
            scores = mm_t(q, k_both)
            halves = []
            for half in range(2):
                part = jnp.where(valid, scores[:, half * KEYS : (half + 1) * KEYS], MASKED)
                part = jnp.exp(part - jnp.max(part, axis=-1, keepdims=True))
                halves.append(low(part / jnp.sum(part, axis=-1, keepdims=True)))
            probs = jnp.concatenate(halves, 1)

            @pl.when(pair >= 2)
            def _():
                wait_all(held.at[slot], held_sem.at[slot])

            held[slot] = probs
            pltpu.make_async_copy(
                held.at[slot], probs_ref.at[seq, pair], held_sem.at[slot]
            ).start()
            ctx[pair, start : start + slots, :] = low(mm(probs, v_both))
            return carry

        lax.fori_loop(0, PAIRS, pair_step, 0)
        for slot in range(2):
            wait_all(held.at[slot], held_sem.at[slot])
    context = jnp.concatenate([ctx[pair] for pair in range(PAIRS)], 1)
    ctx_t_ref[...] = context.T
    first_ref[...] = mm(context, weight[3].reshape(WIDE, WIDE))
    for start, size in chunks(tokens):
        rows = pl.ds(start, size)
        hat, scale = normalize(full(x_ref[rows, :]) + (first_ref[rows, :] + params_ref[3:4, :WIDE]))
        hat_ref[rows, :] = hat
        scale_ref[rows, :] = jnp.broadcast_to(scale, (size, 128))
        first_ref[rows, :] = hat * params_ref[7:8, :WIDE] + params_ref[4:5, :WIDE]
    first_t_ref[...] = low(first_ref[...]).T


def mlp_forward(
    depth, extra, pos_ref, first_ref, params_ref,
    *refs,
):
    parts, refs = refs[:8], refs[8 + extra :]
    out_ref, hat_ref, scale_ref, act_t_ref, slope_ref = refs[:5]
    up, down, pre, act, act_t, slope, up_sem, down_sem, act_sem, slope_sem = refs[5:]
    place = Place(pos_ref)
    load_unit(place, depth, parts, 0, up, up_sem, False)
    load_unit(place, depth, parts, 1, down, down_sem, True)
    tokens = first_ref.shape[0]
    first_low = low(first_ref[...])
    shards = down.shape[0] // 4
    wait_all(up, up_sem)
    total = None
    for tile in range(4):
        slot = tile % 2
        pre[...] = mm(first_low, up[tile].reshape(WIDE, WIDE))
        if tile >= 2:
            wait_all(slope.at[slot], slope_sem.at[slot])
            wait_all(act_t.at[slot], act_sem.at[slot])

        def row_step(step, carry, tile=tile, slot=slot):
            rows = pl.ds(pl.multiple_of(step * 32, 32), 32)
            value = pre[rows, :] + params_ref[0:1, tile * WIDE : (tile + 1) * WIDE]
            gelu, rise = gelu_and_slope(value)
            act[rows, :] = low(gelu)
            slope[slot, rows, :] = low(rise)
            return carry

        lax.fori_loop(0, tokens // 32, row_step, 0)
        pltpu.make_async_copy(slope.at[slot], slope_ref.at[tile], slope_sem.at[slot]).start()
        act_t[slot] = act[...].T
        pltpu.make_async_copy(act_t.at[slot], act_t_ref.at[tile], act_sem.at[slot]).start()
        if tile == 0:
            wait_all(down, down_sem)
        part = mm(act[...], down[tile * shards : (tile + 1) * shards].reshape(WIDE, WIDE))
        if tile == 0:
            out_ref[...] = part
        else:
            out_ref[...] += part
    for start, size in chunks(tokens):
        rows = pl.ds(start, size)
        hat, scale = normalize(first_ref[rows, :] + out_ref[rows, :] + params_ref[5:6, :WIDE])
        hat_ref[rows, :] = hat
        scale_ref[rows, :] = jnp.broadcast_to(scale, (size, 128))
        out_ref[rows, :] = hat * params_ref[8:9, :WIDE] + params_ref[6:7, :WIDE]
    for slot in range(2):
        wait_all(slope.at[slot], slope_sem.at[slot])
        wait_all(act_t.at[slot], act_sem.at[slot])


def norm_step(grad_ref, hat_ref, scale_ref, gain, out_ref, sums_ref):
    sums = [0.0, 0.0, 0.0]
    for start, size in chunks(grad_ref.shape[0]):
        rows = pl.ds(start, size)
        grad, hat = full(grad_ref[rows, :]), hat_ref[rows, :]
        grad_in = norm_backward(grad, hat, scale_ref[rows, :][:, :1], gain)
        out_ref[rows, :] = grad_in
        for at, value in enumerate((grad * hat, grad, full(low(grad_in)))):
            sums[at] += jnp.sum(value, axis=0, keepdims=True)
    sums_ref[...] = jnp.zeros_like(sums_ref)
    for at in range(3):
        sums_ref[at : at + 1, :] = sums[at]


def down_backward(
    depth, extra, pos_ref, grad_ref, hat_ref, scale_ref, params_ref, act_t_ref, *refs,
):
    second_ref, sums_ref, near_ref, far_ref = refs[extra : extra + 4]
    act_t, held, act_sem, held_sem = refs[extra + 4 :]
    place = Place(pos_ref)
    pltpu.make_async_copy(act_t_ref, act_t, act_sem).start()
    norm_step(grad_ref, hat_ref, scale_ref, params_ref[8:9, :WIDE], second_ref, sums_ref)
    grad_low = low(second_ref[...])
    wait_all(act_t, act_sem)
    for tile in range(4):
        slot = tile % 2
        if tile >= 2:
            wait_all(held.at[slot], held_sem.at[slot])
        held[slot] = low(mm(act_t[tile], grad_low)).reshape(held.shape[1:])
        store_rows(place, tile, held.at[slot], (near_ref, far_ref), held_sem.at[slot])
    for slot in range(2):
        wait_all(held.at[slot], held_sem.at[slot])


def up_backward(
    depth, extra, pos_ref, second_ref, slope_ref, first_t_ref, hat_ref, scale_ref, params_ref, *refs,
):
    parts, refs = refs[:8], refs[8 + extra :]
    first_in_ref, sums_ref, up_grad_ref, near_ref, far_ref = refs[:5]
    up, down, slope, total, held, up_sem, down_sem, slope_sem, held_sem = refs[5:]
    place = Place(pos_ref)
    load_unit(place, depth, parts, 1, down, down_sem, True)
    load_unit(place, depth, parts, 0, up, up_sem, False)
    pltpu.make_async_copy(slope_ref, slope, slope_sem).start()
    shards = down.shape[0] // 4
    grad_low = low(second_ref[...])
    first_t = first_t_ref[...]
    total[...] = second_ref[...]
    wait_all(down, down_sem)
    wait_all(slope, slope_sem)
    wait_all(up, up_sem)
    for tile in range(4):
        slot = tile % 2
        grad = mm_t(grad_low, down[tile * shards : (tile + 1) * shards].reshape(WIDE, WIDE))
        grad = low(grad * full(slope[tile]))
        up_grad_ref[:, tile * WIDE : (tile + 1) * WIDE] = jnp.sum(
            full(grad), axis=0, keepdims=True
        )
        if tile >= 2:
            wait_all(held.at[slot], held_sem.at[slot])
        held[slot] = low(mm(first_t, grad)).reshape(held.shape[1:])
        store_columns(place, tile, held.at[slot], (near_ref, far_ref), held_sem.at[slot])
        total[...] += mm_t(grad, up[tile].reshape(WIDE, WIDE))
    norm_step(total, hat_ref, scale_ref, params_ref[7:8, :WIDE], first_in_ref, sums_ref)
    for slot in range(2):
        wait_all(held.at[slot], held_sem.at[slot])


def attention_backward(
    depth, seqs, extra, pos_ref, grad_ref, qkv_ref, probs_ref, *refs,
):
    parts, refs = refs[:8], refs[8 + extra :]
    grads_ref = refs[0]
    weight, probs, ctx_grad, weight_sem, probs_sem = refs[1:]
    place = Place(pos_ref)
    load_block(place, depth, 3, parts, weight, weight_sem)
    pltpu.make_async_copy(probs_ref, probs, probs_sem).start()
    tokens = grad_ref.shape[0]
    slots = tokens // seqs
    grad_low = low(grad_ref[...])
    wait_all(weight, weight_sem)
    from_out = low(mm_t(grad_low, weight[...].reshape(WIDE, WIDE)))
    for pair in range(PAIRS):
        ctx_grad[pair] = from_out[:, pair * PAIR : (pair + 1) * PAIR]
    wait_all(probs, probs_sem)
    lane = lax.broadcasted_iota(jnp.int32, (KEYS, PAIR), 1)
    for seq in range(seqs):

        def pair_step(pair, carry, seq=seq):
            start = seq * slots
            q = qkv_ref[pair, start : start + slots, :]
            k = qkv_ref[PAIRS + pair, start : start + KEYS, :]
            v = qkv_ref[2 * PAIRS + pair, start : start + KEYS, :]
            out_grad = ctx_grad[pair, start : start + slots, :]
            none = jnp.zeros_like(k)
            k_both = jnp.concatenate(
                [jnp.where(lane < HEAD_DIM, k, none), jnp.where(lane < HEAD_DIM, none, k)], 0
            )
            v_both = jnp.concatenate(
                [jnp.where(lane < HEAD_DIM, v, none), jnp.where(lane < HEAD_DIM, none, v)], 0
            )
            weights = probs[seq, pair]
            probs_grad = mm_t(out_grad, v_both)
            halves = []
            for half in range(2):
                lanes = slice(half * KEYS, (half + 1) * KEYS)
                weight_part, grad_part = full(weights[:, lanes]), probs_grad[:, lanes]
                dot = jnp.sum(weight_part * grad_part, axis=-1, keepdims=True)
                halves.append(low(weight_part * (grad_part - dot)))
            scores_grad = jnp.concatenate(halves, 1)
            q_grad = mm(scores_grad, k_both) * HEAD_DIM**-0.5
            grads_ref[pair, start : start + slots, :] = low(q_grad)
            k_grad = t_mm(q, scores_grad) * HEAD_DIM**-0.5
            v_grad = t_mm(out_grad, weights)
            for at, value in ((PAIRS, k_grad), (2 * PAIRS, v_grad)):
                value = jnp.concatenate(
                    [value[:HEAD_DIM, :KEYS], value[HEAD_DIM:, KEYS:]], 0
                )
                grads_ref[at + pair, start : start + KEYS, :] = low(value.T)
                grads_ref[at + pair, start + KEYS : start + slots, :] = jnp.zeros(
                    (slots - KEYS, PAIR), jnp.bfloat16
                )
            return carry

        lax.fori_loop(0, PAIRS, pair_step, 0)


def qkv_weights(
    depth, up_size, width, extra, pos_ref, grad_ref, grads_ref, ctx_t_ref, x_t_ref, down_sums_ref, up_sums_ref, up_bias_ref, *refs,
):
    near_ref, far_ref = refs[extra : extra + 2]
    held, sums, block_rows, small, held_sem, small_sem = refs[extra + 2 :]
    place = Place(pos_ref)
    outs = (near_ref, far_ref)
    x_t = x_t_ref[...]
    for block in range(3):
        slot = block % 2
        grad = jnp.concatenate([grads_ref[block * PAIRS + pair] for pair in range(PAIRS)], 1)
        if block != 1:
            sums[1 + block // 2 : 2 + block // 2, :] = jnp.sum(full(grad), axis=0, keepdims=True)
        if block >= 2:
            wait_all(held.at[slot], held_sem.at[slot])
        held[slot] = low(mm(x_t, grad)).reshape(held.shape[1:])
        store_columns(place, block, held.at[slot], outs, held_sem.at[slot])
    sums[3:4, :], sums[4:5, :], sums[7:8, :] = up_sums_ref[2:3, :], up_sums_ref[1:2, :], up_sums_ref[0:1, :]
    sums[5:6, :], sums[6:7, :], sums[8:9, :] = down_sums_ref[2:3, :], down_sums_ref[1:2, :], down_sums_ref[0:1, :]
    block_rows[...] = jnp.zeros_like(block_rows)
    for shard in range(2 * depth):
        block_rows[0:1, :up_size] = up_bias_ref[:, shard * up_size : (shard + 1) * up_size]
        block_rows[1:9, :width] = sums[1:9, shard * width : (shard + 1) * width]
        small[shard] = low(block_rows[...])
    rows = held.shape[2]
    for out in outs:
        for far_row in range(2):
            for far_side in range(2):
                for level in range(depth):
                    source = small.at[place.shard(level, far_row)]
                    for path in range(2):
                        target = sum_place(out, path, far_row, far_side, level).at[pl.ds(rows, SMALL)]
                        pltpu.make_async_copy(source, target, small_sem).start()
    wait_all(held.at[1], held_sem.at[1])
    held[1] = low(mm(ctx_t_ref[...], low(grad_ref[...]))).reshape(held.shape[1:])
    store_columns(place, 3, held.at[1], outs, held_sem.at[1])
    for slot in range(2):
        wait_all(held.at[slot], held_sem.at[slot])
    for _ in range(8):
        wait_all(small, small_sem)


def qkv_backward(depth, extra, pos_ref, grad_ref, grads_ref, *refs):
    parts, refs = refs[:8], refs[8 + extra :]
    x_grad_ref, weight, weight_sem = refs
    place = Place(pos_ref)
    for block in range(3):
        load_block(place, depth, block, parts, weight.at[block], weight_sem.at[block])
    x_grad_ref[...] = grad_ref[...]
    for block in range(3):
        grad = jnp.concatenate([grads_ref[block * PAIRS + pair] for pair in range(PAIRS)], 1)
        wait_all(weight.at[block], weight_sem.at[block])
        x_grad_ref[...] += mm_t(grad, weight[block].reshape(WIDE, WIDE))


def finish_first(pos_ref, *refs):
    core, side = pos_ref[0], pos_ref[1]
    quarters, (qkv_ref, out_ref, up_bias_ref, biases_ref, gains_ref) = refs[: 4 * LAYERS], refs[4 * LAYERS :]
    rows = qkv_ref.shape[1]
    for layer in range(LAYERS):
        small = full(quarters[4 * layer][0, rows : rows + SMALL, :])
        up_bias_ref[layer : layer + 1, :] = small[0:1, : up_bias_ref.shape[1]]
        biases_ref[layer] = small[1:7, : biases_ref.shape[2]]
        gains_ref[layer] = small[7:9, : gains_ref.shape[2]]
        for far in range(4):
            part = quarters[4 * layer + far]
            at_core, at_side = flip(core, far // 2), flip(side, far % 2)
            half = at_core * HALF
            lanes = pl.ds(pl.multiple_of(at_side * (2 * WIDE) + half, HALF), HALF)
            qkv_ref[layer, :, lanes] = full(part[0, :rows, :])
            last = full(part[1, :rows, :])

            @pl.when(at_side == 0)
            def _():
                qkv_ref[layer, :, pl.ds(pl.multiple_of(WIDE + half, HALF), HALF)] = last

            @pl.when(at_side == 1)
            def _():
                out_ref[layer, :, half_lanes(at_core)] = last


def finish_second(extra, pos_ref, *refs):
    core, side = pos_ref[0], pos_ref[1]
    quarters, (up_ref, down_ref) = refs[: 4 * LAYERS], refs[4 * LAYERS + extra :]
    rows = up_ref.shape[1]
    for layer in range(LAYERS):
        for far in range(4):
            part = quarters[4 * layer + far]
            at_core, at_side = flip(core, far // 2), flip(side, far % 2)
            for block in range(2):
                lanes = pl.ds(
                    pl.multiple_of(at_side * (2 * WIDE) + block * WIDE + at_core * HALF, HALF), HALF
                )
                up_ref[layer, :, lanes] = full(part[block])
                down_rows = pl.ds(pl.multiple_of((at_side * 2 + block) * rows, rows), rows)
                down_ref[layer, down_rows, half_lanes(at_core)] = full(part[2 + block])


def prepare(
    pos_ref, qkv_ref, out_ref, up_ref, down_ref, up_bias_ref, biases_ref, gains_ref,
    first_group, second_group, third_group, rows_of, sem,
):
    core, side = pos_ref[0], pos_ref[1]
    rows = out_ref.shape[1]
    up_size, width = up_bias_ref.shape[1], biases_ref.shape[2]
    for layer in range(LAYERS):
        for block in range(2):
            at = side * 2 + block
            lanes = pl.ds(pl.multiple_of(at * WIDE + core * HALF, HALF), HALF)
            if layer == 0:
                target = first_group.at[block, 0, pl.ds(0, rows)]
                up, down = second_group.at[block, 0], second_group.at[block, 1]
            else:
                target, up, down = (third_group.at[block, unit] for unit in range(3))
            if block == 0:
                pltpu.make_async_copy(qkv_ref.at[layer, :, lanes], target, sem.at[layer, 0, 0]).start()
            else:

                @pl.when(side == 0)
                def _():
                    lanes = pl.ds(pl.multiple_of(WIDE + core * HALF, HALF), HALF)
                    pltpu.make_async_copy(qkv_ref.at[layer, :, lanes], target, sem.at[layer, 0, 1]).start()

                @pl.when(side == 1)
                def _():
                    pltpu.make_async_copy(
                        out_ref.at[layer, :, half_lanes(core)], target, sem.at[layer, 0, 1]
                    ).start()

            pltpu.make_async_copy(up_ref.at[layer, :, lanes], up, sem.at[layer, 1, block]).start()
            down_rows = pl.ds(pl.multiple_of(at * rows, rows), rows)
            pltpu.make_async_copy(
                down_ref.at[layer, down_rows, half_lanes(core)], down, sem.at[layer, 2, block]
            ).start()
    for layer in range(LAYERS):
        rows_of[...] = jnp.zeros_like(rows_of)
        rows_of[0:1, :up_size] = full(up_bias_ref[layer : layer + 1, :])
        rows_of[1:7, :width] = full(biases_ref[layer])
        rows_of[7:9, :width] = full(gains_ref[layer])
        first_group[layer, 0, rows : rows + SMALL, :] = low(rows_of[...])
    for layer in range(LAYERS):
        for block in range(2):
            for unit in range(3):
                if layer:
                    part = third_group.at[block, unit]
                elif unit:
                    part = second_group.at[block, unit - 1]
                else:
                    part = first_group.at[block, 0, pl.ds(0, rows)]
                wait_all(part, sem.at[layer, unit, block])


def columns_of(depth, pos_ref, *refs):
    level = pos_ref[3]
    for path, out in enumerate(refs[-2:]):
        for far_level, piece in enumerate(refs[:depth]):
            out[lax.rem(level + depth - far_level, depth)] = piece[path]


def split_paths(sizes, column_ref, *refs):
    start = 0
    for at, size in enumerate(sizes):
        for path in range(2):
            refs[-2 * len(sizes) + 2 * at + path][...] = column_ref[:, path, start : start + size]
        start += size


def join(*refs):
    for path, out in enumerate(refs[-2:]):
        out[0] = refs[2 * path][...]
        out[1] = refs[2 * path + 1][...]


def add_up(counts, stacked, *refs):
    start = 0
    for at, count in enumerate(counts):
        total = full(refs[start][...])
        for ref in refs[start + 1 : start + count]:
            total = total + full(ref[...])
        if stacked:
            refs[-1][:, at] = low(total)
        else:
            refs[at - len(counts)][...] = low(total)
        start += count


def add_up_far(depth, count, pos_ref, *refs):
    inputs, outs = refs[: 2 * count], refs[2 * count :]
    step = pl.program_id(0)
    for path in range(2):
        total = full(inputs[path * count][...])
        for ref in inputs[path * count + 1 : (path + 1) * count]:
            total = total + full(ref[...])
        for at in range(depth):

            @pl.when(step == at)
            def _():
                outs[at][path] = total[0].astype(outs[at].dtype)


def add_all(*refs):
    total = full(refs[0][...])
    for ref in refs[1:-1]:
        total = total + full(ref[...])
    refs[-1][...] = low(total)


def spread(depth, up_size, width, near_at, far_at, pos_ref, near_ref, far_ref, params_ref, small, sem):
    place = Place(pos_ref)
    rows = near_ref.shape[3] - SMALL
    for far_row, part in enumerate((near_ref.at[near_at], far_ref.at[far_at])):
        for level in range(depth):
            pltpu.make_async_copy(
                part.at[level, 0, pl.ds(rows, SMALL)], small.at[far_row, level], sem
            ).start()
    wait_all(small, sem)
    ups, others = 0.0, 0.0
    for far_row in range(2):
        for level in range(depth):
            shard = place.shard(level, far_row)
            block = full(small[far_row, level])
            up = jnp.concatenate([block, jnp.zeros((SMALL, 4 * WIDE - HALF), F32)], 1)
            ups += pltpu.roll(up, shard * up_size, 1)
            other = jnp.concatenate([block[:, :128], jnp.zeros((SMALL, WIDE - 128), F32)], 1)
            others += pltpu.roll(other, shard * width, 1)
    params_ref[...] = ups
    params_ref[1:9, :WIDE] = others[1:9]


VMEM = pltpu.MemorySpace.VMEM
SMEM = pltpu.MemorySpace.SMEM
ANY = pl.ANY
F32 = jnp.float32
BF16 = jnp.bfloat16


def call(kernel, spaces, outs, scratch, cost, after=(), limit=VMEM_LIMIT):
    run = pl.pallas_call(
        kernel,
        in_specs=[pl.BlockSpec(memory_space=space) for space in spaces + [ANY] * len(after)],
        out_specs=[pl.BlockSpec(memory_space=space) for _, _, space in outs],
        out_shape=[jax.ShapeDtypeStruct(shape, dtype) for shape, dtype, _ in outs],
        scratch_shapes=scratch,
        compiler_params=pltpu.CompilerParams(vmem_limit_bytes=limit),
        cost_estimate=pl.CostEstimate(flops=int(cost * COST), bytes_accessed=0, transcendentals=0),
    )
    return lambda *args: run(*args, *after)


def pass_through(*refs):
    pass


def tie(values, after):
    count = len(values)
    return pl.pallas_call(
        pass_through,
        in_specs=[pl.BlockSpec(memory_space=ANY)] * (count + len(after)),
        out_specs=[pl.BlockSpec(memory_space=ANY)] * count,
        out_shape=[jax.ShapeDtypeStruct(value.shape, value.dtype) for value in values],
        input_output_aliases={at: at for at in range(count)},
    )(*values, *after)


DMA = pltpu.SemaphoreType.DMA


class Sizes:
    def __init__(self, tokens, seqs, shards, rows, up_size, width):
        self.tokens, self.seqs, self.shards, self.rows = tokens, seqs, shards, rows
        self.up_size, self.width = up_size, width
        self.depth = shards // 2
        self.slots = tokens // seqs

    def columns(self, count):
        return pltpu.VMEM((count, self.shards, self.rows, WIDE), BF16)

    def by_rows(self):
        return pltpu.VMEM((self.shards, 4, self.rows, WIDE), BF16)

    def unit_grad(self, more=0):
        return [((2, 2, 2, self.depth, self.rows + more, HALF), BF16, ANY)] * 2


def run_attention_forward(z, pos, counts, x, unit, params, after=()):
    t = z.tokens
    return call(
        functools.partial(attention_forward, z.depth, z.seqs, len(after)),
        [SMEM, SMEM] + [VMEM] * 2 + [ANY] * 8,
        [
            ((t, WIDE), F32, VMEM),
            ((t, WIDE), F32, VMEM),
            ((t, 128), F32, VMEM),
            ((WIDE, t), BF16, VMEM),
            ((WIDE, t), BF16, VMEM),
            ((WIDE, t), BF16, VMEM),
            ((3 * PAIRS, t, PAIR), BF16, VMEM),
            ((z.seqs, PAIRS, z.slots, 2 * KEYS), BF16, ANY),
        ],
        [
            z.columns(4),
            pltpu.VMEM((PAIRS, t, PAIR), BF16),
            pltpu.VMEM((2, z.slots, 2 * KEYS), BF16),
            DMA,
            DMA((2,)),
        ],
        21,
        after,
    )(pos, counts, x, params, *unit)


def run_mlp_forward(z, pos, first, group, params, after=()):
    t = z.tokens
    return call(
        functools.partial(mlp_forward, z.depth, len(after)),
        [SMEM] + [VMEM] * 2 + [ANY] * 8,
        [
            ((t, WIDE), F32, VMEM),
            ((t, WIDE), F32, VMEM),
            ((t, 128), F32, VMEM),
            ((4, WIDE, t), BF16, ANY),
            ((4, t, WIDE), BF16, ANY),
        ],
        [
            z.columns(4),
            z.by_rows(),
            pltpu.VMEM((t, WIDE), F32),
            pltpu.VMEM((t, WIDE), BF16),
            pltpu.VMEM((2, WIDE, t), BF16),
            pltpu.VMEM((2, t, WIDE), BF16),
            DMA,
            DMA,
            DMA((2,)),
            DMA((2,)),
        ],
        20,
        after,
    )(pos, first, params, *group)


def run_down_backward(z, pos, grad, hat, scale, params, act_t, after=()):
    t = z.tokens
    return call(
        functools.partial(down_backward, z.depth, len(after)),
        [SMEM, VMEM, VMEM, VMEM, VMEM, ANY],
        [
            ((t, WIDE), F32, VMEM),
            ((8, WIDE), F32, VMEM),
            *z.unit_grad(),
        ],
        [
            pltpu.VMEM((4, WIDE, t), BF16),
            pltpu.VMEM((2, z.shards // 4, 4, z.rows, WIDE), BF16),
            DMA,
            DMA((2,)),
        ],
        11.3,
        after,
    )(pos, grad, hat, scale, params, act_t)


def run_up_backward(z, pos, second, group, slope, first_t, hat, scale, params, after=()):
    t = z.tokens
    return call(
        functools.partial(up_backward, z.depth, len(after)),
        [SMEM, VMEM, ANY] + [VMEM] * 4 + [ANY] * 8,
        [
            ((t, WIDE), F32, VMEM),
            ((8, WIDE), F32, VMEM),
            ((1, 4 * WIDE), F32, VMEM),
            *z.unit_grad(),
        ],
        [
            z.columns(4),
            z.by_rows(),
            pltpu.VMEM((4, t, WIDE), BF16),
            pltpu.VMEM((t, WIDE), F32),
            pltpu.VMEM((2, z.shards, z.rows, WIDE), BF16),
            DMA,
            DMA,
            DMA,
            DMA((2,)),
        ],
        20,
        after,
    )(pos, second, slope, first_t, hat, scale, params, *group)


def run_attention_backward(z, pos, grad, unit, qkv, probs, after=()):
    t = z.tokens
    return call(
        functools.partial(attention_backward, z.depth, z.seqs, len(after)),
        [SMEM] + [VMEM] * 2 + [ANY] * 9,
        [((3 * PAIRS, t, PAIR), BF16, VMEM)],
        [
            pltpu.VMEM((z.shards, z.rows, WIDE), BF16),
            pltpu.VMEM((z.seqs, PAIRS, z.slots, 2 * KEYS), BF16),
            pltpu.VMEM((PAIRS, t, PAIR), BF16),
            DMA,
            DMA,
        ],
        15.4,
        after,
    )(pos, grad, qkv, probs, *unit)[0]


def run_qkv_weights(z, pos, grad, grads, ctx_t, x_t, down_sums, up_sums, up_bias, after=()):
    return call(
        functools.partial(qkv_weights, z.depth, z.up_size, z.width, len(after)),
        [SMEM] + [VMEM] * 7,
        z.unit_grad(SMALL),
        [
            pltpu.VMEM((2, z.shards, z.rows, WIDE), BF16),
            pltpu.VMEM((SMALL, WIDE), F32),
            pltpu.VMEM((SMALL, HALF), F32),
            pltpu.VMEM((z.shards, SMALL, HALF), BF16),
            DMA((2,)),
            DMA,
        ],
        8,
        after,
    )(pos, grad, grads, ctx_t, x_t, down_sums, up_sums, up_bias)


def run_qkv_backward(z, pos, grad, grads, unit, after=()):
    return call(
        functools.partial(qkv_backward, z.depth, len(after)),
        [SMEM] + [VMEM] * 2 + [ANY] * 8,
        [((z.tokens, WIDE), F32, VMEM)],
        [
            z.columns(3),
            DMA((3,)),
        ],
        7,
        after,
    )(pos, grad, grads, *unit)[0]


def run_finish_first(z, pos, quarters):
    r = z.rows
    return call(
        finish_first,
        [SMEM] + [VMEM] * (4 * LAYERS),
        [
            ((LAYERS, r, 3 * WIDE), F32, VMEM),
            ((LAYERS, r, WIDE), F32, VMEM),
            ((LAYERS, z.up_size), F32, VMEM),
            ((LAYERS, 6, z.width), F32, VMEM),
            ((LAYERS, 2, z.width), F32, VMEM),
        ],
        [],
        3,
        limit=SMALL_LIMIT,
    )(pos, *quarters)


def run_finish_second(z, pos, quarters, after=()):
    r = z.rows
    return call(
        functools.partial(finish_second, len(after)),
        [SMEM] + [VMEM] * (4 * LAYERS),
        [
            ((LAYERS, r, 4 * WIDE), F32, VMEM),
            ((LAYERS, 4 * r, WIDE), F32, VMEM),
        ],
        [],
        5,
        after,
        limit=SMALL_LIMIT,
    )(pos, *quarters)


def run_prepare(z, pos, *arrays):
    r = z.rows
    return call(
        prepare,
        [SMEM] + [ANY] * 4 + [VMEM] * 3,
        [
            ((2, 1, r + SMALL, HALF), BF16, VMEM),
            ((2, 2, r, HALF), BF16, VMEM),
            ((2, 3, r, HALF), BF16, VMEM),
        ],
        [
            pltpu.VMEM((SMALL, HALF), F32),
            DMA((LAYERS, 3, 2)),
        ],
        1,
        limit=SMALL_LIMIT,
    )(pos, *arrays)


def run_columns_of(pos, pieces):
    depth = len(pieces)
    return call(
        functools.partial(columns_of, depth),
        [SMEM] + [VMEM] * depth,
        [((depth,) + pieces[0].shape[1:], BF16, VMEM)] * 2,
        [],
        2,
        limit=SMALL_LIMIT,
    )(pos, *pieces)


def run_split_paths(column, sizes):
    outs = []
    for size in sizes:
        outs += [(column.shape[:1] + (size,) + column.shape[3:], BF16, VMEM)] * 2
    return call(functools.partial(split_paths, sizes), [VMEM], outs, [], 2, limit=SMALL_LIMIT)(column)


def run_join(pairs):
    return call(
        join, [VMEM] * 4, [((2,) + near.shape, BF16, VMEM) for near, _ in pairs], [], 2,
        limit=SMALL_LIMIT,
    )(*[part for pair in pairs for part in pair])


def add_specs(sums, size, place):
    specs = []
    for parts in sums:
        for array, lead in parts:
            rest = array.shape[len(lead) + 1 :]
            specs.append(
                pl.BlockSpec(
                    (None,) * len(lead) + (size,) + rest,
                    lambda *at, lead=lead, rest=len(rest): lead + (place(*at),) + (0,) * rest,
                )
            )
    return specs


def run_add_up(sums, stacked=False):
    array, lead = sums[0][0]
    shape = array.shape[len(lead) :]
    size = shape[0] // 2
    if stacked:
        outs = [(shape[0], len(sums)) + shape[1:]]
    else:
        outs = [shape] * len(sums)
    return pl.pallas_call(
        functools.partial(add_up, [len(parts) for parts in sums], stacked),
        grid=(2,),
        in_specs=add_specs(sums, size, lambda step: step),
        out_specs=[
            pl.BlockSpec((size,) + out[1:], lambda step, rest=len(out) - 1: (step,) + (0,) * rest) for out in outs
        ],
        out_shape=[jax.ShapeDtypeStruct(out, BF16) for out in outs],
        compiler_params=pltpu.CompilerParams(vmem_limit_bytes=SMALL_LIMIT),
        cost_estimate=pl.CostEstimate(flops=int(3 * COST), bytes_accessed=0, transcendentals=0),
    )(*[array for parts in sums for array, _ in parts])


def run_add_up_far(pos, sums):
    array, lead = sums[0][0]
    depth, *rest = array.shape[len(lead) :]
    outs = [jax.ShapeDtypeStruct((2, *rest), F32 if at == 0 else BF16) for at in range(depth)]
    return pl.pallas_call(
        functools.partial(add_up_far, depth, len(sums[0])),
        grid_spec=pltpu.PrefetchScalarGridSpec(
            num_scalar_prefetch=1,
            grid=(depth,),
            in_specs=add_specs(sums, 1, lambda step, pos_ref: lax.rem(pos_ref[3] + step, depth)),
            out_specs=[pl.BlockSpec(out.shape, lambda step, pos_ref: (0, 0, 0)) for out in outs],
        ),
        out_shape=outs,
        compiler_params=pltpu.CompilerParams(vmem_limit_bytes=SMALL_LIMIT),
        cost_estimate=pl.CostEstimate(flops=int(3 * COST), bytes_accessed=0, transcendentals=0),
    )(pos, *[array for parts in sums for array, _ in parts])


def run_add_all(arrays):
    return call(add_all, [VMEM] * len(arrays), [(arrays[0].shape, BF16, VMEM)], [], 1, limit=SMALL_LIMIT)(*arrays)[0]


def run_spread(z, pos, near, near_at, far, far_at):
    return call(
        functools.partial(spread, z.depth, z.up_size, z.width, near_at, far_at),
        [SMEM, ANY, ANY],
        [((SMALL, 4 * WIDE), F32, VMEM)],
        [pltpu.VMEM((2, z.depth, SMALL, HALF), BF16), DMA],
        2,
        limit=SMALL_LIMIT,
    )(pos, near, far)[0]


class Links:
    def __init__(self, rep_size, fsdp_size):
        self.rep_size, self.fsdp_size = rep_size, fsdp_size
        self.depth = fsdp_size // 2
        rep_at, fsdp_at = lax.axis_index("rep"), lax.axis_index("fsdp")
        self.core, self.side = rep_at % 2, (rep_at // 2) % 2
        self.row, self.level = fsdp_at % 2, fsdp_at // 2

    def permute(self, value, target):
        pairs = []
        for rep_at in range(self.rep_size):
            for fsdp_at in range(self.fsdp_size):
                to_rep, to_fsdp = target(rep_at, fsdp_at)
                pairs.append((rep_at * self.fsdp_size + fsdp_at, to_rep * self.fsdp_size + to_fsdp))
        return lax.ppermute(value, AXES, pairs)

    def other_core(self, value):
        return self.permute(value, lambda r, f: (r ^ 1, f))

    def other_side(self, value):
        return self.permute(value, lambda r, f: (r ^ 2, f))

    def other_row(self, value):
        return self.permute(value, lambda r, f: (r, f ^ 1))

    def level_up(self, value, step):
        return self.permute(value, lambda r, f: (r, ((f // 2 + step) % self.depth) * 2 + f % 2))

    def levels(self):
        return [list(range(row, self.fsdp_size, 2)) for row in range(2)]


class Gather:
    def __init__(self, name, links, columns):
        self.name, self.links, self.live, self.moving = name, links, list(columns), []

    def scope(self, stage):
        return jax.named_scope("gather_" + self.name + "_" + stage)

    def first(self):
        with self.scope("first"):
            self.moving = [self.links.other_row(self.live[0]), self.links.other_side(self.live[1])]

    def join(self):
        with self.scope("join"):
            self.live, self.moving = list(run_join(list(zip(self.live, self.moving)))), []

    def second(self, cores=2):
        with self.scope("second"):
            self.moving = [self.links.other_side(self.live[0]), self.links.other_row(self.live[1])]
        with self.scope("cores"):
            self.moving += [self.links.other_core(part) for part in self.live[:cores]]

    def last(self):
        self.live += self.moving
        near, gone = self.live[:4], len(self.live) - 4
        with self.scope("last"):
            self.moving = [self.links.other_core(part) for part in near[gone:]]

    def arrays(self):
        near, far = self.live[:4], self.live[4:] + self.moving
        return [part for path in range(2) for part in (near[path], near[2 + path], far[path], far[2 + path])]


class Sum:
    def __init__(self, name, links, near, far):
        self.name, self.links, self.near, self.sends = name, links, near, [far]
        self.hops = ((links.other_row, links.other_side), (links.other_side, links.other_row))

    def scope(self, stage):
        return jax.named_scope("sum_" + self.name + "_" + stage)

    def cores(self):
        with self.scope("cores"):
            self.moving = [self.links.other_core(self.sends[0])]

    def after_cores(self):
        self.parts = [[(self.near, (path,)), (self.moving[0], (path,))] for path in range(2)]
        with self.scope("first"):
            self.sends = list(run_add_up(self.at(1)))

    def at(self, far):
        return [[(array, lead + (far,)) for array, lead in parts] for parts in self.parts]

    def first(self):
        with self.scope("first"):
            self.moving = [self.hops[path][0](self.sends[path]) for path in range(2)]

    def after_first(self):
        self.parts = [parts + [(moved, ())] for parts, moved in zip(self.at(0), self.moving)]
        with self.scope("second"):
            self.sends = list(run_add_up(self.at(1)))

    def second(self):
        with self.scope("second"):
            self.moving = [self.hops[path][1](self.sends[path]) for path in range(2)]

    def after_second(self):
        self.parts = [parts + [(moved, ())] for parts, moved in zip(self.at(0), self.moving)]


class Share:
    def __init__(self, name, links, pos, sums, offload):
        self.name, self.links, self.offload = name, links, offload
        with self.scope():
            parts = [part for one in sums for part in one.parts]
            if offload:
                total = run_add_up(parts, stacked=True)[0]
                self.sends = [
                    lax.psum_scatter(total, "fsdp", scatter_dimension=0, axis_index_groups=links.levels())
                ]
            else:
                self.kept, *self.sends = run_add_up_far(pos, parts)

    def scope(self):
        return jax.named_scope("share_" + self.name)

    def levels(self):
        with self.scope():
            self.moving = [self.links.level_up(send, at + 1) for at, send in enumerate(self.sends)]

    def after_levels(self):
        with self.scope():
            self.sends = [run_add_all([self.kept] + self.moving)]

    def copies(self):
        if self.links.rep_size > 4:
            groups = [list(range(first, self.links.rep_size, 4)) for first in range(4)]
            self.sends = [lax.psum(self.sends[0], "rep", axis_index_groups=groups)]

    def sides(self):
        with self.scope():
            self.sends += [self.links.other_side(self.sends[0])]

    def last(self):
        with self.scope():
            self.moving = [self.links.other_core(send) for send in self.sends]

    def quarters(self):
        return self.sends + self.moving


def order(steps, after=()):
    names = ("live", "moving", "sends")
    held = [(step, name) for step in steps for name in (names[:2] if hasattr(step, "live") else names[2:])]
    values = [value for step, name in held for value in getattr(step, name)]
    values = list(tie(values, list(after)))
    token = min(values, key=lambda value: value.size)
    for step, name in held:
        size = len(getattr(step, name))
        setattr(step, name, values[:size])
        values = values[size:]
    return [token]


def shards(
    rep_size, fsdp_size, hidden, region_counts, w_qkv, w_out, w_up, w_down, bias_up, biases, norm_gains, cotangent
):
    links = Links(rep_size, fsdp_size)
    z = Sizes(
        hidden.shape[0], region_counts.shape[0], fsdp_size, w_qkv.shape[1], bias_up.shape[1], biases.shape[2]
    )
    pos = jnp.stack([links.core, links.side, links.row, links.level]).astype(jnp.int32)
    quarters = run_prepare(z, pos, w_qkv, w_out, w_up, w_down, bias_up, biases, norm_gains)
    kept, groups, params = [], [None] * 4, [None] * 2

    def run_first(layer, states, after):
        return run_attention_forward(z, pos, region_counts, states, groups[2 * layer], params[layer], after)

    def run_second(layer, first, after):
        return run_mlp_forward(z, pos, first, groups[2 * layer + 1], params[layer], after)

    def columns(name, quarter, after=()):
        with jax.named_scope("columns_" + name):
            if after:
                quarter = tie([quarter], list(after))[0]
            pieces = [quarter] + [links.level_up(quarter, step) for step in range(1, links.depth)]
            return run_columns_of(pos, pieces)

    first_0 = Gather("first0", links, columns("first0", quarters[0]))
    first_0.first()
    second_0 = Gather("second0", links, columns("second0", quarters[1], first_0.live))

    first_0.join()
    first_0.second()

    order([first_0, second_0])
    first_0.last()
    second_0.first()
    with jax.named_scope("columns_third"):
        third = tie([quarters[2]], second_0.live)[0]
        third = lax.all_gather(third, "fsdp", axis_index_groups=links.levels())
    params[0] = run_spread(z, pos, first_0.live[0], 0, first_0.live[0], 1)
    params[1] = run_spread(z, pos, first_0.live[1], 0, first_0.live[3], 0)
    groups[0] = first_0.arrays()

    second_0.join()
    token = order([second_0], first_0.moving)
    second_0.second()
    one = run_first(0, hidden, token)

    with jax.named_scope("columns_third"):
        third = run_split_paths(third, (1, 2))
    first_1, second_1 = Gather("first1", links, third[:2]), Gather("second1", links, third[2:])
    order([second_0, first_1], one[2:3])
    second_0.last()
    first_1.first()
    groups[1] = second_0.arrays()

    first_1.join()
    token = order([first_1, second_1], second_0.moving)
    first_1.second(cores=1)
    second_1.first()
    two = run_second(0, one[0], token)
    kept.append((one, two))

    second_1.join()
    order([first_1, second_1], two[2:3])
    first_1.last()
    groups[2] = first_1.arrays()

    token = order([second_1], first_1.moving)
    second_1.second()
    one = run_first(1, two[0], token)

    order([second_1], one[2:3])
    second_1.last()
    groups[3] = second_1.arrays()
    two = run_second(1, one[0], ())
    kept.append((one, two))
    output = low(two[0])

    def run_down(layer, gradient, after):
        hat, scale, act_t = kept[layer][1][1:4]
        return run_down_backward(z, pos, gradient, hat, scale, params[layer], act_t, after)

    def run_up(layer, second, after):
        hat, scale, first_t = kept[layer][0][1], kept[layer][0][2], kept[layer][0][5]
        return run_up_backward(
            z, pos, second, groups[2 * layer + 1], kept[layer][1][4], first_t, hat, scale, params[layer], after
        )

    def run_attention(layer, first_in, after):
        qkv, probs = kept[layer][0][6:8]
        return run_attention_backward(z, pos, first_in, groups[2 * layer], qkv, probs, after)

    def run_weights(layer, first_in, grads, small, after):
        x_t, ctx_t = kept[layer][0][3:5]
        return run_qkv_weights(z, pos, first_in, grads, ctx_t, x_t, *small, after)

    def run_states(layer, first_in, grads, after):
        return run_qkv_backward(z, pos, first_in, grads, groups[2 * layer], after)

    second, down_sums, near, far = run_down(1, cotangent, ())
    sum_down_1 = Sum("down1", links, near, far)

    token = order([sum_down_1])
    sum_down_1.cores()
    first_in, up_sums, up_bias, near, far = run_up(1, second, token)
    sum_up_1 = Sum("up1", links, near, far)

    sum_down_1.after_cores()
    token = order([sum_down_1, sum_up_1])
    sum_down_1.first()
    sum_up_1.cores()
    grads = run_attention(1, first_in, token)

    sum_down_1.after_first()
    sum_up_1.after_cores()
    token = order([sum_down_1, sum_up_1], [grads])
    sum_up_1.first()
    sum_down_1.second()
    near, far = run_weights(1, first_in, grads, (down_sums, up_sums, up_bias), token)
    sum_first_1 = Sum("first1", links, near, far)
    gradient = run_states(1, first_in, grads, sum_first_1.sends)

    sum_up_1.after_first()
    sum_down_1.after_second()
    token = order([sum_up_1, sum_first_1], sum_down_1.moving + [gradient])
    sum_up_1.second()
    sum_first_1.cores()
    second, down_sums, near, far = run_down(0, gradient, token)
    sum_down_0 = Sum("down0", links, near, far)

    sum_up_1.after_second()
    sum_first_1.after_cores()
    token = order([sum_first_1, sum_down_0], sum_up_1.moving)
    sum_first_1.first()
    sum_down_0.cores()
    share_second_1 = Share("second1", links, pos, [sum_up_1, sum_down_1], True)
    first_in, up_sums, up_bias, near, far = run_up(0, second, token)
    sum_up_0 = Sum("up0", links, near, far)

    sum_first_1.after_first()
    sum_down_0.after_cores()
    token = order([sum_first_1, sum_down_0, sum_up_0])
    sum_first_1.second()
    sum_down_0.first()
    sum_up_0.cores()
    grads = run_attention(0, first_in, token)

    sum_first_1.after_second()
    sum_down_0.after_first()
    sum_up_0.after_cores()
    share_second_1.copies()
    share_first_1 = Share("first1", links, pos, [sum_first_1], True)
    token = order([sum_down_0, sum_up_0, share_second_1], [grads] + sum_first_1.moving)
    sum_up_0.first()
    sum_down_0.second()
    share_second_1.sides()
    near, far = run_weights(0, first_in, grads, (down_sums, up_sums, up_bias), token)
    sum_first_0 = Sum("first0", links, near, far)

    sum_up_0.after_first()
    sum_down_0.after_second()
    token = order([sum_up_0, sum_first_0, share_second_1], sum_down_0.moving)
    sum_first_0.cores()
    sum_up_0.second()
    share_second_1.last()
    gradient = run_states(0, first_in, grads, token)

    sum_first_0.after_cores()
    sum_up_0.after_second()
    share_first_1.copies()
    order([sum_first_0, share_first_1], sum_up_0.moving + [gradient])
    sum_first_0.first()
    share_second_0 = Share("second0", links, pos, [sum_up_0, sum_down_0], True)
    share_first_1.sides()

    sum_first_0.after_first()
    order([sum_first_0, share_first_1])
    sum_first_0.second()
    share_first_1.last()

    sum_first_0.after_second()
    share_first_0 = Share("first0", links, pos, [sum_first_0], False)
    share_second_0.copies()
    order([share_first_0, share_second_0], share_first_1.moving)
    share_first_0.levels()
    share_second_0.sides()

    share_first_0.after_levels()
    share_first_0.copies()
    order([share_first_0, share_second_0])
    share_first_0.sides()
    share_second_0.last()

    order([share_first_0], share_second_0.moving)
    share_first_0.last()
    up_grad, down_grad = run_finish_second(z, pos, share_second_0.quarters() + share_second_1.quarters())
    qkv_grad, out_grad, *small = run_finish_first(z, pos, share_first_0.quarters() + share_first_1.quarters())
    return (output, gradient, qkv_grad, out_grad, up_grad, down_grad) + tuple(small)


def solution(mesh):
    in_specs = (
        P(("rep", "fsdp"), None),
        P(("rep", "fsdp")),
        P(None, "fsdp", None),
        P(None, "fsdp", None),
        P(None, "fsdp", None),
        P(None, "fsdp", None),
        P(None, "fsdp"),
        P(None, None, "fsdp"),
        P(None, None, "fsdp"),
        P(("rep", "fsdp"), None),
    )
    out_specs = (
        P(("rep", "fsdp"), None),
        P(("rep", "fsdp"), None),
        P(None, "fsdp", None),
        P(None, "fsdp", None),
        P(None, "fsdp", None),
        P(None, "fsdp", None),
        P(None, "fsdp"),
        P(None, None, "fsdp"),
        P(None, None, "fsdp"),
    )
    local = functools.partial(shards, mesh.shape["rep"], mesh.shape["fsdp"])
    return jax.shard_map(local, mesh=mesh, in_specs=in_specs, out_specs=out_specs, check_vma=False)
```

```python
import functools

import jax
import jax.numpy as jnp
from jax import lax
from jax.experimental import pallas as pl
from jax.experimental.pallas import tpu as pltpu
from jax.sharding import PartitionSpec as P

HEADS = 12
HEAD_DIM = 64
LAYERS = 2
TEXT = 128
KEYS = 256
WIDE = 768
HALF = WIDE // 2
PAIR = 2 * HEAD_DIM
PAIRS = HEADS // 2
EPSILON = 1e-12
MASKED = -1000000000.0
AXES = ("rep", "fsdp")
COST = 1.15e9
SMALL = 16
VMEM_LIMIT = 64 * 1024 * 1024
SMALL_LIMIT = VMEM_LIMIT


def low(value):
    return value.astype(jnp.bfloat16)


def full(value):
    return value.astype(jnp.float32)


def mm(left, right):
    return jnp.dot(left, right, preferred_element_type=jnp.float32)


def mm_t(left, right):
    return lax.dot_general(
        left, right, (((1,), (1,)), ((), ())), preferred_element_type=jnp.float32
    )


def t_mm(left, right):
    return lax.dot_general(
        left, right, (((0,), (0,)), ((), ())), preferred_element_type=jnp.float32
    )


def flip(at, by):
    return 1 - at if by else at


class Place:
    def __init__(self, pos_ref):
        self.core, self.side = pos_ref[0], pos_ref[1]
        self.row, self.level = pos_ref[2], pos_ref[3]

    def shard(self, level, far_row):
        return level * 2 + flip(self.row, far_row)


def half_lanes(at):
    return pl.ds(pl.multiple_of(at * HALF, HALF), HALF)


def part_of(arrays, path, far_core, far_side, far_row):
    arrays = arrays[5 * far_core : 5 * far_core + 5]
    if far_side and far_row:
        return arrays[3 + path]
    return arrays[2 * far_side + far_row].at[path]


def load_unit(place, depth, arrays, unit, whole, sems, by_rows):
    rows = pl.ds(0, whole.shape[2])
    for far_side in range(2):
        for path in range(2):
            block = flip(place.side, far_side) * 2 + path
            for far_core in range(2):
                lanes = half_lanes(flip(place.core, far_core))
                for far_row in range(2):
                    part = part_of(arrays, path, far_core, far_side, far_row)
                    for level in range(depth):
                        shard = place.shard(level, far_row)
                        at = (shard, block) if by_rows else (block, shard)
                        sem = sems.at[level * 4 // depth if by_rows else block]
                        target = whole.at[at[0], at[1], :, lanes]
                        pltpu.make_async_copy(part.at[level, unit, rows], target, sem).start()


def load_block(place, depth, block, arrays, whole, sem):
    path = block % 2
    rows = pl.ds(0, whole.shape[1])
    needed_side = place.side if block // 2 == 0 else 1 - place.side
    for far_side in range(2):

        @pl.when(needed_side == far_side)
        def _():
            for far_core in range(2):
                lanes = half_lanes(flip(place.core, far_core))
                for far_row in range(2):
                    part = part_of(arrays, path, far_core, far_side, far_row)
                    for level in range(depth):
                        target = whole.at[place.shard(level, far_row), :, lanes]
                        pltpu.make_async_copy(part.at[level, 0, rows], target, sem).start()


def wait_all(ref, sem):
    pltpu.make_async_copy(ref, ref, sem).wait()


def either(choice, one, other):
    return other + choice * (one - other)


def sum_place(out, block, far_row, far_side, level):
    path = block % 2
    return out.at[path, either(path, far_side, far_row), either(path, far_row, far_side), level]


def side_distance(place, block):
    return either(place.side, 1 - block // 2, block // 2)


def store_columns(place, block, held, outs, sem):
    rows = pl.ds(0, held.shape[1])
    far_side = side_distance(place, block)
    for far_core, out in enumerate(outs):
        core = flip(place.core, far_core)
        for far_row in range(2):
            for level in range(held.shape[0] // 2):
                source = held.at[place.shard(level, far_row), :, half_lanes(core)]
                target = sum_place(out, block, far_row, far_side, level).at[rows]
                pltpu.make_async_copy(source, target, sem).start()


def store_rows(place, tile, held, outs, sem):
    count = held.shape[0]
    for inner in range(count):
        far_row = either(place.row, 1 - inner % 2, inner % 2)
        level = (tile * count + inner) // 2
        for block in range(4):
            far_side = side_distance(place, block)
            for far_core, out in enumerate(outs):
                source = held.at[inner, block, :, half_lanes(flip(place.core, far_core))]
                target = sum_place(out, block, far_row, far_side, level)
                pltpu.make_async_copy(source, target, sem).start()


def copy(source, target, sem):
    pltpu.make_async_copy(source, target, sem).start()


def chunks(rows):
    edges = [rows // 16 * at // 4 * 16 for at in range(4)] + [rows]
    return [(start, end - start) for start, end in zip(edges, edges[1:])]


def normalize(value):
    centered = value - jnp.mean(value, axis=-1, keepdims=True)
    scale = lax.rsqrt(jnp.mean(centered * centered, axis=-1, keepdims=True) + EPSILON)
    return centered * scale, scale


def norm_backward(grad, hat, scale, gain):
    direct = grad * gain
    return (
        direct
        - jnp.mean(direct, axis=-1, keepdims=True)
        - hat * jnp.mean(direct * hat, axis=-1, keepdims=True)
    ) * scale


def gelu_and_slope(value):
    size = jnp.abs(value) * 0.7071067811865476
    t = 1.0 / (1.0 + 0.3275911 * size)
    series = t * (
        0.127414796
        + t * (-0.142248368 + t * (0.7107068705 + t * (-0.7265760135 + t * 0.5307027145)))
    )
    bell = jnp.exp(-0.5 * value * value)
    tail = series * bell
    below = jnp.where(value >= 0, 1.0 - tail, tail)
    return value * below, below + value * bell * 0.3989422804014327


def head_masks(value, lane):
    none = jnp.zeros_like(value)
    return jnp.concatenate(
        [jnp.where(lane < HEAD_DIM, value, none), jnp.where(lane < HEAD_DIM, none, value)], 0
    )


def side_by_side(ref, block):
    return jnp.concatenate([ref[block * PAIRS + pair] for pair in range(PAIRS)], 1)


def attention_forward(depth, seqs, extra, pos_ref, counts_ref, x_ref, params_ref, *refs):
    parts, refs = refs[:10], refs[10 + extra :]
    first_ref, first_low_ref, hat_ref, scale_ref, ctx_ref, qkv_ref, probs_ref = refs[:7]
    weight, held, weight_sem, held_sem = refs[7:]
    place = Place(pos_ref)
    load_unit(place, depth, parts, 0, weight, weight_sem, False)
    tokens = x_ref.shape[0]
    slots = tokens // seqs
    x_low = low(x_ref[...])

    for block in range(3):
        wait_all(weight.at[block], weight_sem.at[block])

    def project(block, carry):
        out = mm(x_low, weight[block].reshape(WIDE, WIDE))
        bias = params_ref[pl.ds(1 + block // 2, 1), :WIDE]
        out = low(out + jnp.where(block == 1, jnp.zeros_like(bias), bias))
        for pair in range(PAIRS):
            qkv_ref[block * PAIRS + pair] = out[:, pair * PAIR : (pair + 1) * PAIR]
        return carry

    lax.fori_loop(0, 3, project, 0)
    lane = lax.broadcasted_iota(jnp.int32, (KEYS, PAIR), 1)
    key = lax.broadcasted_iota(jnp.int32, (slots, KEYS), 1)

    def pair_step(step, carry):
        seq, pair = step // PAIRS, lax.rem(step, PAIRS)
        rows = pl.ds(pl.multiple_of(seq * slots, 16), slots)
        key_rows = pl.ds(pl.multiple_of(seq * slots, 16), KEYS)
        valid = key < TEXT + counts_ref[seq]
        q = qkv_ref[pair, rows, :] * jnp.bfloat16(HEAD_DIM**-0.5)
        scores = mm_t(q, head_masks(qkv_ref[PAIRS + pair, key_rows, :], lane))
        halves = []
        for half in range(2):
            part = jnp.where(valid, scores[:, half * KEYS : (half + 1) * KEYS], MASKED)
            part = jnp.exp(part - jnp.max(part, axis=-1, keepdims=True))
            halves.append(low(part * (1.0 / jnp.sum(part, axis=-1, keepdims=True))))
        probs = jnp.concatenate(halves, 1)
        held[seq, pair] = probs
        copy(held.at[seq, pair], probs_ref.at[seq, pair], held_sem)
        ctx_ref[pair, rows, :] = low(mm(probs, head_masks(qkv_ref[2 * PAIRS + pair, key_rows, :], lane)))
        return carry

    lax.fori_loop(0, seqs * PAIRS, pair_step, 0, unroll=2)
    wait_all(weight.at[3], weight_sem.at[3])
    first_ref[...] = mm(side_by_side(ctx_ref, 0), weight[3].reshape(WIDE, WIDE))
    for start, size in chunks(tokens):
        rows = pl.ds(start, size)
        hat, scale = normalize(full(x_ref[rows, :]) + (first_ref[rows, :] + params_ref[3:4, :WIDE]))
        hat_ref[rows, :] = hat
        scale_ref[rows, :] = jnp.broadcast_to(scale, (size, 128))
        first = hat * params_ref[7:8, :WIDE] + params_ref[4:5, :WIDE]
        first_ref[rows, :] = first
        first_low_ref[rows, :] = low(first)
    wait_all(held, held_sem)


def mlp_forward(depth, extra, pos_ref, first_ref, params_ref, *refs):
    parts, refs = refs[:10], refs[10 + extra :]
    out_ref, out_low_ref, hat_ref, scale_ref, act_ref, slope_ref = refs[:6]
    up, down, pre, first_low, act, slope, up_sem, down_sem, act_sem, slope_sem = refs[6:]
    place = Place(pos_ref)
    load_unit(place, depth, parts, 0, up, up_sem, False)
    load_unit(place, depth, parts, 1, down, down_sem, True)
    tokens = first_ref.shape[0]
    half = tokens // 2
    first_low[...] = low(first_ref[...])
    shards = down.shape[0] // 4
    out_ref[...] = first_ref[...] + params_ref[5:6, :WIDE]
    act[3, half:, :] = jnp.zeros((half, WIDE), BF16)
    for tile in range(4):
        wait_all(up.at[tile], up_sem.at[tile])
    pre[0] = mm(first_low[...], up[0].reshape(WIDE, WIDE))
    for tile in range(4):
        wait_all(down.at[pl.ds(tile * shards, shards)], down_sem.at[tile])

    def half_rows(step):
        return pl.ds(pl.multiple_of(lax.rem(step, 2) * half, 16), half)

    def below(step):
        tile, rows = step // 2, half_rows(step)
        weight = down[pl.ds(tile * shards, shards)].reshape(WIDE, WIDE)
        out_ref[rows, :] += mm(act[tile, rows, :], weight)

    def half_step(step, carry):
        tile, rows = step // 2, half_rows(step)
        slot, later = lax.rem(tile, 2), lax.rem(tile + 1, 4)
        bias = params_ref[0:1, pl.ds(pl.multiple_of(tile * WIDE, WIDE), WIDE)]
        below(lax.rem(step + 7, 8))
        pre[1 - slot, rows, :] = mm(first_low[rows, :], up[later].reshape(WIDE, WIDE))
        gelu, rise = gelu_and_slope(pre[slot, rows, :] + bias)
        act[tile, rows, :] = low(gelu)
        slope[tile, rows, :] = low(rise)
        copy(slope.at[tile, rows], slope_ref.at[tile, rows], slope_sem)
        copy(act.at[tile, rows], act_ref.at[tile, rows], act_sem)
        return carry

    lax.fori_loop(0, 8, half_step, 0)
    below(7)
    for start, size in chunks(tokens):
        rows = pl.ds(start, size)
        hat, scale = normalize(out_ref[rows, :])
        hat_ref[rows, :] = hat
        scale_ref[rows, :] = jnp.broadcast_to(scale, (size, 128))
        out = hat * params_ref[8:9, :WIDE] + params_ref[6:7, :WIDE]
        out_ref[rows, :] = out
        out_low_ref[rows, :] = low(out)
    wait_all(slope, slope_sem)
    wait_all(act, act_sem)


def load_rows(pairs, sem):
    for at, (start, size) in enumerate(chunks(pairs[0][0].shape[0])):
        for source, target in pairs:
            rows = pl.ds(start, size)
            copy(source.at[rows], target.at[rows], sem.at[at])


def norm_step(grad, hat, scale, gain, out, out_ref, sums_ref, waits, sem, out_sem):
    sums = [0.0, 0.0, 0.0]
    for at, (start, size) in enumerate(chunks(grad.shape[0])):
        rows = pl.ds(start, size)
        for array in waits:
            wait_all(array.at[rows], sem.at[at])
        value, hat_rows = full(grad[rows, :]), hat[rows, :]
        grad_in = norm_backward(value, hat_rows, scale[rows, :][:, :1], gain)
        out[rows, :] = grad_in
        copy(out.at[rows], out_ref.at[rows], out_sem)
        for number, part in enumerate((value * hat_rows, value, full(low(grad_in)))):
            sums[number] += jnp.sum(part, axis=0, keepdims=True)
    sums_ref[...] = jnp.zeros_like(sums_ref)
    for number in range(3):
        sums_ref[number : number + 1, :] = sums[number]


def down_backward(depth, extra, pos_ref, params_ref, grad_ref, hat_ref, scale_ref, act_ref, *refs):
    second_ref, sums_ref, near_ref, far_ref = refs[extra : extra + 4]
    grad, hat, scale, second, act, held, row_sem, act_sem, out_sem, held_sem = refs[extra + 4 :]
    place = Place(pos_ref)
    load_rows([(grad_ref, grad), (hat_ref, hat), (scale_ref, scale)], row_sem)
    for tile in range(4):
        copy(act_ref.at[tile], act.at[tile], act_sem.at[tile])
    norm_step(
        grad, hat, scale, params_ref[8:9, :WIDE], second, second_ref, sums_ref, (grad, hat, scale), row_sem, out_sem
    )
    grad_low = low(second[...])
    for tile in range(4):
        wait_all(act.at[tile], act_sem.at[tile])

    def tile_step(tile, carry):
        held[tile] = low(t_mm(act[tile], grad_low)).reshape(held.shape[1:])
        store_rows(place, tile, held.at[tile], (near_ref, far_ref), held_sem)
        return carry

    lax.fori_loop(0, 4, tile_step, 0)
    wait_all(second, out_sem)
    wait_all(held, held_sem)


def up_backward(
    depth, extra, pos_ref, params_ref, second_ref, slope_ref, first_low_ref, hat_ref, scale_ref, *refs
):
    parts, refs = refs[:10], refs[10 + extra :]
    first_in_ref, sums_ref, up_grad_ref, near_ref, far_ref = refs[:5]
    up, down, slope, total, first_low, hat, scale, held, *sems = refs[5:]
    up_sem, down_sem, slope_sem, second_sem, first_sem, row_sem, out_sem, held_sem = sems
    place = Place(pos_ref)
    copy(second_ref, total, second_sem)
    load_unit(place, depth, parts, 1, down, down_sem, True)
    for tile in range(4):
        copy(slope_ref.at[tile], slope.at[tile], slope_sem.at[tile])
    copy(first_low_ref, first_low, first_sem)
    load_unit(place, depth, parts, 0, up, up_sem, False)
    load_rows([(hat_ref, hat), (scale_ref, scale)], row_sem)
    shards = down.shape[0] // 4
    wait_all(total, second_sem)
    grad_low = low(total[...])
    wait_all(first_low, first_sem)
    for tile in range(4):
        wait_all(down.at[pl.ds(tile * shards, shards)], down_sem.at[tile])
        wait_all(slope.at[tile], slope_sem.at[tile])
        wait_all(up.at[tile], up_sem.at[tile])

    def tile_step(tile, carry):
        below = pl.ds(tile * shards, shards)
        grad = mm_t(grad_low, down[below].reshape(WIDE, WIDE))
        grad = low(grad * full(slope[tile]))
        up_grad_ref[:, pl.ds(pl.multiple_of(tile * WIDE, WIDE), WIDE)] = jnp.sum(
            full(grad), axis=0, keepdims=True
        )
        held[tile] = low(t_mm(first_low[...], grad)).reshape(held.shape[1:])
        total[...] += mm_t(grad, up[tile].reshape(WIDE, WIDE))
        store_columns(place, tile, held.at[tile], (near_ref, far_ref), held_sem)
        return carry

    lax.fori_loop(0, 4, tile_step, 0)
    norm_step(
        total, hat, scale, params_ref[7:8, :WIDE], total, first_in_ref, sums_ref, (hat, scale), row_sem, out_sem
    )
    wait_all(total, out_sem)
    wait_all(held, held_sem)


def attention_backward(depth, seqs, extra, pos_ref, grad_ref, qkv_ref, probs_ref, *refs):
    parts, refs = refs[:10], refs[10 + extra :]
    grads_ref = refs[0]
    weight, grad, qkv, probs, ctx_grad, grads, weight_sem, grad_sem, qkv_sem, probs_sem, out_sem = refs[1:]
    place = Place(pos_ref)
    copy(grad_ref, grad, grad_sem)
    load_block(place, depth, 3, parts, weight, weight_sem)
    copy(qkv_ref, qkv, qkv_sem)
    copy(probs_ref, probs, probs_sem)
    tokens = grad.shape[0]
    slots = tokens // seqs
    wait_all(grad, grad_sem)
    wait_all(weight, weight_sem)
    from_out = low(mm_t(low(grad[...]), weight[...].reshape(WIDE, WIDE)))
    for pair in range(PAIRS):
        ctx_grad[pair] = from_out[:, pair * PAIR : (pair + 1) * PAIR]
    wait_all(qkv, qkv_sem)
    wait_all(probs, probs_sem)
    lane = lax.broadcasted_iota(jnp.int32, (KEYS, PAIR), 1)

    def pair_step(step, carry):
        seq, pair = step // PAIRS, lax.rem(step, PAIRS)
        start = pl.multiple_of(seq * slots, 16)
        rows, key_rows = pl.ds(start, slots), pl.ds(start, KEYS)
        q = qkv[pair, rows, :]
        out_grad = ctx_grad[pair, rows, :]
        weights = probs[seq, pair]
        probs_grad = mm_t(out_grad, head_masks(qkv[2 * PAIRS + pair, key_rows, :], lane))
        halves = []
        for half in range(2):
            lanes = slice(half * KEYS, (half + 1) * KEYS)
            weight_part, grad_part = full(weights[:, lanes]), probs_grad[:, lanes]
            dot = jnp.sum(weight_part * grad_part, axis=-1, keepdims=True)
            halves.append(low(weight_part * (grad_part - dot)))
        scores_grad = jnp.concatenate(halves, 1)
        q_grad = mm(scores_grad, head_masks(qkv[PAIRS + pair, key_rows, :], lane)) * HEAD_DIM**-0.5
        grads[pair, rows, :] = low(q_grad)
        k_grad = t_mm(q, scores_grad) * HEAD_DIM**-0.5
        v_grad = t_mm(out_grad, weights)
        for at, value in ((PAIRS, k_grad), (2 * PAIRS, v_grad)):
            value = jnp.concatenate([value[:HEAD_DIM, :KEYS], value[HEAD_DIM:, KEYS:]], 0)
            grads[at + pair, key_rows, :] = low(value.T)
            grads[at + pair, pl.ds(pl.multiple_of(start + KEYS, 16), slots - KEYS), :] = jnp.zeros(
                (slots - KEYS, PAIR), BF16
            )
        for at in range(3):
            copy(grads.at[at * PAIRS + pair, rows], grads_ref.at[at * PAIRS + pair, rows], out_sem)
        return carry

    lax.fori_loop(0, seqs * PAIRS, pair_step, 0, unroll=2)
    wait_all(grads, out_sem)


def qkv_weights(
    depth, up_size, width, extra, pos_ref, down_sums_ref, up_sums_ref, up_bias_ref, grad_ref, grads_ref, ctx_ref, x_ref,
    *refs,
):
    outs, refs = refs[extra : extra + 2], refs[extra + 2 :]
    grad, grads, ctx, x_low, held, sums, block_rows, small, grad_sem, grads_sem, ctx_sem, x_sem, held_sem, small_sem = refs
    place = Place(pos_ref)
    copy(x_ref, x_low, x_sem)
    for block in range(3):
        panels = pl.ds(block * PAIRS, PAIRS)
        copy(grads_ref.at[panels], grads.at[panels], grads_sem.at[block])
    copy(ctx_ref, ctx, ctx_sem)
    copy(grad_ref, grad, grad_sem)
    wait_all(x_low, x_sem)
    for block in range(3):
        wait_all(grads.at[pl.ds(block * PAIRS, PAIRS)], grads_sem.at[block])

    def block_step(block, carry):
        part = side_by_side(grads, block)
        sums[pl.ds(block, 1), :] = jnp.sum(full(part), axis=0, keepdims=True)
        held[block] = low(t_mm(x_low[...], part)).reshape(held.shape[1:])
        store_columns(place, block, held.at[block], outs, held_sem)
        return carry

    lax.fori_loop(0, 3, block_step, 0)
    sums[1:2, :] = sums[2:3, :]
    block_rows[...] = jnp.zeros_like(block_rows)
    for shard in range(2 * depth):
        lanes = slice(shard * width, (shard + 1) * width)
        block_rows[0:1, :up_size] = up_bias_ref[:, shard * up_size : (shard + 1) * up_size]
        block_rows[1:3, :width] = sums[0:2, lanes]
        for row, (ref, at) in enumerate(
            ((up_sums_ref, 2), (up_sums_ref, 1), (down_sums_ref, 2), (down_sums_ref, 1), (up_sums_ref, 0), (down_sums_ref, 0))
        ):
            block_rows[3 + row : 4 + row, :width] = ref[at : at + 1, lanes]
        small[shard] = low(block_rows[...])
    rows = held.shape[2]
    for out in outs:
        for far_row in range(2):
            for far_side in range(2):
                for level in range(depth):
                    source = small.at[place.shard(level, far_row)]
                    for path in range(2):
                        target = sum_place(out, path, far_row, far_side, level).at[pl.ds(rows, SMALL)]
                        copy(source, target, small_sem)
    wait_all(ctx, ctx_sem)
    wait_all(grad, grad_sem)
    held[3] = low(t_mm(side_by_side(ctx, 0), low(grad[...]))).reshape(held.shape[1:])
    store_columns(place, 3, held.at[3], outs, held_sem)
    wait_all(held, held_sem)
    for _ in range(8):
        wait_all(small, small_sem)


def qkv_backward(depth, extra, pos_ref, grad_ref, grads_ref, *refs):
    parts, refs = refs[:10], refs[10 + extra :]
    x_grad_ref, weight, grads, weight_sem, grads_sem, grad_sem = refs
    place = Place(pos_ref)
    copy(grad_ref, x_grad_ref, grad_sem)
    for block in range(3):
        panels = pl.ds(block * PAIRS, PAIRS)
        copy(grads_ref.at[panels], grads.at[panels], grads_sem.at[block])
        load_block(place, depth, block, parts, weight.at[block], weight_sem.at[block])
    wait_all(x_grad_ref, grad_sem)
    for block in range(3):
        wait_all(grads.at[pl.ds(block * PAIRS, PAIRS)], grads_sem.at[block])
        wait_all(weight.at[block], weight_sem.at[block])

    def block_step(block, carry):
        x_grad_ref[...] += mm_t(side_by_side(grads, block), weight[block].reshape(WIDE, WIDE))
        return carry

    lax.fori_loop(0, 3, block_step, 0)


def finish_first(pos_ref, *refs):
    core, side = pos_ref[0], pos_ref[1]
    quarters, (qkv_ref, out_ref, up_bias_ref, biases_ref, gains_ref) = refs[: 4 * LAYERS], refs[4 * LAYERS :]
    rows = qkv_ref.shape[1]
    for layer in range(LAYERS):
        small = full(quarters[4 * layer][0, rows : rows + SMALL, :])
        up_bias_ref[layer : layer + 1, :] = small[0:1, : up_bias_ref.shape[1]]
        biases_ref[:, layer] = small[1:7, : biases_ref.shape[2]]
        gains_ref[layer] = small[7:9, : gains_ref.shape[2]]
        for far in range(4):
            part = quarters[4 * layer + far]
            at_core, at_side = flip(core, far // 2), flip(side, far % 2)
            half = at_core * HALF
            lanes = pl.ds(pl.multiple_of(at_side * (2 * WIDE) + half, HALF), HALF)
            qkv_ref[layer, :, lanes] = full(part[0, :rows, :])
            last = full(part[1, :rows, :])

            @pl.when(at_side == 0)
            def _():
                qkv_ref[layer, :, pl.ds(pl.multiple_of(WIDE + half, HALF), HALF)] = last

            @pl.when(at_side == 1)
            def _():
                out_ref[layer, :, half_lanes(at_core)] = last


def finish_second(extra, pos_ref, *refs):
    core, side = pos_ref[0], pos_ref[1]
    quarters, (up_ref, down_ref) = refs[: 4 * LAYERS], refs[4 * LAYERS + extra :]
    rows = up_ref.shape[1]
    for layer in range(LAYERS):
        for far in range(4):
            part = quarters[4 * layer + far]
            at_core, at_side = flip(core, far // 2), flip(side, far % 2)
            for block in range(2):
                lanes = pl.ds(
                    pl.multiple_of(at_side * (2 * WIDE) + block * WIDE + at_core * HALF, HALF), HALF
                )
                up_ref[layer, :, lanes] = full(part[block])
                down_rows = pl.ds(pl.multiple_of((at_side * 2 + block) * rows, rows), rows)
                down_ref[layer, down_rows, half_lanes(at_core)] = full(part[2 + block])


def prepare(
    pos_ref, qkv_ref, out_ref, up_ref, down_ref, up_bias_ref, biases_ref, gains_ref,
    first_group, second_group, third_group, rows_of, sem,
):
    core, side = pos_ref[0], pos_ref[1]
    rows = out_ref.shape[1]
    up_size, width = up_bias_ref.shape[1], biases_ref.shape[2]
    for layer in range(LAYERS):
        for block in range(2):
            at = side * 2 + block
            lanes = pl.ds(pl.multiple_of(at * WIDE + core * HALF, HALF), HALF)
            if layer == 0:
                target = first_group.at[block, 0, pl.ds(0, rows)]
                up, down = second_group.at[block, 0], second_group.at[block, 1]
            else:
                target, up, down = (third_group.at[block, unit] for unit in range(3))
            if block == 0:
                pltpu.make_async_copy(qkv_ref.at[layer, :, lanes], target, sem.at[layer, 0, 0]).start()
            else:

                @pl.when(side == 0)
                def _():
                    lanes = pl.ds(pl.multiple_of(WIDE + core * HALF, HALF), HALF)
                    pltpu.make_async_copy(qkv_ref.at[layer, :, lanes], target, sem.at[layer, 0, 1]).start()

                @pl.when(side == 1)
                def _():
                    pltpu.make_async_copy(
                        out_ref.at[layer, :, half_lanes(core)], target, sem.at[layer, 0, 1]
                    ).start()

            pltpu.make_async_copy(up_ref.at[layer, :, lanes], up, sem.at[layer, 1, block]).start()
            down_rows = pl.ds(pl.multiple_of(at * rows, rows), rows)
            pltpu.make_async_copy(
                down_ref.at[layer, down_rows, half_lanes(core)], down, sem.at[layer, 2, block]
            ).start()
    for layer in range(LAYERS):
        rows_of[...] = jnp.zeros_like(rows_of)
        rows_of[0:1, :up_size] = full(up_bias_ref[layer : layer + 1, :])
        rows_of[1:7, :width] = full(biases_ref[:, layer])
        rows_of[7:9, :width] = full(gains_ref[layer])
        first_group[layer, 0, rows : rows + SMALL, :] = low(rows_of[...])
    for layer in range(LAYERS):
        for block in range(2):
            for unit in range(3):
                if layer:
                    part = third_group.at[block, unit]
                elif unit:
                    part = second_group.at[block, unit - 1]
                else:
                    part = first_group.at[block, 0, pl.ds(0, rows)]
                wait_all(part, sem.at[layer, unit, block])


def columns_of(depth, pos_ref, *refs):
    level, out = pos_ref[3], refs[-1]
    for path in range(2):
        for far_level, piece in enumerate(refs[:depth]):
            out[path, lax.rem(level + depth - far_level, depth)] = piece[path]


def split_columns(sizes, column_ref, *refs):
    start = 0
    for size, out in zip(sizes, refs[-len(sizes) :]):
        for path in range(2):
            out[path] = column_ref[:, path, start : start + size]
        start += size


def add_up(jobs, *refs):
    start, out = 0, sum(sum(counts) for counts, _ in jobs)
    for counts, form in jobs:
        for at, count in enumerate(counts):
            total = full(refs[start][...])
            for ref in refs[start + 1 : start + count]:
                total = total + full(ref[...])
            if form == "joined":
                refs[out][at] = low(total)
            elif form == "beside":
                refs[out][:, at] = low(total)
            else:
                refs[out + at][...] = low(total)
            start += count
        out += 1 if form else len(counts)


def add_up_far(depth, count, pos_ref, *refs):
    inputs, outs = refs[: 2 * count], refs[2 * count :]
    step = pl.program_id(0)
    for path in range(2):
        total = full(inputs[path * count][...])
        for ref in inputs[path * count + 1 : (path + 1) * count]:
            total = total + full(ref[...])
        for at in range(depth):

            @pl.when(step == at)
            def _():
                outs[at][path] = total[0].astype(outs[at].dtype)


def add_all(*refs):
    total = full(refs[0][...])
    for ref in refs[1:-1]:
        total = total + full(ref[...])
    refs[-1][...] = low(total)


def spread(depth, up_size, width, path, pos_ref, near_ref, far_ref, params_ref, small, sem):
    place = Place(pos_ref)
    rows = near_ref.shape[3] - SMALL
    for far_row, part in enumerate((near_ref.at[path], far_ref.at[path])):
        for level in range(depth):
            pltpu.make_async_copy(
                part.at[level, 0, pl.ds(rows, SMALL)], small.at[far_row, level], sem
            ).start()
    wait_all(small, sem)
    ups, others = 0.0, 0.0
    for far_row in range(2):
        for level in range(depth):
            shard = place.shard(level, far_row)
            block = full(small[far_row, level])
            up = jnp.concatenate([block, jnp.zeros((SMALL, 4 * WIDE - HALF), F32)], 1)
            ups += pltpu.roll(up, shard * up_size, 1)
            other = jnp.concatenate([block[:, :128], jnp.zeros((SMALL, WIDE - 128), F32)], 1)
            others += pltpu.roll(other, shard * width, 1)
    params_ref[...] = ups
    params_ref[1:9, :WIDE] = others[1:9]


VMEM = pltpu.MemorySpace.VMEM
SMEM = pltpu.MemorySpace.SMEM
ANY = pl.ANY
F32 = jnp.float32
BF16 = jnp.bfloat16


def call(kernel, spaces, outs, scratch, cost, after=(), limit=VMEM_LIMIT):
    run = pl.pallas_call(
        kernel,
        in_specs=[pl.BlockSpec(memory_space=space) for space in spaces + [ANY] * len(after)],
        out_specs=[pl.BlockSpec(memory_space=space) for _, _, space in outs],
        out_shape=[jax.ShapeDtypeStruct(shape, dtype) for shape, dtype, _ in outs],
        scratch_shapes=scratch,
        compiler_params=pltpu.CompilerParams(vmem_limit_bytes=limit),
        cost_estimate=pl.CostEstimate(flops=int(cost * COST), bytes_accessed=0, transcendentals=0),
    )
    return lambda *args: run(*args, *after)


def pass_through(*refs):
    pass


def tie(values, after):
    count = len(values)
    return pl.pallas_call(
        pass_through,
        in_specs=[pl.BlockSpec(memory_space=ANY)] * (count + len(after)),
        out_specs=[pl.BlockSpec(memory_space=ANY)] * count,
        out_shape=[jax.ShapeDtypeStruct(value.shape, value.dtype) for value in values],
        input_output_aliases={at: at for at in range(count)},
    )(*values, *after)


DMA = pltpu.SemaphoreType.DMA


class Sizes:
    def __init__(self, tokens, seqs, shards, rows, up_size, width):
        self.tokens, self.seqs, self.shards, self.rows = tokens, seqs, shards, rows
        self.up_size, self.width = up_size, width
        self.depth = shards // 2
        self.slots = tokens // seqs

    def columns(self, count):
        return pltpu.VMEM((count, self.shards, self.rows, WIDE), BF16)

    def by_rows(self):
        return pltpu.VMEM((self.shards, 4, self.rows, WIDE), BF16)

    def unit_grad(self, more=0):
        return [((2, 2, 2, self.depth, self.rows + more, HALF), BF16, ANY)] * 2


def run_attention_forward(z, pos, counts, x, group, params, after=()):
    t = z.tokens
    return call(
        functools.partial(attention_forward, z.depth, z.seqs, len(after)),
        [SMEM, SMEM] + [VMEM] * 2 + [ANY] * 10,
        [
            ((t, WIDE), F32, VMEM),
            ((t, WIDE), BF16, VMEM),
            ((t, WIDE), F32, VMEM),
            ((t, 128), F32, VMEM),
            ((PAIRS, t, PAIR), BF16, VMEM),
            ((3 * PAIRS, t, PAIR), BF16, VMEM),
            ((z.seqs, PAIRS, z.slots, 2 * KEYS), BF16, ANY),
        ],
        [
            z.columns(4),
            pltpu.VMEM((z.seqs, PAIRS, z.slots, 2 * KEYS), BF16),
            DMA((4,)),
            DMA,
        ],
        21,
        after,
    )(pos, counts, x, params, *group)


def run_mlp_forward(z, pos, first, group, params, after=()):
    t = z.tokens
    return call(
        functools.partial(mlp_forward, z.depth, len(after)),
        [SMEM] + [VMEM] * 2 + [ANY] * 10,
        [
            ((t, WIDE), F32, VMEM),
            ((t, WIDE), BF16, VMEM),
            ((t, WIDE), F32, VMEM),
            ((t, 128), F32, VMEM),
            ((4, t, WIDE), BF16, ANY),
            ((4, t, WIDE), BF16, ANY),
        ],
        [
            z.columns(4),
            z.by_rows(),
            pltpu.VMEM((2, t, WIDE), F32),
            pltpu.VMEM((t, WIDE), BF16),
            pltpu.VMEM((4, t, WIDE), BF16),
            pltpu.VMEM((4, t, WIDE), BF16),
            DMA((4,)),
            DMA((4,)),
            DMA,
            DMA,
        ],
        20,
        after,
    )(pos, first, params, *group)


def run_down_backward(z, pos, grad, hat, scale, params, act, after=()):
    t = z.tokens
    return call(
        functools.partial(down_backward, z.depth, len(after)),
        [SMEM, VMEM] + [ANY] * 4,
        [
            ((t, WIDE), F32, ANY),
            ((8, WIDE), F32, VMEM),
            *z.unit_grad(),
        ],
        [
            pltpu.VMEM((t, WIDE), grad.dtype),
            pltpu.VMEM((t, WIDE), F32),
            pltpu.VMEM((t, 128), F32),
            pltpu.VMEM((t, WIDE), F32),
            pltpu.VMEM((4, t, WIDE), BF16),
            pltpu.VMEM((4, z.shards // 4, 4, z.rows, WIDE), BF16),
            DMA((4,)),
            DMA((4,)),
            DMA,
            DMA,
        ],
        10,
        after,
    )(pos, params, grad, hat, scale, act)


def run_up_backward(z, pos, second, group, slope, first_low, hat, scale, params, after=()):
    t = z.tokens
    return call(
        functools.partial(up_backward, z.depth, len(after)),
        [SMEM, VMEM] + [ANY] * 15,
        [
            ((t, WIDE), F32, ANY),
            ((8, WIDE), F32, VMEM),
            ((1, 4 * WIDE), F32, VMEM),
            *z.unit_grad(),
        ],
        [
            z.columns(4),
            z.by_rows(),
            pltpu.VMEM((4, t, WIDE), BF16),
            pltpu.VMEM((t, WIDE), F32),
            pltpu.VMEM((t, WIDE), BF16),
            pltpu.VMEM((t, WIDE), F32),
            pltpu.VMEM((t, 128), F32),
            pltpu.VMEM((4, z.shards, z.rows, WIDE), BF16),
            DMA((4,)),
            DMA((4,)),
            DMA((4,)),
            DMA,
            DMA,
            DMA((4,)),
            DMA,
            DMA,
        ],
        19,
        after,
    )(pos, params, second, slope, first_low, hat, scale, *group)


def run_attention_backward(z, pos, grad, group, qkv, probs, after=()):
    t = z.tokens
    return call(
        functools.partial(attention_backward, z.depth, z.seqs, len(after)),
        [SMEM] + [ANY] * 13,
        [((3 * PAIRS, t, PAIR), BF16, ANY)],
        [
            pltpu.VMEM((z.shards, z.rows, WIDE), BF16),
            pltpu.VMEM((t, WIDE), F32),
            pltpu.VMEM((3 * PAIRS, t, PAIR), BF16),
            pltpu.VMEM((z.seqs, PAIRS, z.slots, 2 * KEYS), BF16),
            pltpu.VMEM((PAIRS, t, PAIR), BF16),
            pltpu.VMEM((3 * PAIRS, t, PAIR), BF16),
            DMA,
            DMA,
            DMA,
            DMA,
            DMA,
        ],
        13,
        after,
    )(pos, grad, qkv, probs, *group)[0]


def run_qkv_weights(z, pos, grad, grads, ctx, x_low, down_sums, up_sums, up_bias, after=()):
    t = z.tokens
    return call(
        functools.partial(qkv_weights, z.depth, z.up_size, z.width, len(after)),
        [SMEM] + [VMEM] * 3 + [ANY] * 4,
        z.unit_grad(SMALL),
        [
            pltpu.VMEM((t, WIDE), F32),
            pltpu.VMEM((3 * PAIRS, t, PAIR), BF16),
            pltpu.VMEM((PAIRS, t, PAIR), BF16),
            pltpu.VMEM((t, WIDE), BF16),
            pltpu.VMEM((4, z.shards, z.rows, WIDE), BF16),
            pltpu.VMEM((8, WIDE), F32),
            pltpu.VMEM((SMALL, HALF), F32),
            pltpu.VMEM((z.shards, SMALL, HALF), BF16),
            DMA,
            DMA((3,)),
            DMA,
            DMA,
            DMA,
            DMA,
        ],
        8,
        after,
    )(pos, down_sums, up_sums, up_bias, grad, grads, ctx, x_low)


def run_qkv_backward(z, pos, grad, grads, group, after=()):
    t = z.tokens
    return call(
        functools.partial(qkv_backward, z.depth, len(after)),
        [SMEM] + [ANY] * 12,
        [((t, WIDE), F32, VMEM)],
        [
            z.columns(3),
            pltpu.VMEM((3 * PAIRS, t, PAIR), BF16),
            DMA((3,)),
            DMA((3,)),
            DMA,
        ],
        6,
        after,
    )(pos, grad, grads, *group)[0]


def run_finish_first(z, pos, quarters):
    r = z.rows
    return call(
        finish_first,
        [SMEM] + [VMEM] * (4 * LAYERS),
        [
            ((LAYERS, r, 3 * WIDE), F32, VMEM),
            ((LAYERS, r, WIDE), F32, VMEM),
            ((LAYERS, z.up_size), F32, VMEM),
            ((6, LAYERS, z.width), F32, VMEM),
            ((LAYERS, 2, z.width), F32, VMEM),
        ],
        [],
        3,
        limit=SMALL_LIMIT,
    )(pos, *quarters)


def run_finish_second(z, pos, quarters, after=()):
    r = z.rows
    return call(
        functools.partial(finish_second, len(after)),
        [SMEM] + [VMEM] * (4 * LAYERS),
        [
            ((LAYERS, r, 4 * WIDE), F32, VMEM),
            ((LAYERS, 4 * r, WIDE), F32, VMEM),
        ],
        [],
        5,
        after,
        limit=SMALL_LIMIT,
    )(pos, *quarters)


def run_prepare(z, pos, *arrays):
    r = z.rows
    return call(
        prepare,
        [SMEM] + [ANY] * 4 + [VMEM] * 3,
        [
            ((2, 1, r + SMALL, HALF), BF16, VMEM),
            ((2, 2, r, HALF), BF16, VMEM),
            ((2, 3, r, HALF), BF16, VMEM),
        ],
        [
            pltpu.VMEM((SMALL, HALF), F32),
            DMA((LAYERS, 3, 2)),
        ],
        1,
        limit=SMALL_LIMIT,
    )(pos, *arrays)


def run_columns_of(pos, pieces):
    depth, shape = len(pieces), pieces[0].shape
    return call(
        functools.partial(columns_of, depth),
        [SMEM] + [VMEM] * depth,
        [((2, depth) + shape[1:], BF16, VMEM)],
        [],
        2,
    )(pos, *pieces)[0]


def run_split_columns(column, sizes):
    depth, _, _, *rest = column.shape
    outs = [((2, depth, size, *rest), BF16, VMEM) for size in sizes]
    return call(functools.partial(split_columns, sizes), [VMEM], outs, [], 2)(column)


def add_specs(sums, size, place):
    specs = []
    for parts in sums:
        for array, lead in parts:
            rest = array.shape[len(lead) + 1 :]
            specs.append(
                pl.BlockSpec(
                    (None,) * len(lead) + (size,) + rest,
                    lambda *at, lead=lead, rest=len(rest): lead + (place(*at),) + (0,) * rest,
                )
            )
    return specs


def run_add_up(jobs):
    specs, arrays, outs, out_specs = [], [], [], []
    for sums, form in jobs:
        array, lead = sums[0][0]
        depth, *rest = array.shape[len(lead) :]
        size, count = depth // 2, len(sums)
        specs += add_specs(sums, size, lambda step: step)
        arrays += [array for parts in sums for array, _ in parts]
        if form == "joined":
            outs.append((count, depth, *rest))
            out_specs.append(pl.BlockSpec((count, size, *rest), lambda step: (0, step, 0, 0)))
        elif form == "beside":
            outs.append((depth, count, *rest))
            out_specs.append(pl.BlockSpec((size, count, *rest), lambda step: (step, 0, 0, 0)))
        else:
            outs += [(depth, *rest)] * count
            out_specs += [
                pl.BlockSpec((size, *rest), lambda step, zeros=(0,) * len(rest): (step,) + zeros)
            ] * count
    results = list(
        pl.pallas_call(
            functools.partial(add_up, [([len(parts) for parts in sums], form) for sums, form in jobs]),
            grid=(2,),
            in_specs=specs,
            out_specs=out_specs,
            out_shape=[jax.ShapeDtypeStruct(out, BF16) for out in outs],
            compiler_params=pltpu.CompilerParams(vmem_limit_bytes=SMALL_LIMIT),
            cost_estimate=pl.CostEstimate(flops=int(3 * COST), bytes_accessed=0, transcendentals=0),
        )(*arrays)
    )
    grouped = []
    for sums, form in jobs:
        count = 1 if form else len(sums)
        grouped.append(results[:count])
        results = results[count:]
    return grouped


def run_add_up_far(pos, sums):
    array, lead = sums[0][0]
    depth, *rest = array.shape[len(lead) :]
    outs = [jax.ShapeDtypeStruct((2, *rest), F32 if at == 0 else BF16) for at in range(depth)]
    return pl.pallas_call(
        functools.partial(add_up_far, depth, len(sums[0])),
        grid_spec=pltpu.PrefetchScalarGridSpec(
            num_scalar_prefetch=1,
            grid=(depth,),
            in_specs=add_specs(sums, 1, lambda step, pos_ref: lax.rem(pos_ref[3] + step, depth)),
            out_specs=[pl.BlockSpec(out.shape, lambda step, pos_ref: (0, 0, 0)) for out in outs],
        ),
        out_shape=outs,
        compiler_params=pltpu.CompilerParams(vmem_limit_bytes=SMALL_LIMIT),
        cost_estimate=pl.CostEstimate(flops=int(3 * COST), bytes_accessed=0, transcendentals=0),
    )(pos, *[array for parts in sums for array, _ in parts])


def run_add_all(arrays):
    return call(add_all, [VMEM] * len(arrays), [(arrays[0].shape, BF16, VMEM)], [], 1, limit=SMALL_LIMIT)(*arrays)[0]


def run_spread(z, pos, near, far, path):
    return call(
        functools.partial(spread, z.depth, z.up_size, z.width, path),
        [SMEM, ANY, ANY],
        [((SMALL, 4 * WIDE), F32, VMEM)],
        [pltpu.VMEM((2, z.depth, SMALL, HALF), BF16), DMA],
        2,
        limit=SMALL_LIMIT,
    )(pos, near, far)[0]


class Links:
    def __init__(self, rep_size, fsdp_size):
        self.rep_size, self.fsdp_size = rep_size, fsdp_size
        self.depth = fsdp_size // 2
        rep_at, fsdp_at = lax.axis_index("rep"), lax.axis_index("fsdp")
        self.core, self.side = rep_at % 2, (rep_at // 2) % 2
        self.row, self.level = fsdp_at % 2, fsdp_at // 2

    def permute(self, value, target):
        pairs = []
        for rep_at in range(self.rep_size):
            for fsdp_at in range(self.fsdp_size):
                to_rep, to_fsdp = target(rep_at, fsdp_at)
                pairs.append((rep_at * self.fsdp_size + fsdp_at, to_rep * self.fsdp_size + to_fsdp))
        return lax.ppermute(value, AXES, pairs)

    def other_core(self, value):
        return self.permute(value, lambda r, f: (r ^ 1, f))

    def other_side(self, value):
        return self.permute(value, lambda r, f: (r ^ 2, f))

    def other_row(self, value):
        return self.permute(value, lambda r, f: (r, f ^ 1))

    def level_up(self, value, step):
        return self.permute(value, lambda r, f: (r, ((f // 2 + step) % self.depth) * 2 + f % 2))

    def levels(self):
        return [list(range(row, self.fsdp_size, 2)) for row in range(2)]


class Gather:
    def __init__(self, name, links, columns):
        self.name, self.links, self.live, self.moving = name, links, [columns], []

    def scope(self, stage):
        return jax.named_scope("gather_" + self.name + "_" + stage)

    def first(self):
        with self.scope("first"):
            self.moving = [self.links.other_row(self.live[0]), self.links.other_side(self.live[0])]

    def second(self):
        self.live += self.moving
        with self.scope("second"):
            rows, sides = self.live[1:3]
            self.moving = [self.links.other_side(rows[0]), self.links.other_row(sides[1])]
        with self.scope("cores"):
            self.moving += [self.links.other_core(part) for part in self.live[:3]]

    def last(self):
        self.live += self.moving[:2]
        self.far = self.moving[2:]
        with self.scope("last"):
            self.moving = [self.links.other_core(part) for part in self.live[3:5]]

    def arrays(self):
        return self.live + self.far + self.moving


class Sum:
    def __init__(self, name, links, near, far):
        self.name, self.links, self.near, self.sends = name, links, near, [far]
        self.hops = ((links.other_row, links.other_side), (links.other_side, links.other_row))

    def scope(self, stage):
        return jax.named_scope("sum_" + self.name + "_" + stage)

    def cores(self):
        with self.scope("cores"):
            self.moving = [self.links.other_core(self.sends[0])]

    def at(self, far):
        return [[(array, lead + (far,)) for array, lead in parts] for parts in self.parts]

    def came(self):
        self.parts = [[(self.near, (path,)), (self.moving[0], (path,))] for path in range(2)]
        return [(self.at(1), None)]

    def first(self):
        with self.scope("first"):
            self.moving = [self.hops[path][0](self.sends[path]) for path in range(2)]


class Second:
    def __init__(self, name, links, sums):
        self.name, self.links, self.sums = name, links, sums

    def came(self):
        for one in self.sums:
            one.parts = [parts + [(move, ())] for parts, move in zip(one.at(0), one.moving)]
        return [([one.at(1)[path] for one in self.sums], "joined") for path in range(2)]

    def second(self):
        with jax.named_scope("sum_" + self.name + "_second"):
            self.moving = [hops[1](send) for hops, send in zip(self.sums[0].hops, self.sends)]


def add(*steps):
    jobs = [step.came() for step in steps]
    with jax.named_scope("add_" + "_".join(step.name for step in steps)):
        outs = run_add_up([job for step_jobs in jobs for job in step_jobs])
    for step, step_jobs in zip(steps, jobs):
        step.sends = [out for group in outs[: len(step_jobs)] for out in group]
        outs = outs[len(step_jobs) :]


class Share:
    def __init__(self, name, links, second):
        self.name, self.links, self.second = name, links, second

    def scope(self):
        return jax.named_scope("share_" + self.name)

    def parts(self):
        return [
            one.at(0)[path] + [(self.second.moving[path], (unit,))]
            for unit, one in enumerate(self.second.sums)
            for path in range(2)
        ]

    def came(self):
        return [(self.parts(), "beside")]

    def scatter(self):
        with self.scope():
            self.sends = [
                lax.psum_scatter(
                    self.sends[0], "fsdp", scatter_dimension=0, axis_index_groups=self.links.levels()
                )
            ]

    def add_far(self, pos):
        with self.scope():
            self.kept, *self.sends = run_add_up_far(pos, self.parts())

    def levels(self):
        with self.scope():
            self.moving = [self.links.level_up(send, at + 1) for at, send in enumerate(self.sends)]

    def after_levels(self):
        with self.scope():
            self.sends = [run_add_all([self.kept] + self.moving)]

    def copies(self):
        if self.links.rep_size > 4:
            groups = [list(range(first, self.links.rep_size, 4)) for first in range(4)]
            self.sends = [lax.psum(self.sends[0], "rep", axis_index_groups=groups)]

    def sides(self):
        with self.scope():
            self.sends += [self.links.other_side(self.sends[0])]

    def last(self):
        with self.scope():
            self.moving = [self.links.other_core(send) for send in self.sends]

    def quarters(self):
        return self.sends + self.moving


def order(steps, after=()):
    names = ("live", "moving", "sends")
    held = [(step, name) for step in steps for name in (names[:2] if hasattr(step, "live") else names[2:])]
    values = [value for step, name in held for value in getattr(step, name)]
    values = list(tie(values, list(after)))
    token = min(values, key=lambda value: value.size)
    for step, name in held:
        size = len(getattr(step, name))
        setattr(step, name, values[:size])
        values = values[size:]
    return [token]


def shards(
    rep_size, fsdp_size, hidden, region_counts, w_qkv, w_out, w_up, w_down, bias_up, biases, norm_gains, cotangent
):
    links = Links(rep_size, fsdp_size)
    z = Sizes(
        hidden.shape[0], region_counts.shape[0], fsdp_size, w_qkv.shape[1], bias_up.shape[1], biases.shape[2]
    )
    pos = jnp.stack([links.core, links.side, links.row, links.level]).astype(jnp.int32)
    quarters = run_prepare(
        z, pos, w_qkv, w_out, w_up, w_down, bias_up, jnp.transpose(biases, (1, 0, 2)), norm_gains
    )
    kept, groups, params = [], [None] * 4, [None] * 2

    def run_first(layer, states, after):
        return run_attention_forward(z, pos, region_counts, states, groups[2 * layer], params[layer], after)

    def run_second(layer, first, after):
        return run_mlp_forward(z, pos, first, groups[2 * layer + 1], params[layer], after)

    def columns(name, quarter, after=()):
        with jax.named_scope("columns_" + name):
            if after:
                quarter = tie([quarter], list(after))[0]
            pieces = [quarter] + [links.level_up(quarter, step) for step in range(1, links.depth)]
            return run_columns_of(pos, pieces)

    first_0 = Gather("first0", links, columns("first0", quarters[0]))
    first_0.first()
    second_0 = Gather("second0", links, columns("second0", quarters[1], first_0.live))

    order([first_0])
    first_0.second()

    order([first_0, second_0])
    first_0.last()
    second_0.first()
    with jax.named_scope("columns_third"):
        third = tie([quarters[2]], first_0.live[1:3])[0]
        third = lax.all_gather(third, "fsdp", axis_index_groups=links.levels())
    params = [run_spread(z, pos, *first_0.live[:2], layer) for layer in range(LAYERS)]
    groups[0] = first_0.arrays()
    one = run_first(0, hidden, params[1:])

    order([second_0], one[3:4])
    second_0.second()
    with jax.named_scope("columns_third"):
        third = run_split_columns(third, (1, 2))
    first_1, second_1 = (Gather(name, links, part) for name, part in zip(("first1", "second1"), third))

    first_1.first()

    order([second_0, second_1])
    second_0.last()
    second_1.first()
    groups[1] = second_0.arrays()
    two = run_second(0, one[0], ())
    kept.append((hidden, one, two))

    order([first_1], two[3:4])
    first_1.second()

    order([first_1, second_1])
    first_1.last()
    second_1.second()
    groups[2] = first_1.arrays()
    one = run_first(1, two[0], ())

    order([second_1], one[3:4])
    second_1.last()
    groups[3] = second_1.arrays()
    low_states = two[1]
    two = run_second(1, one[0], ())
    kept.append((low_states, one, two))
    output = two[1]

    def run_down(layer, gradient, after):
        _, _, hat, scale, act, _ = kept[layer][2]
        return run_down_backward(z, pos, gradient, hat, scale, params[layer], act, after)

    def run_up(layer, second, after):
        _, first_low, hat, scale, *_ = kept[layer][1]
        return run_up_backward(
            z, pos, second, groups[2 * layer + 1], kept[layer][2][5], first_low, hat, scale, params[layer], after
        )

    def run_attention(layer, first_in, after):
        qkv, probs = kept[layer][1][5:7]
        return run_attention_backward(z, pos, first_in, groups[2 * layer], qkv, probs, after)

    def run_weights(layer, first_in, grads, small, after):
        return run_qkv_weights(z, pos, first_in, grads, kept[layer][1][4], kept[layer][0], *small, after)

    def run_states(layer, first_in, grads, after):
        return run_qkv_backward(z, pos, first_in, grads, groups[2 * layer], after)

    second, down_sums, near, far = run_down(1, cotangent, ())
    down_1 = Sum("down1", links, near, far)

    token = order([down_1])
    down_1.cores()
    first_in, up_sums, up_bias, near, far = run_up(1, second, token)
    up_1 = Sum("up1", links, near, far)

    add(down_1)
    token = order([down_1, up_1])
    down_1.first()
    up_1.cores()
    grads = run_attention(1, first_in, token)

    add(up_1)
    token = order([up_1], [grads] + down_1.moving)
    up_1.first()
    near, far = run_weights(1, first_in, grads, (down_sums, up_sums, up_bias), token)
    first_1 = Sum("first1", links, near, far)
    gradient = run_states(1, first_in, grads, first_1.sends)

    second_1 = Second("second1", links, [up_1, down_1])
    add(second_1)
    token = order([second_1, first_1], [gradient])
    second_1.second()
    first_1.cores()
    second, down_sums, near, far = run_down(0, gradient, token)
    down_0 = Sum("down0", links, near, far)

    share_second_1 = Share("second1", links, second_1)
    order([down_0], second_1.moving + first_1.moving)
    down_0.cores()
    add(first_1, share_second_1)
    order([first_1, share_second_1])
    first_1.first()
    share_second_1.scatter()
    add(down_0)
    token = order([down_0])
    down_0.first()
    first_in, up_sums, up_bias, near, far = run_up(0, second, token)
    up_0 = Sum("up0", links, near, far)

    first_second_1 = Second("first1", links, [first_1])
    order([up_0], first_1.moving + down_0.moving)
    up_0.cores()
    add(first_second_1)
    order([first_second_1])
    first_second_1.second()
    add(up_0)
    token = order([up_0])
    up_0.first()
    grads = run_attention(0, first_in, token)

    second_0 = Second("second0", links, [up_0, down_0])
    share_first_1 = Share("first1", links, first_second_1)
    add(second_0, share_first_1)
    token = order([second_0, share_first_1], [grads])
    second_0.second()
    share_first_1.scatter()
    near, far = run_weights(0, first_in, grads, (down_sums, up_sums, up_bias), token)
    first_0 = Sum("first0", links, near, far)

    share_second_0 = Share("second0", links, second_0)
    order([first_0], second_0.moving)
    first_0.cores()
    add(share_second_0)
    share_second_1.copies()
    token = order([share_second_0, share_second_1], [first_0.near])
    share_second_0.scatter()
    share_second_1.sides()
    gradient = run_states(0, first_in, grads, token)

    add(first_0)
    order([first_0, share_second_1], [gradient])
    first_0.first()
    share_second_1.last()

    first_second_0 = Second("first0", links, [first_0])
    add(first_second_0)
    share_first_1.copies()
    order([first_second_0, share_first_1], share_second_1.moving)
    first_second_0.second()
    share_first_1.sides()

    share_first_0 = Share("first0", links, first_second_0)
    share_first_0.add_far(pos)
    share_second_0.copies()
    order([share_first_0, share_second_0, share_first_1])
    share_first_0.levels()
    share_second_0.sides()
    share_first_1.last()

    share_first_0.after_levels()
    share_first_0.copies()
    order([share_first_0, share_second_0], share_first_1.moving)
    share_first_0.sides()
    share_second_0.last()
    up_grad, down_grad = run_finish_second(z, pos, share_second_0.quarters() + share_second_1.quarters())

    order([share_first_0], [up_grad])
    share_first_0.last()
    qkv_grad, out_grad, up_bias_grad, biases_grad, gains_grad = run_finish_first(
        z, pos, share_first_0.quarters() + share_first_1.quarters()
    )
    biases_grad = jnp.transpose(biases_grad, (1, 0, 2))
    return output, gradient, qkv_grad, out_grad, up_grad, down_grad, up_bias_grad, biases_grad, gains_grad


def solution(mesh):
    in_specs = (
        P(("rep", "fsdp"), None),
        P(("rep", "fsdp")),
        P(None, "fsdp", None),
        P(None, "fsdp", None),
        P(None, "fsdp", None),
        P(None, "fsdp", None),
        P(None, "fsdp"),
        P(None, None, "fsdp"),
        P(None, None, "fsdp"),
        P(("rep", "fsdp"), None),
    )
    out_specs = (
        P(("rep", "fsdp"), None),
        P(("rep", "fsdp"), None),
        P(None, "fsdp", None),
        P(None, "fsdp", None),
        P(None, "fsdp", None),
        P(None, "fsdp", None),
        P(None, "fsdp"),
        P(None, None, "fsdp"),
        P(None, None, "fsdp"),
    )
    local = functools.partial(shards, mesh.shape["rep"], mesh.shape["fsdp"])
    return jax.shard_map(local, mesh=mesh, in_specs=in_specs, out_specs=out_specs, check_vma=False)
```

```python
import functools

import jax
import jax.numpy as jnp
from jax import lax
from jax.experimental import pallas as pl
from jax.experimental.pallas import tpu as pltpu
from jax.sharding import PartitionSpec as P

HEADS = 12
HEAD_DIM = 64
LAYERS = 2
TEXT = 128
KEYS = 256
WIDE = 768
HALF = WIDE // 2
PAIR = 2 * HEAD_DIM
PAIRS = HEADS // 2
EPSILON = 1e-12
MASKED = -1000000000.0
AXES = ("rep", "fsdp")
COST = 1.15e9
SMALL = 16
VMEM_LIMIT = 64 * 1024 * 1024
SMALL_LIMIT = VMEM_LIMIT


def low(value):
    return value.astype(jnp.bfloat16)


def full(value):
    return value.astype(jnp.float32)


def mm(left, right):
    return jnp.dot(left, right, preferred_element_type=jnp.float32)


def mm_t(left, right):
    return lax.dot_general(
        left, right, (((1,), (1,)), ((), ())), preferred_element_type=jnp.float32
    )


def t_mm(left, right):
    return lax.dot_general(
        left, right, (((0,), (0,)), ((), ())), preferred_element_type=jnp.float32
    )


def flip(at, by):
    return 1 - at if by else at


class Place:
    def __init__(self, pos_ref):
        self.core, self.side = pos_ref[0], pos_ref[1]
        self.row, self.level = pos_ref[2], pos_ref[3]

    def shard(self, level, far_row):
        return level * 2 + flip(self.row, far_row)


def half_lanes(at):
    return pl.ds(pl.multiple_of(at * HALF, HALF), HALF)


def part_of(arrays, path, far_core, far_side, far_row):
    arrays = arrays[5 * far_core : 5 * far_core + 5]
    if far_side and far_row:
        return arrays[3 + path]
    return arrays[2 * far_side + far_row].at[path]


def load_unit(place, arrays, unit, whole, sems, by_rows):
    rows = pl.ds(0, whole.shape[3])
    for far_side in range(2):
        for path in range(2):
            block = flip(place.side, far_side) * 2 + path
            for far_core in range(2):
                lanes = half_lanes(flip(place.core, far_core))
                for far_row in range(2):
                    row = flip(place.row, far_row)
                    part = part_of(arrays, path, far_core, far_side, far_row).at[:, unit, rows]
                    if by_rows:
                        copy(part, whole.at[:, row, block, :, lanes], sems)
                    else:
                        copy(part, whole.at[block, :, row, :, lanes], sems.at[block])


def load_block(place, block, arrays, whole, sem):
    path = block % 2
    rows = pl.ds(0, whole.shape[2])
    needed_side = place.side if block // 2 == 0 else 1 - place.side
    for far_side in range(2):

        @pl.when(needed_side == far_side)
        def _():
            for far_core in range(2):
                lanes = half_lanes(flip(place.core, far_core))
                for far_row in range(2):
                    part = part_of(arrays, path, far_core, far_side, far_row).at[:, 0, rows]
                    copy(part, whole.at[:, flip(place.row, far_row), :, lanes], sem)


def copy(source, target, sem):
    pltpu.make_async_copy(source, target, sem).start()


def wait_all(ref, sem):
    pltpu.make_async_copy(ref, ref, sem).wait()


def either(choice, one, other):
    return other + choice * (one - other)


def either(choice, one, other):
    return other + choice * (one - other)


def sum_place(out, block, far_row, far_side):
    path = block % 2
    return out.at[path, either(path, far_side, far_row), either(path, far_row, far_side)]


def side_distance(place, block):
    return either(place.side, 1 - block // 2, block // 2)


def store_columns(place, block, held, outs, sem):
    rows = pl.ds(0, held.shape[2])
    far_side = side_distance(place, block)
    for far_core, out in enumerate(outs):
        lanes = half_lanes(flip(place.core, far_core))
        for far_row in range(2):
            source = held.at[:, flip(place.row, far_row), :, lanes]
            copy(source, sum_place(out, block, far_row, far_side).at[:, rows], sem)


def store_rows(place, levels, held, outs, sem):
    for far_core, out in enumerate(outs):
        lanes = half_lanes(flip(place.core, far_core))
        for block in range(4):
            far_side = side_distance(place, block)
            for far_row in range(2):
                source = held.at[levels, flip(place.row, far_row), block, :, lanes]
                copy(source, sum_place(out, block, far_row, far_side).at[levels], sem)


def chunks(rows):
    edges = [rows // 16 * at // 4 * 16 for at in range(4)] + [rows]
    return [(start, end - start) for start, end in zip(edges, edges[1:])]


def normalize(value):
    centered = value - jnp.mean(value, axis=-1, keepdims=True)
    scale = lax.rsqrt(jnp.mean(centered * centered, axis=-1, keepdims=True) + EPSILON)
    return centered * scale, scale


def norm_backward(grad, hat, scale, gain):
    direct = grad * gain
    return (
        direct
        - jnp.mean(direct, axis=-1, keepdims=True)
        - hat * jnp.mean(direct * hat, axis=-1, keepdims=True)
    ) * scale


def gelu_and_slope(value):
    size = jnp.abs(value) * 0.7071067811865476
    t = 1.0 / (1.0 + 0.3275911 * size)
    series = t * (
        0.127414796
        + t * (-0.142248368 + t * (0.7107068705 + t * (-0.7265760135 + t * 0.5307027145)))
    )
    bell = jnp.exp(-0.5 * value * value)
    tail = series * bell
    below = jnp.where(value >= 0, 1.0 - tail, tail)
    return value * below, below + value * bell * 0.3989422804014327


def head_masks(value, lane):
    none = jnp.zeros_like(value)
    return jnp.concatenate(
        [jnp.where(lane < HEAD_DIM, value, none), jnp.where(lane < HEAD_DIM, none, value)], 0
    )


def side_by_side(ref, block):
    return jnp.concatenate([ref[block * PAIRS + pair] for pair in range(PAIRS)], 1)


def attention_forward(depth, seqs, extra, pos_ref, counts_ref, x_ref, params_ref, *refs):
    parts, refs = refs[:10], refs[10 + extra :]
    first_out, first_low_out, hat_out, scale_out, ctx_out, qkv_out, probs_ref = refs[:7]
    x, params, first, first_low, hat, scale, ctx, qkv, weight, held, *sems = refs[7:]
    x_sem, params_sem, row_sem, ctx_sem, qkv_sem, weight_sem, held_sem = sems
    place = Place(pos_ref)
    copy(x_ref, x, x_sem)
    load_unit(place, parts, 0, weight, weight_sem, False)
    copy(params_ref.at[:, pl.ds(0, WIDE)], params, params_sem)
    tokens = x.shape[0]
    slots = tokens // seqs
    wait_all(x, x_sem)
    x_low = low(x[...])
    wait_all(params, params_sem)

    for block in range(3):
        wait_all(weight.at[block], weight_sem.at[block])

    def project(block, carry):
        out = mm(x_low, weight[block].reshape(WIDE, WIDE))
        bias = params[pl.ds(1 + block // 2, 1), :]
        out = low(out + jnp.where(block == 1, jnp.zeros_like(bias), bias))
        for pair in range(PAIRS):
            qkv[block * PAIRS + pair] = out[:, pair * PAIR : (pair + 1) * PAIR]
        return carry

    lax.fori_loop(0, 3, project, 0)
    copy(qkv, qkv_out, qkv_sem)
    lane = lax.broadcasted_iota(jnp.int32, (KEYS, PAIR), 1)
    key = lax.broadcasted_iota(jnp.int32, (slots, KEYS), 1)

    def pair_step(step, carry):
        seq, pair = step // PAIRS, lax.rem(step, PAIRS)
        rows = pl.ds(pl.multiple_of(seq * slots, 16), slots)
        key_rows = pl.ds(pl.multiple_of(seq * slots, 16), KEYS)
        valid = key < TEXT + counts_ref[seq]
        q = qkv[pair, rows, :] * jnp.bfloat16(HEAD_DIM**-0.5)
        scores = mm_t(q, head_masks(qkv[PAIRS + pair, key_rows, :], lane))
        halves = []
        for half in range(2):
            part = jnp.where(valid, scores[:, half * KEYS : (half + 1) * KEYS], MASKED)
            part = jnp.exp(part - jnp.max(part, axis=-1, keepdims=True))
            halves.append(low(part * (1.0 / jnp.sum(part, axis=-1, keepdims=True))))
        probs = jnp.concatenate(halves, 1)
        held[seq, pair] = probs
        copy(held.at[seq, pair], probs_ref.at[seq, pair], held_sem)
        ctx[pair, rows, :] = low(mm(probs, head_masks(qkv[2 * PAIRS + pair, key_rows, :], lane)))
        return carry

    lax.fori_loop(0, seqs * PAIRS, pair_step, 0, unroll=2)
    copy(ctx, ctx_out, ctx_sem)
    wait_all(weight.at[3], weight_sem.at[3])
    first[...] = mm(side_by_side(ctx, 0), weight[3].reshape(WIDE, WIDE))
    outs = ((first, first_out), (first_low, first_low_out), (hat, hat_out), (scale, scale_out))
    for start, size in chunks(tokens):
        rows = pl.ds(start, size)
        normal, factor = normalize(full(x[rows, :]) + (first[rows, :] + params[3:4, :]))
        hat[rows, :] = normal
        scale[rows, :] = jnp.broadcast_to(factor, (size, 128))
        value = normal * params[7:8, :] + params[4:5, :]
        first[rows, :] = value
        first_low[rows, :] = low(value)
        for at, (source, target) in enumerate(outs):
            copy(source.at[rows], target.at[rows], row_sem.at[at])
    for at, (source, _) in enumerate(outs):
        wait_all(source, row_sem.at[at])
    wait_all(ctx, ctx_sem)
    wait_all(qkv, qkv_sem)
    wait_all(held, held_sem)


def mlp_forward(depth, extra, pos_ref, first_ref, params_ref, *refs):
    parts, refs = refs[:10], refs[10 + extra :]
    out_out, out_low_out, hat_out, scale_out, act_ref, slope_ref = refs[:6]
    params, out, out_low, hat, scale, up, down, pre, first_low, act, slope, *sems = refs[6:]
    params_sem, first_sem, row_sem, up_sem, down_sem, act_sem, slope_sem = sems
    place = Place(pos_ref)
    copy(first_ref, out, first_sem)
    load_unit(place, parts, 0, up, up_sem, False)
    copy(params_ref, params, params_sem)
    load_unit(place, parts, 1, down, down_sem, True)
    tokens = out.shape[0]
    half = tokens // 2
    levels = depth // 4
    wait_all(out, first_sem)
    first_low[...] = low(out[...])
    act[3, half:, :] = jnp.zeros((half, WIDE), BF16)
    for tile in range(4):
        wait_all(up.at[tile], up_sem.at[tile])
    pre[0] = mm(first_low[...], up[0].reshape(WIDE, WIDE))
    wait_all(params, params_sem)
    out[...] += params[5:6, :WIDE]
    wait_all(down, down_sem)

    def half_rows(step):
        return pl.ds(pl.multiple_of(lax.rem(step, 2) * half, 16), half)

    def below(step):
        tile, rows = step // 2, half_rows(step)
        weight = down[pl.ds(tile * levels, levels)].reshape(WIDE, WIDE)
        out[rows, :] += mm(act[tile, rows, :], weight)

    def half_step(step, carry):
        tile, rows = step // 2, half_rows(step)
        slot, later = lax.rem(tile, 2), lax.rem(tile + 1, 4)
        bias = params[0:1, pl.ds(pl.multiple_of(tile * WIDE, WIDE), WIDE)]
        below(lax.rem(step + 7, 8))
        pre[1 - slot, rows, :] = mm(first_low[rows, :], up[later].reshape(WIDE, WIDE))
        gelu, rise = gelu_and_slope(pre[slot, rows, :] + bias)
        act[tile, rows, :] = low(gelu)
        slope[tile, rows, :] = low(rise)
        copy(slope.at[tile, rows], slope_ref.at[tile, rows], slope_sem)
        copy(act.at[tile, rows], act_ref.at[tile, rows], act_sem)
        return carry

    lax.fori_loop(0, 8, half_step, 0)
    below(7)
    outs = ((out, out_out), (out_low, out_low_out), (hat, hat_out), (scale, scale_out))
    for start, size in chunks(tokens):
        rows = pl.ds(start, size)
        normal, factor = normalize(out[rows, :])
        hat[rows, :] = normal
        scale[rows, :] = jnp.broadcast_to(factor, (size, 128))
        value = normal * params[8:9, :WIDE] + params[6:7, :WIDE]
        out[rows, :] = value
        out_low[rows, :] = low(value)
        for at, (source, target) in enumerate(outs):
            copy(source.at[rows], target.at[rows], row_sem.at[at])
    for at, (source, _) in enumerate(outs):
        wait_all(source, row_sem.at[at])
    wait_all(slope, slope_sem)
    wait_all(act, act_sem)


def load_rows(pairs, sem):
    for at, (start, size) in enumerate(chunks(pairs[0][0].shape[0])):
        for source, target in pairs:
            rows = pl.ds(start, size)
            copy(source.at[rows], target.at[rows], sem.at[at])


def norm_step(grad, hat, scale, gain, out, out_ref, sums, sums_ref, waits, sem, out_sem, sums_sem):
    totals = [0.0, 0.0, 0.0]
    for at, (start, size) in enumerate(chunks(grad.shape[0])):
        rows = pl.ds(start, size)
        for array in waits:
            wait_all(array.at[rows], sem.at[at])
        value, hat_rows = full(grad[rows, :]), hat[rows, :]
        grad_in = norm_backward(value, hat_rows, scale[rows, :][:, :1], gain)
        out[rows, :] = grad_in
        copy(out.at[rows], out_ref.at[rows], out_sem)
        for number, part in enumerate((value * hat_rows, value, full(low(grad_in)))):
            totals[number] += jnp.sum(part, axis=0, keepdims=True)
    sums[...] = jnp.zeros_like(sums)
    for number in range(3):
        sums[number : number + 1, :] = totals[number]
    copy(sums, sums_ref, sums_sem)


def down_backward(depth, extra, pos_ref, params_ref, grad_ref, hat_ref, scale_ref, act_ref, *refs):
    second_ref, sums_ref, near_ref, far_ref = refs[extra : extra + 4]
    params, sums, grad, hat, scale, second, act, held, *sems = refs[extra + 4 :]
    params_sem, sums_sem, row_sem, act_sem, out_sem, held_sem = sems
    place = Place(pos_ref)
    copy(params_ref.at[:, pl.ds(0, WIDE)], params, params_sem)
    load_rows([(grad_ref, grad), (hat_ref, hat), (scale_ref, scale)], row_sem)
    for tile in range(4):
        copy(act_ref.at[tile], act.at[tile], act_sem.at[tile])
    wait_all(params, params_sem)
    norm_step(
        grad, hat, scale, params[8:9, :], second, second_ref, sums, sums_ref, (grad, hat, scale), row_sem, out_sem, sums_sem
    )
    grad_low = low(second[...])
    for tile in range(4):
        wait_all(act.at[tile], act_sem.at[tile])

    levels = depth // 4

    def tile_step(tile, carry):
        held[pl.ds(tile * levels, levels)] = low(t_mm(act[tile], grad_low)).reshape((levels,) + held.shape[1:])
        return carry

    for start in (0, 2):
        lax.fori_loop(start, start + 2, tile_step, 0)
        store_rows(place, pl.ds(start * levels, 2 * levels), held, (near_ref, far_ref), held_sem)
    wait_all(second, out_sem)
    wait_all(sums, sums_sem)
    wait_all(held, held_sem)


def up_backward(
    depth, extra, pos_ref, params_ref, second_ref, slope_ref, first_low_ref, hat_ref, scale_ref, *refs
):
    parts, refs = refs[:10], refs[10 + extra :]
    first_in_ref, sums_ref, up_grad_ref, near_ref, far_ref = refs[:5]
    params, sums, up_grad, up, down, slope, total, first_low, hat, scale, held, *sems = refs[5:]
    params_sem, sums_sem, up_grad_sem, up_sem, down_sem, slope_sem, second_sem, first_sem, row_sem, out_sem, held_sem = sems
    place = Place(pos_ref)
    copy(second_ref, total, second_sem)
    load_unit(place, parts, 1, down, down_sem, True)
    copy(slope_ref, slope, slope_sem)
    levels = depth // 4
    wait_all(total, second_sem)
    grad_low = low(total[...])
    wait_all(down, down_sem)
    wait_all(slope, slope_sem)
    load_unit(place, parts, 0, up, up_sem, False)
    copy(first_low_ref, first_low, first_sem)
    load_rows([(hat_ref, hat), (scale_ref, scale)], row_sem)
    copy(params_ref.at[:, pl.ds(0, WIDE)], params, params_sem)

    def pre_step(tile, carry):
        weight = down[pl.ds(tile * levels, levels)].reshape(WIDE, WIDE)
        grad = low(mm_t(grad_low, weight) * full(slope[tile]))
        slope[tile] = grad
        up_grad[:, pl.ds(pl.multiple_of(tile * WIDE, WIDE), WIDE)] = jnp.sum(
            full(grad), axis=0, keepdims=True
        )
        return carry

    lax.fori_loop(0, 4, pre_step, 0)
    copy(up_grad, up_grad_ref, up_grad_sem)
    wait_all(first_low, first_sem)
    for tile in range(4):
        wait_all(up.at[tile], up_sem.at[tile])

    def tile_step(tile, carry):
        held[tile] = low(t_mm(first_low[...], slope[tile])).reshape(held.shape[1:])
        total[...] += mm_t(slope[tile], up[tile].reshape(WIDE, WIDE))
        store_columns(place, tile, held.at[tile], (near_ref, far_ref), held_sem)
        return carry

    lax.fori_loop(0, 4, tile_step, 0)
    wait_all(params, params_sem)
    norm_step(
        total, hat, scale, params[7:8, :], total, first_in_ref, sums, sums_ref, (hat, scale), row_sem, out_sem, sums_sem
    )
    wait_all(total, out_sem)
    wait_all(sums, sums_sem)
    wait_all(up_grad, up_grad_sem)
    wait_all(held, held_sem)


def attention_backward(depth, seqs, extra, pos_ref, grad_ref, qkv_ref, probs_ref, *refs):
    parts, refs = refs[:10], refs[10 + extra :]
    grads_ref = refs[0]
    weight, grad, qkv, probs, ctx_grad, grads, weight_sem, grad_sem, qkv_sem, probs_sem, out_sem = refs[1:]
    place = Place(pos_ref)
    copy(grad_ref, grad, grad_sem)
    load_block(place, 3, parts, weight, weight_sem)
    copy(qkv_ref, qkv, qkv_sem)
    copy(probs_ref, probs, probs_sem)
    tokens = grad.shape[0]
    slots = tokens // seqs
    wait_all(grad, grad_sem)
    wait_all(weight, weight_sem)
    from_out = low(mm_t(low(grad[...]), weight[...].reshape(WIDE, WIDE)))
    for pair in range(PAIRS):
        ctx_grad[pair] = from_out[:, pair * PAIR : (pair + 1) * PAIR]
    wait_all(qkv, qkv_sem)
    wait_all(probs, probs_sem)
    lane = lax.broadcasted_iota(jnp.int32, (KEYS, PAIR), 1)

    def pair_step(step, carry):
        seq, pair = step // PAIRS, lax.rem(step, PAIRS)
        start = pl.multiple_of(seq * slots, 16)
        rows, key_rows = pl.ds(start, slots), pl.ds(start, KEYS)
        q = qkv[pair, rows, :]
        out_grad = ctx_grad[pair, rows, :]
        weights = probs[seq, pair]
        probs_grad = mm_t(out_grad, head_masks(qkv[2 * PAIRS + pair, key_rows, :], lane))
        halves = []
        for half in range(2):
            lanes = slice(half * KEYS, (half + 1) * KEYS)
            weight_part, grad_part = full(weights[:, lanes]), probs_grad[:, lanes]
            dot = jnp.sum(weight_part * grad_part, axis=-1, keepdims=True)
            halves.append(low(weight_part * (grad_part - dot)))
        scores_grad = jnp.concatenate(halves, 1)
        q_grad = mm(scores_grad, head_masks(qkv[PAIRS + pair, key_rows, :], lane)) * HEAD_DIM**-0.5
        grads[pair, rows, :] = low(q_grad)
        k_grad = t_mm(q, scores_grad) * HEAD_DIM**-0.5
        v_grad = t_mm(out_grad, weights)
        for at, value in ((PAIRS, k_grad), (2 * PAIRS, v_grad)):
            value = jnp.concatenate([value[:HEAD_DIM, :KEYS], value[HEAD_DIM:, KEYS:]], 0)
            grads[at + pair, key_rows, :] = low(value.T)
            grads[at + pair, pl.ds(pl.multiple_of(start + KEYS, 16), slots - KEYS), :] = jnp.zeros(
                (slots - KEYS, PAIR), BF16
            )
        for at in range(3):
            copy(grads.at[at * PAIRS + pair, rows], grads_ref.at[at * PAIRS + pair, rows], out_sem)
        return carry

    lax.fori_loop(0, seqs * PAIRS, pair_step, 0, unroll=2)
    wait_all(grads, out_sem)


def qkv_weights(
    depth, up_size, width, with_states, extra, pos_ref, down_sums_ref, up_sums_ref, up_bias_ref, grad_ref, grads_ref, ctx_ref, x_ref,
    *refs,
):
    parts, refs = refs[: 10 * with_states], refs[10 * with_states + extra :]
    outs, refs = refs[:2], refs[2:]
    if with_states:
        x_grad_ref, *refs = refs
        *refs, weight, weight_sem, out_sem = refs
    down_sums, up_sums, up_bias, bias_sem, *refs = refs
    grad, grads, ctx, x_low, held, sums, block_rows, small, grad_sem, grads_sem, ctx_sem, x_sem, held_sem, small_sem = refs
    place = Place(pos_ref)
    copy(x_ref, x_low, x_sem)
    for block in range(3):
        panels = pl.ds(block * PAIRS, PAIRS)
        copy(grads_ref.at[panels], grads.at[panels], grads_sem.at[block])
    copy(ctx_ref, ctx, ctx_sem)
    copy(grad_ref, grad, grad_sem)
    if with_states:
        for block in range(3):
            load_block(place, block, parts, weight.at[block], weight_sem.at[block])
    biases = ((down_sums_ref, down_sums), (up_sums_ref, up_sums), (up_bias_ref, up_bias))
    for at, (source, target) in enumerate(biases):
        copy(source, target, bias_sem.at[at])
    wait_all(x_low, x_sem)
    for block in range(3):
        wait_all(grads.at[pl.ds(block * PAIRS, PAIRS)], grads_sem.at[block])

    def block_step(block, carry):
        part = side_by_side(grads, block)
        sums[pl.ds(block, 1), :] = jnp.sum(full(part), axis=0, keepdims=True)
        held[block] = low(t_mm(x_low[...], part)).reshape(held.shape[1:])
        store_columns(place, block, held.at[block], outs, held_sem)
        return carry

    lax.fori_loop(0, 3, block_step, 0)
    sums[1:2, :] = sums[2:3, :]
    for at, (_, target) in enumerate(biases):
        wait_all(target, bias_sem.at[at])
    block_rows[...] = jnp.zeros_like(block_rows)
    for shard in range(2 * depth):
        lanes = slice(shard * width, (shard + 1) * width)
        block_rows[0:1, :up_size] = up_bias[:, shard * up_size : (shard + 1) * up_size]
        block_rows[1:3, :width] = sums[0:2, lanes]
        for row, (ref, at) in enumerate(
            ((up_sums, 2), (up_sums, 1), (down_sums, 2), (down_sums, 1), (up_sums, 0), (down_sums, 0))
        ):
            block_rows[3 + row : 4 + row, :width] = ref[at : at + 1, lanes]
        small[shard // 2, shard % 2] = low(block_rows[...])
    rows = held.shape[3]
    for out in outs:
        for far_row in range(2):
            for far_side in range(2):
                for path in range(2):
                    target = sum_place(out, path, far_row, far_side).at[:, pl.ds(rows, SMALL)]
                    copy(small.at[:, flip(place.row, far_row)], target, small_sem)
    wait_all(ctx, ctx_sem)
    wait_all(grad, grad_sem)
    held[3] = low(t_mm(side_by_side(ctx, 0), low(grad[...]))).reshape(held.shape[1:])
    store_columns(place, 3, held.at[3], outs, held_sem)
    if with_states:
        for block in range(3):
            wait_all(weight.at[block], weight_sem.at[block])

        def state_step(block, carry):
            grad[...] += mm_t(side_by_side(grads, block), weight[block].reshape(WIDE, WIDE))
            return carry

        lax.fori_loop(0, 3, state_step, 0)
        copy(grad, x_grad_ref, out_sem)
        wait_all(grad, out_sem)
    wait_all(held, held_sem)
    for _ in range(8):
        wait_all(small, small_sem)


def qkv_backward(depth, extra, pos_ref, grad_ref, grads_ref, *refs):
    parts, refs = refs[:10], refs[10 + extra :]
    x_grad_ref, total, weight, grads, weight_sem, grads_sem, grad_sem, out_sem = refs
    place = Place(pos_ref)
    copy(grads_ref, grads, grads_sem)
    for block in range(3):
        load_block(place, block, parts, weight.at[block], weight_sem.at[block])
    copy(grad_ref, total, grad_sem)
    wait_all(grads, grads_sem)
    for block in range(3):
        wait_all(weight.at[block], weight_sem.at[block])
    wait_all(total, grad_sem)

    def block_step(block, carry):
        total[...] += mm_t(side_by_side(grads, block), weight[block].reshape(WIDE, WIDE))
        return carry

    lax.fori_loop(0, 3, block_step, 0)
    copy(total, x_grad_ref, out_sem)
    wait_all(total, out_sem)


def finish_first(extra, pos_ref, *refs):
    core, side = pos_ref[0], pos_ref[1]
    quarters, refs = refs[: 4 * LAYERS], refs[4 * LAYERS + extra :]
    qkv_ref, out_ref, up_bias_ref, biases_ref, gains_ref = refs
    rows = qkv_ref.shape[1]
    for layer in range(LAYERS):
        small = full(quarters[4 * layer][0, rows : rows + SMALL, :])
        up_bias_ref[layer : layer + 1, :] = small[0:1, : up_bias_ref.shape[1]]
        biases_ref[:, layer] = small[1:7, : biases_ref.shape[2]]
        gains_ref[layer] = small[7:9, : gains_ref.shape[2]]
        for far in range(4):
            part = quarters[4 * layer + far]
            at_core, at_side = flip(core, far // 2), flip(side, far % 2)
            half = at_core * HALF
            lanes = pl.ds(pl.multiple_of(at_side * (2 * WIDE) + half, HALF), HALF)
            qkv_ref[layer, :, lanes] = full(part[0, :rows, :])
            last = full(part[1, :rows, :])

            @pl.when(at_side == 0)
            def _():
                qkv_ref[layer, :, pl.ds(pl.multiple_of(WIDE + half, HALF), HALF)] = last

            @pl.when(at_side == 1)
            def _():
                out_ref[layer, :, half_lanes(at_core)] = last


def finish_second(extra, pos_ref, *refs):
    core, side = pos_ref[0], pos_ref[1]
    quarters, (up_ref, down_ref) = refs[: 4 * LAYERS], refs[4 * LAYERS + extra :]
    rows = up_ref.shape[1]
    for layer in range(LAYERS):
        for far in range(4):
            part = quarters[4 * layer + far]
            at_core, at_side = flip(core, far // 2), flip(side, far % 2)
            for block in range(2):
                lanes = pl.ds(
                    pl.multiple_of(at_side * (2 * WIDE) + block * WIDE + at_core * HALF, HALF), HALF
                )
                up_ref[layer, :, lanes] = full(part[block])
                down_rows = pl.ds(pl.multiple_of((at_side * 2 + block) * rows, rows), rows)
                down_ref[layer, down_rows, half_lanes(at_core)] = full(part[2 + block])


def prepare(
    pos_ref, qkv_ref, out_ref, up_ref, down_ref, up_bias_ref, biases_ref, gains_ref,
    first_group, second_group, third_group, rows_of, sem,
):
    core, side = pos_ref[0], pos_ref[1]
    rows = out_ref.shape[1]
    up_size, width = up_bias_ref.shape[1], biases_ref.shape[2]
    for layer in range(LAYERS):
        for block in range(2):
            at = side * 2 + block
            lanes = pl.ds(pl.multiple_of(at * WIDE + core * HALF, HALF), HALF)
            if layer == 0:
                target = first_group.at[block, 0, pl.ds(0, rows)]
                up, down = second_group.at[block, 0], second_group.at[block, 1]
            else:
                target, up, down = (third_group.at[block, unit] for unit in range(3))
            if block == 0:
                pltpu.make_async_copy(qkv_ref.at[layer, :, lanes], target, sem.at[layer, 0, 0]).start()
            else:

                @pl.when(side == 0)
                def _():
                    lanes = pl.ds(pl.multiple_of(WIDE + core * HALF, HALF), HALF)
                    pltpu.make_async_copy(qkv_ref.at[layer, :, lanes], target, sem.at[layer, 0, 1]).start()

                @pl.when(side == 1)
                def _():
                    pltpu.make_async_copy(
                        out_ref.at[layer, :, half_lanes(core)], target, sem.at[layer, 0, 1]
                    ).start()

            pltpu.make_async_copy(up_ref.at[layer, :, lanes], up, sem.at[layer, 1, block]).start()
            down_rows = pl.ds(pl.multiple_of(at * rows, rows), rows)
            pltpu.make_async_copy(
                down_ref.at[layer, down_rows, half_lanes(core)], down, sem.at[layer, 2, block]
            ).start()
    for layer in range(LAYERS):
        rows_of[...] = jnp.zeros_like(rows_of)
        rows_of[0:1, :up_size] = full(up_bias_ref[layer : layer + 1, :])
        rows_of[1:7, :width] = full(biases_ref[:, layer])
        rows_of[7:9, :width] = full(gains_ref[layer])
        first_group[layer, 0, rows : rows + SMALL, :] = low(rows_of[...])
    for layer in range(LAYERS):
        for block in range(2):
            for unit in range(3):
                if layer:
                    part = third_group.at[block, unit]
                elif unit:
                    part = second_group.at[block, unit - 1]
                else:
                    part = first_group.at[block, 0, pl.ds(0, rows)]
                wait_all(part, sem.at[layer, unit, block])


def columns_of(depth, pos_ref, *refs):
    level, out = pos_ref[3], refs[-1]
    for path in range(2):
        for far_level, piece in enumerate(refs[:depth]):
            out[path, lax.rem(level + depth - far_level, depth)] = piece[path]


def split_columns(sizes, column_ref, *refs):
    start = 0
    for size, out in zip(sizes, refs[-len(sizes) :]):
        for path in range(2):
            out[path] = column_ref[:, path, start : start + size]
        start += size


def add_up(jobs, *refs):
    start, out = 0, sum(sum(counts) for counts, _ in jobs)
    for counts, form in jobs:
        for at, count in enumerate(counts):
            total = full(refs[start][...])
            for ref in refs[start + 1 : start + count]:
                total = total + full(ref[...])
            if form == "joined":
                refs[out][at] = low(total)
            elif form == "beside":
                refs[out][:, at] = low(total)
            else:
                refs[out + at][...] = low(total)
            start += count
        out += 1 if form else len(counts)


def add_up_far(depth, count, pos_ref, *refs):
    inputs, outs = refs[: 2 * count], refs[2 * count :]
    step = pl.program_id(0)
    for path in range(2):
        total = full(inputs[path * count][...])
        for ref in inputs[path * count + 1 : (path + 1) * count]:
            total = total + full(ref[...])
        for at in range(depth):

            @pl.when(step == at)
            def _():
                outs[at][path] = total[0].astype(outs[at].dtype)


def add_all(*refs):
    total = full(refs[0][...])
    for ref in refs[1:-1]:
        total = total + full(ref[...])
    refs[-1][...] = low(total)


def spread(depth, up_size, width, path, pos_ref, near_ref, far_ref, params_ref, small, sem):
    place = Place(pos_ref)
    rows = near_ref.shape[3] - SMALL
    for far_row, part in enumerate((near_ref.at[path], far_ref.at[path])):
        for level in range(depth):
            pltpu.make_async_copy(
                part.at[level, 0, pl.ds(rows, SMALL)], small.at[far_row, level], sem
            ).start()
    wait_all(small, sem)
    ups, others = 0.0, 0.0
    for far_row in range(2):
        for level in range(depth):
            shard = place.shard(level, far_row)
            block = full(small[far_row, level])
            up = jnp.concatenate([block, jnp.zeros((SMALL, 4 * WIDE - HALF), F32)], 1)
            ups += pltpu.roll(up, shard * up_size, 1)
            other = jnp.concatenate([block[:, :128], jnp.zeros((SMALL, WIDE - 128), F32)], 1)
            others += pltpu.roll(other, shard * width, 1)
    params_ref[...] = ups
    params_ref[1:9, :WIDE] = others[1:9]


VMEM = pltpu.MemorySpace.VMEM
SMEM = pltpu.MemorySpace.SMEM
ANY = pl.ANY
F32 = jnp.float32
BF16 = jnp.bfloat16


def call(kernel, spaces, outs, scratch, cost, after=(), limit=VMEM_LIMIT):
    run = pl.pallas_call(
        kernel,
        in_specs=[pl.BlockSpec(memory_space=space) for space in spaces + [ANY] * len(after)],
        out_specs=[pl.BlockSpec(memory_space=space) for _, _, space in outs],
        out_shape=[jax.ShapeDtypeStruct(shape, dtype) for shape, dtype, _ in outs],
        scratch_shapes=scratch,
        compiler_params=pltpu.CompilerParams(vmem_limit_bytes=limit),
        cost_estimate=pl.CostEstimate(flops=int(cost * COST), bytes_accessed=0, transcendentals=0),
    )
    return lambda *args: run(*args, *after)


def pass_through(*refs):
    pass


def tie(values, after):
    count = len(values)
    return pl.pallas_call(
        pass_through,
        in_specs=[pl.BlockSpec(memory_space=ANY)] * (count + len(after)),
        out_specs=[pl.BlockSpec(memory_space=ANY)] * count,
        out_shape=[jax.ShapeDtypeStruct(value.shape, value.dtype) for value in values],
        input_output_aliases={at: at for at in range(count)},
    )(*values, *after)


DMA = pltpu.SemaphoreType.DMA


class Sizes:
    def __init__(self, tokens, seqs, shards, rows, up_size, width):
        self.tokens, self.seqs, self.shards, self.rows = tokens, seqs, shards, rows
        self.up_size, self.width = up_size, width
        self.depth = shards // 2
        self.slots = tokens // seqs

    def columns(self, count):
        return pltpu.VMEM((count, self.depth, 2, self.rows, WIDE), BF16)

    def by_rows(self):
        return pltpu.VMEM((self.depth, 2, 4, self.rows, WIDE), BF16)

    def unit_grad(self, more=0):
        return [((2, 2, 2, self.depth, self.rows + more, HALF), BF16, ANY)] * 2


def run_attention_forward(z, pos, counts, x, group, params, after=()):
    t = z.tokens
    rows = [((t, WIDE), F32), ((t, WIDE), BF16), ((t, WIDE), F32), ((t, 128), F32)]
    panels = [((PAIRS, t, PAIR), BF16), ((3 * PAIRS, t, PAIR), BF16)]
    probs = ((z.seqs, PAIRS, z.slots, 2 * KEYS), BF16)
    return call(
        functools.partial(attention_forward, z.depth, z.seqs, len(after)),
        [SMEM, SMEM] + [ANY] * 12,
        [(*out, ANY) for out in rows + panels + [probs]],
        [
            pltpu.VMEM((t, WIDE), x.dtype),
            pltpu.VMEM((SMALL, WIDE), F32),
            *[pltpu.VMEM(*out) for out in rows + panels],
            z.columns(4),
            pltpu.VMEM(*probs),
            DMA,
            DMA,
            DMA((4,)),
            DMA,
            DMA,
            DMA((4,)),
            DMA,
        ],
        21,
        after,
    )(pos, counts, x, params, *group)


def run_mlp_forward(z, pos, first, group, params, after=()):
    t = z.tokens
    rows = [((t, WIDE), F32), ((t, WIDE), BF16), ((t, WIDE), F32), ((t, 128), F32)]
    tiles = [((4, t, WIDE), BF16)] * 2
    return call(
        functools.partial(mlp_forward, z.depth, len(after)),
        [SMEM] + [ANY] * 12,
        [(*out, ANY) for out in rows + tiles],
        [
            pltpu.VMEM((SMALL, 4 * WIDE), F32),
            *[pltpu.VMEM(*out) for out in rows],
            z.columns(4),
            z.by_rows(),
            pltpu.VMEM((2, t, WIDE), F32),
            pltpu.VMEM((t, WIDE), BF16),
            *[pltpu.VMEM(*out) for out in tiles],
            DMA,
            DMA,
            DMA((4,)),
            DMA((4,)),
            DMA,
            DMA,
            DMA,
        ],
        20,
        after,
    )(pos, first, params, *group)


def run_down_backward(z, pos, grad, hat, scale, params, act, after=()):
    t = z.tokens
    return call(
        functools.partial(down_backward, z.depth, len(after)),
        [SMEM] + [ANY] * 5,
        [
            ((t, WIDE), F32, ANY),
            ((8, WIDE), F32, ANY),
            *z.unit_grad(),
        ],
        [
            pltpu.VMEM((SMALL, WIDE), F32),
            pltpu.VMEM((8, WIDE), F32),
            pltpu.VMEM((t, WIDE), grad.dtype),
            pltpu.VMEM((t, WIDE), F32),
            pltpu.VMEM((t, 128), F32),
            pltpu.VMEM((t, WIDE), F32),
            pltpu.VMEM((4, t, WIDE), BF16),
            z.by_rows(),
            DMA,
            DMA,
            DMA((4,)),
            DMA((4,)),
            DMA,
            DMA,
        ],
        10,
        after,
    )(pos, params, grad, hat, scale, act)


def run_up_backward(z, pos, second, group, slope, first_low, hat, scale, params, after=()):
    t = z.tokens
    return call(
        functools.partial(up_backward, z.depth, len(after)),
        [SMEM] + [ANY] * 16,
        [
            ((t, WIDE), F32, ANY),
            ((8, WIDE), F32, ANY),
            ((1, 4 * WIDE), F32, ANY),
            *z.unit_grad(),
        ],
        [
            pltpu.VMEM((SMALL, WIDE), F32),
            pltpu.VMEM((8, WIDE), F32),
            pltpu.VMEM((1, 4 * WIDE), F32),
            z.columns(4),
            z.by_rows(),
            pltpu.VMEM((4, t, WIDE), BF16),
            pltpu.VMEM((t, WIDE), F32),
            pltpu.VMEM((t, WIDE), BF16),
            pltpu.VMEM((t, WIDE), F32),
            pltpu.VMEM((t, 128), F32),
            z.columns(4),
            DMA,
            DMA,
            DMA,
            DMA((4,)),
            DMA,
            DMA,
            DMA,
            DMA,
            DMA((4,)),
            DMA,
            DMA,
        ],
        19,
        after,
    )(pos, params, second, slope, first_low, hat, scale, *group)


def run_attention_backward(z, pos, grad, group, qkv, probs, after=()):
    t = z.tokens
    return call(
        functools.partial(attention_backward, z.depth, z.seqs, len(after)),
        [SMEM] + [ANY] * 13,
        [((3 * PAIRS, t, PAIR), BF16, ANY)],
        [
            pltpu.VMEM((z.depth, 2, z.rows, WIDE), BF16),
            pltpu.VMEM((t, WIDE), F32),
            pltpu.VMEM((3 * PAIRS, t, PAIR), BF16),
            pltpu.VMEM((z.seqs, PAIRS, z.slots, 2 * KEYS), BF16),
            pltpu.VMEM((PAIRS, t, PAIR), BF16),
            pltpu.VMEM((3 * PAIRS, t, PAIR), BF16),
            DMA,
            DMA,
            DMA,
            DMA,
            DMA,
        ],
        13,
        after,
    )(pos, grad, qkv, probs, *group)[0]


def run_qkv_weights(z, pos, grad, grads, ctx, x_low, down_sums, up_sums, up_bias, group=(), after=()):
    t = z.tokens
    more = [z.columns(3), DMA((3,)), DMA] if group else []
    return call(
        functools.partial(qkv_weights, z.depth, z.up_size, z.width, bool(group), len(after)),
        [SMEM] + [ANY] * (7 + len(group)),
        z.unit_grad(SMALL) + ([((t, WIDE), F32, ANY)] if group else []),
        [
            pltpu.VMEM((8, WIDE), F32),
            pltpu.VMEM((8, WIDE), F32),
            pltpu.VMEM((1, 4 * WIDE), F32),
            DMA((3,)),
            pltpu.VMEM((t, WIDE), F32),
            pltpu.VMEM((3 * PAIRS, t, PAIR), BF16),
            pltpu.VMEM((PAIRS, t, PAIR), BF16),
            pltpu.VMEM((t, WIDE), BF16),
            z.columns(4),
            pltpu.VMEM((8, WIDE), F32),
            pltpu.VMEM((SMALL, HALF), F32),
            pltpu.VMEM((z.depth, 2, SMALL, HALF), BF16),
            DMA,
            DMA((3,)),
            DMA,
            DMA,
            DMA,
            DMA,
            *more,
        ],
        8,
        after,
    )(pos, down_sums, up_sums, up_bias, grad, grads, ctx, x_low, *group)


def run_qkv_backward(z, pos, grad, grads, group, after=()):
    t = z.tokens
    return call(
        functools.partial(qkv_backward, z.depth, len(after)),
        [SMEM] + [ANY] * 12,
        [((t, WIDE), F32, ANY)],
        [
            pltpu.VMEM((t, WIDE), F32),
            z.columns(3),
            pltpu.VMEM((3 * PAIRS, t, PAIR), BF16),
            DMA((3,)),
            DMA,
            DMA,
            DMA,
        ],
        6,
        after,
    )(pos, grad, grads, *group)[0]


def run_finish_first(z, pos, quarters, after=()):
    r = z.rows
    return call(
        functools.partial(finish_first, len(after)),
        [SMEM] + [VMEM] * (4 * LAYERS),
        [
            ((LAYERS, r, 3 * WIDE), F32, VMEM),
            ((LAYERS, r, WIDE), F32, VMEM),
            ((LAYERS, z.up_size), F32, VMEM),
            ((6, LAYERS, z.width), F32, VMEM),
            ((LAYERS, 2, z.width), F32, VMEM),
        ],
        [],
        3,
        after,
        limit=SMALL_LIMIT,
    )(pos, *quarters)


def run_finish_second(z, pos, quarters, after=()):
    r = z.rows
    return call(
        functools.partial(finish_second, len(after)),
        [SMEM] + [VMEM] * (4 * LAYERS),
        [
            ((LAYERS, r, 4 * WIDE), F32, VMEM),
            ((LAYERS, 4 * r, WIDE), F32, VMEM),
        ],
        [],
        5,
        after,
        limit=SMALL_LIMIT,
    )(pos, *quarters)


def run_prepare(z, pos, *arrays):
    r = z.rows
    return call(
        prepare,
        [SMEM] + [ANY] * 4 + [VMEM] * 3,
        [
            ((2, 1, r + SMALL, HALF), BF16, VMEM),
            ((2, 2, r, HALF), BF16, VMEM),
            ((2, 3, r, HALF), BF16, VMEM),
        ],
        [
            pltpu.VMEM((SMALL, HALF), F32),
            DMA((LAYERS, 3, 2)),
        ],
        1,
        limit=SMALL_LIMIT,
    )(pos, *arrays)


def run_columns_of(pos, pieces):
    depth, shape = len(pieces), pieces[0].shape
    return call(
        functools.partial(columns_of, depth),
        [SMEM] + [VMEM] * depth,
        [((2, depth) + shape[1:], BF16, VMEM)],
        [],
        2,
    )(pos, *pieces)[0]


def run_split_columns(column, sizes):
    depth, _, _, *rest = column.shape
    outs = [((2, depth, size, *rest), BF16, VMEM) for size in sizes]
    return call(functools.partial(split_columns, sizes), [VMEM], outs, [], 2)(column)


def add_specs(sums, size, place):
    specs = []
    for parts in sums:
        for array, lead in parts:
            rest = array.shape[len(lead) + 1 :]
            specs.append(
                pl.BlockSpec(
                    (None,) * len(lead) + (size,) + rest,
                    lambda *at, lead=lead, rest=len(rest): lead + (place(*at),) + (0,) * rest,
                )
            )
    return specs


def run_add_up(jobs):
    specs, arrays, outs, out_specs = [], [], [], []
    for sums, form in jobs:
        array, lead = sums[0][0]
        depth, *rest = array.shape[len(lead) :]
        size, count = depth // 2, len(sums)
        specs += add_specs(sums, size, lambda step: step)
        arrays += [array for parts in sums for array, _ in parts]
        if form == "joined":
            outs.append((count, depth, *rest))
            out_specs.append(pl.BlockSpec((count, size, *rest), lambda step: (0, step, 0, 0)))
        elif form == "beside":
            outs.append((depth, count, *rest))
            out_specs.append(pl.BlockSpec((size, count, *rest), lambda step: (step, 0, 0, 0)))
        else:
            outs += [(depth, *rest)] * count
            out_specs += [
                pl.BlockSpec((size, *rest), lambda step, zeros=(0,) * len(rest): (step,) + zeros)
            ] * count
    results = list(
        pl.pallas_call(
            functools.partial(add_up, [([len(parts) for parts in sums], form) for sums, form in jobs]),
            grid=(2,),
            in_specs=specs,
            out_specs=out_specs,
            out_shape=[jax.ShapeDtypeStruct(out, BF16) for out in outs],
            compiler_params=pltpu.CompilerParams(vmem_limit_bytes=SMALL_LIMIT),
            cost_estimate=pl.CostEstimate(flops=int(3 * COST), bytes_accessed=0, transcendentals=0),
        )(*arrays)
    )
    grouped = []
    for sums, form in jobs:
        count = 1 if form else len(sums)
        grouped.append(results[:count])
        results = results[count:]
    return grouped


def run_add_up_far(pos, sums):
    array, lead = sums[0][0]
    depth, *rest = array.shape[len(lead) :]
    outs = [jax.ShapeDtypeStruct((2, *rest), F32 if at == 0 else BF16) for at in range(depth)]
    return pl.pallas_call(
        functools.partial(add_up_far, depth, len(sums[0])),
        grid_spec=pltpu.PrefetchScalarGridSpec(
            num_scalar_prefetch=1,
            grid=(depth,),
            in_specs=add_specs(sums, 1, lambda step, pos_ref: lax.rem(pos_ref[3] + step, depth)),
            out_specs=[pl.BlockSpec(out.shape, lambda step, pos_ref: (0, 0, 0)) for out in outs],
        ),
        out_shape=outs,
        compiler_params=pltpu.CompilerParams(vmem_limit_bytes=SMALL_LIMIT),
        cost_estimate=pl.CostEstimate(flops=int(3 * COST), bytes_accessed=0, transcendentals=0),
    )(pos, *[array for parts in sums for array, _ in parts])


def run_add_all(arrays):
    return call(add_all, [VMEM] * len(arrays), [(arrays[0].shape, BF16, VMEM)], [], 1, limit=SMALL_LIMIT)(*arrays)[0]


def run_spread(z, pos, near, far, path):
    return call(
        functools.partial(spread, z.depth, z.up_size, z.width, path),
        [SMEM, ANY, ANY],
        [((SMALL, 4 * WIDE), F32, VMEM)],
        [pltpu.VMEM((2, z.depth, SMALL, HALF), BF16), DMA],
        2,
        limit=SMALL_LIMIT,
    )(pos, near, far)[0]


class Links:
    def __init__(self, rep_size, fsdp_size):
        self.rep_size, self.fsdp_size = rep_size, fsdp_size
        self.depth = fsdp_size // 2
        rep_at, fsdp_at = lax.axis_index("rep"), lax.axis_index("fsdp")
        self.core, self.side = rep_at % 2, (rep_at // 2) % 2
        self.row, self.level = fsdp_at % 2, fsdp_at // 2

    def permute(self, value, target):
        pairs = []
        for rep_at in range(self.rep_size):
            for fsdp_at in range(self.fsdp_size):
                to_rep, to_fsdp = target(rep_at, fsdp_at)
                pairs.append((rep_at * self.fsdp_size + fsdp_at, to_rep * self.fsdp_size + to_fsdp))
        return lax.ppermute(value, AXES, pairs)

    def other_core(self, value):
        return self.permute(value, lambda r, f: (r ^ 1, f))

    def other_side(self, value):
        return self.permute(value, lambda r, f: (r ^ 2, f))

    def other_row(self, value):
        return self.permute(value, lambda r, f: (r, f ^ 1))

    def level_up(self, value, step):
        return self.permute(value, lambda r, f: (r, ((f // 2 + step) % self.depth) * 2 + f % 2))

    def levels(self):
        return [list(range(row, self.fsdp_size, 2)) for row in range(2)]


class Gather:
    def __init__(self, name, links, columns):
        self.name, self.links, self.live, self.moving = name, links, [columns], []

    def scope(self, stage):
        return jax.named_scope("gather_" + self.name + "_" + stage)

    def first(self):
        with self.scope("first"):
            self.moving = [self.links.other_row(self.live[0]), self.links.other_side(self.live[0])]

    def second(self):
        self.live += self.moving
        with self.scope("second"):
            rows, sides = self.live[1:3]
            self.moving = [self.links.other_side(rows[0]), self.links.other_row(sides[1])]
        with self.scope("cores"):
            self.moving += [self.links.other_core(part) for part in self.live[:3]]

    def last(self):
        self.live += self.moving[:2]
        self.far = self.moving[2:]
        with self.scope("last"):
            self.moving = [self.links.other_core(part) for part in self.live[3:5]]

    def arrays(self):
        return self.live + self.far + self.moving


class Sum:
    def __init__(self, name, links, near, far):
        self.name, self.links, self.near, self.sends = name, links, near, [far]
        self.hops = ((links.other_row, links.other_side), (links.other_side, links.other_row))

    def scope(self, stage):
        return jax.named_scope("sum_" + self.name + "_" + stage)

    def cores(self):
        with self.scope("cores"):
            self.moving = [self.links.other_core(self.sends[0])]

    def at(self, far):
        return [[(array, lead + (far,)) for array, lead in parts] for parts in self.parts]

    def came(self):
        self.parts = [[(self.near, (path,)), (self.moving[0], (path,))] for path in range(2)]
        return [(self.at(1), None)]

    def first(self):
        with self.scope("first"):
            self.moving = [self.hops[path][0](self.sends[path]) for path in range(2)]


class Second:
    def __init__(self, name, links, sums):
        self.name, self.links, self.sums = name, links, sums

    def came(self):
        for one in self.sums:
            one.parts = [parts + [(move, ())] for parts, move in zip(one.at(0), one.moving)]
        return [([one.at(1)[path] for one in self.sums], "joined") for path in range(2)]

    def second(self):
        with jax.named_scope("sum_" + self.name + "_second"):
            self.moving = [hops[1](send) for hops, send in zip(self.sums[0].hops, self.sends)]


def add(*steps):
    jobs = [step.came() for step in steps]
    with jax.named_scope("add_" + "_".join(step.name for step in steps)):
        outs = run_add_up([job for step_jobs in jobs for job in step_jobs])
    for step, step_jobs in zip(steps, jobs):
        step.sends = [out for group in outs[: len(step_jobs)] for out in group]
        outs = outs[len(step_jobs) :]


class Share:
    def __init__(self, name, links, second):
        self.name, self.links, self.second = name, links, second

    def scope(self):
        return jax.named_scope("share_" + self.name)

    def parts(self):
        return [
            one.at(0)[path] + [(self.second.moving[path], (unit,))]
            for unit, one in enumerate(self.second.sums)
            for path in range(2)
        ]

    def came(self):
        return [(self.parts(), "beside")]

    def scatter(self):
        with self.scope():
            self.sends = [
                lax.psum_scatter(
                    self.sends[0], "fsdp", scatter_dimension=0, axis_index_groups=self.links.levels()
                )
            ]

    def add_far(self, pos):
        with self.scope():
            self.kept, *self.sends = run_add_up_far(pos, self.parts())

    def levels(self):
        with self.scope():
            self.moving = [self.links.level_up(send, at + 1) for at, send in enumerate(self.sends)]

    def after_levels(self):
        with self.scope():
            self.sends = [run_add_all([self.kept] + self.moving)]

    def copies(self):
        if self.links.rep_size > 4:
            groups = [list(range(first, self.links.rep_size, 4)) for first in range(4)]
            self.sends = [lax.psum(self.sends[0], "rep", axis_index_groups=groups)]

    def sides(self):
        with self.scope():
            self.sends += [self.links.other_side(self.sends[0])]

    def last(self):
        with self.scope():
            self.moving = [self.links.other_core(send) for send in self.sends]

    def quarters(self):
        return self.sends + self.moving


def order(steps, after=()):
    names = ("live", "moving", "sends")
    held = [(step, name) for step in steps for name in (names[:2] if hasattr(step, "live") else names[2:])]
    values = [value for step, name in held for value in getattr(step, name)]
    values = list(tie(values, list(after)))
    token = min(values, key=lambda value: value.size)
    for step, name in held:
        size = len(getattr(step, name))
        setattr(step, name, values[:size])
        values = values[size:]
    return [token]


def shards(
    rep_size, fsdp_size, hidden, region_counts, w_qkv, w_out, w_up, w_down, bias_up, biases, norm_gains, cotangent
):
    links = Links(rep_size, fsdp_size)
    z = Sizes(
        hidden.shape[0], region_counts.shape[0], fsdp_size, w_qkv.shape[1], bias_up.shape[1], biases.shape[2]
    )
    pos = jnp.stack([links.core, links.side, links.row, links.level]).astype(jnp.int32)
    quarters = run_prepare(
        z, pos, w_qkv, w_out, w_up, w_down, bias_up, jnp.transpose(biases, (1, 0, 2)), norm_gains
    )
    kept, groups, params = [], [None] * 4, [None] * 2

    def run_first(layer, states, after):
        return run_attention_forward(z, pos, region_counts, states, groups[2 * layer], params[layer], after)

    def run_second(layer, first, after):
        return run_mlp_forward(z, pos, first, groups[2 * layer + 1], params[layer], after)

    def columns(name, quarter, after=()):
        with jax.named_scope("columns_" + name):
            if after:
                quarter = tie([quarter], list(after))[0]
            pieces = [quarter] + [links.level_up(quarter, step) for step in range(1, links.depth)]
            return run_columns_of(pos, pieces)

    first_0 = Gather("first0", links, columns("first0", quarters[0]))
    first_0.first()
    second_0 = Gather("second0", links, columns("second0", quarters[1], first_0.live))

    order([first_0])
    first_0.second()

    second_0.first()
    order([first_0])
    first_0.last()
    with jax.named_scope("columns_third"):
        third = tie([quarters[2]], first_0.live[1:3])[0]
        third = lax.all_gather(third, "fsdp", axis_index_groups=links.levels())
    params = [run_spread(z, pos, *first_0.live[:2], layer) for layer in range(LAYERS)]
    groups[0] = first_0.arrays()
    one = run_first(0, hidden, params[1:])

    order([second_0], one[3:4])
    second_0.second()
    with jax.named_scope("columns_third"):
        third = run_split_columns(third, (1, 2))
    first_1, second_1 = (Gather(name, links, part) for name, part in zip(("first1", "second1"), third))

    first_1.first()

    order([second_0, second_1])
    second_0.last()
    second_1.first()
    groups[1] = second_0.arrays()
    two = run_second(0, one[0], ())
    kept.append((hidden, one, two))

    order([first_1], two[3:4])
    first_1.second()

    order([first_1, second_1])
    first_1.last()
    second_1.second()
    groups[2] = first_1.arrays()
    one = run_first(1, two[0], ())

    order([second_1], one[3:4])
    second_1.last()
    groups[3] = second_1.arrays()
    low_states = two[1]
    two = run_second(1, one[0], ())
    kept.append((low_states, one, two))
    output = two[1]

    def run_down(layer, gradient, after):
        _, _, hat, scale, act, _ = kept[layer][2]
        return run_down_backward(z, pos, gradient, hat, scale, params[layer], act, after)

    def run_up(layer, second, after):
        _, first_low, hat, scale, *_ = kept[layer][1]
        return run_up_backward(
            z, pos, second, groups[2 * layer + 1], kept[layer][2][5], first_low, hat, scale, params[layer], after
        )

    def run_attention(layer, first_in, after):
        qkv, probs = kept[layer][1][5:7]
        return run_attention_backward(z, pos, first_in, groups[2 * layer], qkv, probs, after)

    def run_weights(layer, first_in, grads, small, group, after):
        return run_qkv_weights(z, pos, first_in, grads, kept[layer][1][4], kept[layer][0], *small, group, after)

    def run_states(layer, first_in, grads, after):
        return run_qkv_backward(z, pos, first_in, grads, groups[2 * layer], after)

    second, down_sums, near, far = run_down(1, cotangent, ())
    down_1 = Sum("down1", links, near, far)

    token = order([down_1])
    down_1.cores()
    first_in, up_sums, up_bias, near, far = run_up(1, second, token)
    up_1 = Sum("up1", links, near, far)

    add(down_1)
    token = order([down_1, up_1])
    down_1.first()
    up_1.cores()
    grads = run_attention(1, first_in, token)

    add(up_1)
    token = order([up_1], [grads] + down_1.moving)
    up_1.first()
    near, far, gradient = run_weights(1, first_in, grads, (down_sums, up_sums, up_bias), groups[2], token)
    first_1 = Sum("first1", links, near, far)

    second_1 = Second("second1", links, [up_1, down_1])
    add(second_1)
    token = order([second_1, first_1], [gradient])
    second_1.second()
    first_1.cores()
    second, down_sums, near, far = run_down(0, gradient, token)
    down_0 = Sum("down0", links, near, far)

    share_second_1 = Share("second1", links, second_1)
    order([down_0], second_1.moving + first_1.moving)
    down_0.cores()
    add(first_1, share_second_1)
    order([first_1, share_second_1])
    first_1.first()
    share_second_1.scatter()
    add(down_0)
    token = order([down_0])
    down_0.first()
    first_in, up_sums, up_bias, near, far = run_up(0, second, token)
    up_0 = Sum("up0", links, near, far)

    first_second_1 = Second("first1", links, [first_1])
    order([up_0], first_1.moving + down_0.moving)
    up_0.cores()
    add(first_second_1)
    order([first_second_1])
    first_second_1.second()
    add(up_0)
    token = order([up_0])
    up_0.first()
    grads = run_attention(0, first_in, token)

    second_0 = Second("second0", links, [up_0, down_0])
    share_first_1 = Share("first1", links, first_second_1)
    add(second_0, share_first_1)
    token = order([second_0, share_first_1], [grads])
    second_0.second()
    share_first_1.scatter()
    near, far = run_weights(0, first_in, grads, (down_sums, up_sums, up_bias), (), token)
    first_0 = Sum("first0", links, near, far)

    share_second_0 = Share("second0", links, second_0)
    order([first_0], second_0.moving)
    first_0.cores()
    add(share_second_0)
    share_second_1.copies()
    order([share_second_0, share_second_1])
    share_second_0.scatter()
    add(first_0)
    token = order([first_0, share_second_1])
    first_0.first()
    share_second_1.sides()
    gradient = run_states(0, first_in, grads, token)

    order([share_second_1], first_0.moving + [gradient])
    share_second_1.last()
    first_second_0 = Second("first0", links, [first_0])
    add(first_second_0)
    share_first_1.copies()
    order([first_second_0, share_first_1], share_second_1.moving)
    first_second_0.second()
    share_first_1.sides()

    share_first_0 = Share("first0", links, first_second_0)
    share_first_0.add_far(pos)
    share_second_0.copies()
    order([share_first_0, share_second_0, share_first_1])
    share_first_0.levels()
    share_second_0.sides()
    share_first_1.last()

    share_first_0.after_levels()
    share_first_0.copies()
    order([share_first_0, share_second_0], share_first_1.moving)
    share_first_0.sides()
    share_second_0.last()
    up_grad, down_grad = run_finish_second(z, pos, share_second_0.quarters() + share_second_1.quarters())

    order([share_first_0], [up_grad])
    share_first_0.last()
    qkv_grad, out_grad, up_bias_grad, biases_grad, gains_grad = run_finish_first(
        z, pos, share_first_0.quarters() + share_first_1.quarters()
    )
    biases_grad = jnp.transpose(biases_grad, (1, 0, 2))
    return output, gradient, qkv_grad, out_grad, up_grad, down_grad, up_bias_grad, biases_grad, gains_grad


def solution(mesh):
    in_specs = (
        P(("rep", "fsdp"), None),
        P(("rep", "fsdp")),
        P(None, "fsdp", None),
        P(None, "fsdp", None),
        P(None, "fsdp", None),
        P(None, "fsdp", None),
        P(None, "fsdp"),
        P(None, None, "fsdp"),
        P(None, None, "fsdp"),
        P(("rep", "fsdp"), None),
    )
    out_specs = (
        P(("rep", "fsdp"), None),
        P(("rep", "fsdp"), None),
        P(None, "fsdp", None),
        P(None, "fsdp", None),
        P(None, "fsdp", None),
        P(None, "fsdp", None),
        P(None, "fsdp"),
        P(None, None, "fsdp"),
        P(None, None, "fsdp"),
    )
    local = functools.partial(shards, mesh.shape["rep"], mesh.shape["fsdp"])
    return jax.shard_map(local, mesh=mesh, in_specs=in_specs, out_specs=out_specs, check_vma=False)
```

```python
import functools

import jax
import jax.numpy as jnp
from jax import lax
from jax.experimental import pallas as pl
from jax.experimental.pallas import tpu as pltpu
from jax.sharding import PartitionSpec as P

HEADS = 12
HEAD_DIM = 64
LAYERS = 2
TEXT = 128
KEYS = 256
WIDE = 768
HALF = WIDE // 2
PAIR = 2 * HEAD_DIM
PAIRS = HEADS // 2
EPSILON = 1e-12
MASKED = -1000000000.0
AXES = ("rep", "fsdp")
COST = 1.15e9
SMALL = 16
VMEM_LIMIT = 64 * 1024 * 1024
SMALL_LIMIT = VMEM_LIMIT


def low(value):
    return value.astype(jnp.bfloat16)


def full(value):
    return value.astype(jnp.float32)


def mm(left, right):
    return jnp.dot(left, right, preferred_element_type=jnp.float32)


def mm_t(left, right):
    return lax.dot_general(
        left, right, (((1,), (1,)), ((), ())), preferred_element_type=jnp.float32
    )


def t_mm(left, right):
    return lax.dot_general(
        left, right, (((0,), (0,)), ((), ())), preferred_element_type=jnp.float32
    )


def flip(at, by):
    return 1 - at if by else at


class Place:
    def __init__(self, pos_ref):
        self.core, self.side = pos_ref[0], pos_ref[1]
        self.row, self.level = pos_ref[2], pos_ref[3]

    def shard(self, level, far_row):
        return level * 2 + flip(self.row, far_row)


def half_lanes(at):
    return pl.ds(pl.multiple_of(at * HALF, HALF), HALF)


def part_of(arrays, path, far_core, far_side, far_row):
    arrays = arrays[5 * far_core : 5 * far_core + 5]
    if far_side and far_row:
        return arrays[3 + path]
    return arrays[2 * far_side + far_row].at[path]


def load_unit(place, arrays, unit, whole, sems, by_rows):
    rows = pl.ds(0, whole.shape[3])
    for far_side in range(2):
        for path in range(2):
            block = flip(place.side, far_side) * 2 + path
            for far_core in range(2):
                lanes = half_lanes(flip(place.core, far_core))
                for far_row in range(2):
                    row = flip(place.row, far_row)
                    part = part_of(arrays, path, far_core, far_side, far_row).at[:, unit, rows]
                    if by_rows:
                        copy(part, whole.at[:, row, block, :, lanes], sems)
                    else:
                        copy(part, whole.at[block, :, row, :, lanes], sems.at[block])


def load_block(place, block, arrays, whole, sem):
    path = block % 2
    rows = pl.ds(0, whole.shape[2])
    needed_side = place.side if block // 2 == 0 else 1 - place.side
    for far_side in range(2):

        @pl.when(needed_side == far_side)
        def _():
            for far_core in range(2):
                lanes = half_lanes(flip(place.core, far_core))
                for far_row in range(2):
                    part = part_of(arrays, path, far_core, far_side, far_row).at[:, 0, rows]
                    copy(part, whole.at[:, flip(place.row, far_row), :, lanes], sem)


def copy(source, target, sem):
    pltpu.make_async_copy(source, target, sem).start()


def wait_all(ref, sem):
    pltpu.make_async_copy(ref, ref, sem).wait()


def either(choice, one, other):
    return other + choice * (one - other)


def either(choice, one, other):
    return other + choice * (one - other)


def sum_place(out, block, far_row, far_side):
    path = block % 2
    return out.at[path, either(path, far_side, far_row), either(path, far_row, far_side)]


def side_distance(place, block):
    return either(place.side, 1 - block // 2, block // 2)


def store_columns(place, block, held, outs, sem):
    rows = pl.ds(0, held.shape[2])
    far_side = side_distance(place, block)
    for far_core, out in enumerate(outs):
        lanes = half_lanes(flip(place.core, far_core))
        for far_row in range(2):
            source = held.at[:, flip(place.row, far_row), :, lanes]
            copy(source, sum_place(out, block, far_row, far_side).at[:, rows], sem)


def store_rows(place, levels, held, outs, sem):
    for far_core, out in enumerate(outs):
        lanes = half_lanes(flip(place.core, far_core))
        for block in range(4):
            far_side = side_distance(place, block)
            for far_row in range(2):
                source = held.at[levels, flip(place.row, far_row), block, :, lanes]
                copy(source, sum_place(out, block, far_row, far_side).at[levels], sem)


def chunks(rows):
    edges = [rows // 16 * at // 4 * 16 for at in range(4)] + [rows]
    return [(start, end - start) for start, end in zip(edges, edges[1:])]


def normalize(value):
    centered = value - jnp.mean(value, axis=-1, keepdims=True)
    scale = lax.rsqrt(jnp.mean(centered * centered, axis=-1, keepdims=True) + EPSILON)
    return centered * scale, scale


def norm_backward(grad, hat, scale, gain):
    direct = grad * gain
    return (
        direct
        - jnp.mean(direct, axis=-1, keepdims=True)
        - hat * jnp.mean(direct * hat, axis=-1, keepdims=True)
    ) * scale


def gelu_and_slope(value):
    size = jnp.abs(value) * 0.7071067811865476
    t = 1.0 / (1.0 + 0.3275911 * size)
    series = t * (
        0.127414796
        + t * (-0.142248368 + t * (0.7107068705 + t * (-0.7265760135 + t * 0.5307027145)))
    )
    bell = jnp.exp(-0.5 * value * value)
    tail = series * bell
    below = jnp.where(value >= 0, 1.0 - tail, tail)
    return value * below, below + value * bell * 0.3989422804014327


def head_masks(value, lane):
    none = jnp.zeros_like(value)
    return jnp.concatenate(
        [jnp.where(lane < HEAD_DIM, value, none), jnp.where(lane < HEAD_DIM, none, value)], 0
    )


def side_by_side(ref, block):
    return jnp.concatenate([ref[block * PAIRS + pair] for pair in range(PAIRS)], 1)


def attention_forward(depth, seqs, extra, pos_ref, counts_ref, x_ref, params_ref, *refs):
    parts, refs = refs[:10], refs[10 + extra :]
    first_out, first_low_out, hat_out, scale_out, ctx_out, qkv_out, probs_ref = refs[:7]
    x, params, first, first_low, hat, scale, ctx, qkv, weight, held, *sems = refs[7:]
    x_sem, params_sem, row_sem, ctx_sem, qkv_sem, weight_sem, held_sem = sems
    place = Place(pos_ref)
    copy(x_ref, x, x_sem)
    load_unit(place, parts, 0, weight, weight_sem, False)
    copy(params_ref.at[:, pl.ds(0, WIDE)], params, params_sem)
    tokens = x.shape[0]
    slots = tokens // seqs
    wait_all(x, x_sem)
    x_low = low(x[...])
    wait_all(params, params_sem)

    for block in range(3):
        wait_all(weight.at[block], weight_sem.at[block])

    def project(block, carry):
        out = mm(x_low, weight[block].reshape(WIDE, WIDE))
        bias = params[pl.ds(1 + block // 2, 1), :]
        out = low(out + jnp.where(block == 1, jnp.zeros_like(bias), bias))
        for pair in range(PAIRS):
            qkv[block * PAIRS + pair] = out[:, pair * PAIR : (pair + 1) * PAIR]
        return carry

    lax.fori_loop(0, 3, project, 0)
    copy(qkv, qkv_out, qkv_sem)
    lane = lax.broadcasted_iota(jnp.int32, (KEYS, PAIR), 1)
    key = lax.broadcasted_iota(jnp.int32, (slots, KEYS), 1)

    def pair_step(step, carry):
        seq, pair = step // PAIRS, lax.rem(step, PAIRS)
        rows = pl.ds(pl.multiple_of(seq * slots, 16), slots)
        key_rows = pl.ds(pl.multiple_of(seq * slots, 16), KEYS)
        valid = key < TEXT + counts_ref[seq]
        q = qkv[pair, rows, :] * jnp.bfloat16(HEAD_DIM**-0.5)
        scores = mm_t(q, head_masks(qkv[PAIRS + pair, key_rows, :], lane))
        halves = []
        for half in range(2):
            part = jnp.where(valid, scores[:, half * KEYS : (half + 1) * KEYS], MASKED)
            part = jnp.exp(part - jnp.max(part, axis=-1, keepdims=True))
            halves.append(low(part * (1.0 / jnp.sum(part, axis=-1, keepdims=True))))
        probs = jnp.concatenate(halves, 1)
        held[seq, pair] = probs
        copy(held.at[seq, pair], probs_ref.at[seq, pair], held_sem)
        ctx[pair, rows, :] = low(mm(probs, head_masks(qkv[2 * PAIRS + pair, key_rows, :], lane)))
        return carry

    lax.fori_loop(0, seqs * PAIRS, pair_step, 0, unroll=2)
    copy(ctx, ctx_out, ctx_sem)
    wait_all(weight.at[3], weight_sem.at[3])
    first[...] = mm(side_by_side(ctx, 0), weight[3].reshape(WIDE, WIDE))
    outs = ((first, first_out), (first_low, first_low_out), (hat, hat_out), (scale, scale_out))
    for start, size in chunks(tokens):
        rows = pl.ds(start, size)
        normal, factor = normalize(full(x[rows, :]) + (first[rows, :] + params[3:4, :]))
        hat[rows, :] = normal
        scale[rows, :] = jnp.broadcast_to(factor, (size, 128))
        value = normal * params[7:8, :] + params[4:5, :]
        first[rows, :] = value
        first_low[rows, :] = low(value)
        for at, (source, target) in enumerate(outs):
            copy(source.at[rows], target.at[rows], row_sem.at[at])
    for at, (source, _) in enumerate(outs):
        wait_all(source, row_sem.at[at])
    wait_all(ctx, ctx_sem)
    wait_all(qkv, qkv_sem)
    wait_all(held, held_sem)


def mlp_forward(depth, extra, pos_ref, first_ref, params_ref, *refs):
    parts, refs = refs[:10], refs[10 + extra :]
    out_out, out_low_out, hat_out, scale_out, act_ref, slope_ref = refs[:6]
    params, out, out_low, hat, scale, up, down, pre, first_low, act, slope, *sems = refs[6:]
    params_sem, first_sem, row_sem, up_sem, down_sem, act_sem, slope_sem = sems
    place = Place(pos_ref)
    copy(first_ref, out, first_sem)
    load_unit(place, parts, 0, up, up_sem, False)
    copy(params_ref, params, params_sem)
    load_unit(place, parts, 1, down, down_sem, True)
    tokens = out.shape[0]
    half = tokens // 2
    levels = depth // 4
    wait_all(out, first_sem)
    first_low[...] = low(out[...])
    act[3, half:, :] = jnp.zeros((half, WIDE), BF16)
    for tile in range(4):
        wait_all(up.at[tile], up_sem.at[tile])
    pre[0] = mm(first_low[...], up[0].reshape(WIDE, WIDE))
    wait_all(params, params_sem)
    out[...] += params[5:6, :WIDE]
    wait_all(down, down_sem)

    def half_rows(step):
        return pl.ds(pl.multiple_of(lax.rem(step, 2) * half, 16), half)

    def below(step):
        tile, rows = step // 2, half_rows(step)
        weight = down[pl.ds(tile * levels, levels)].reshape(WIDE, WIDE)
        out[rows, :] += mm(act[tile, rows, :], weight)

    def half_step(step, carry):
        tile, rows = step // 2, half_rows(step)
        slot, later = lax.rem(tile, 2), lax.rem(tile + 1, 4)
        bias = params[0:1, pl.ds(pl.multiple_of(tile * WIDE, WIDE), WIDE)]
        below(lax.rem(step + 7, 8))
        pre[1 - slot, rows, :] = mm(first_low[rows, :], up[later].reshape(WIDE, WIDE))
        gelu, rise = gelu_and_slope(pre[slot, rows, :] + bias)
        act[tile, rows, :] = low(gelu)
        slope[tile, rows, :] = low(rise)
        copy(slope.at[tile, rows], slope_ref.at[tile, rows], slope_sem)
        copy(act.at[tile, rows], act_ref.at[tile, rows], act_sem)
        return carry

    lax.fori_loop(0, 8, half_step, 0)
    below(7)
    outs = ((out, out_out), (out_low, out_low_out), (hat, hat_out), (scale, scale_out))
    for start, size in chunks(tokens):
        rows = pl.ds(start, size)
        normal, factor = normalize(out[rows, :])
        hat[rows, :] = normal
        scale[rows, :] = jnp.broadcast_to(factor, (size, 128))
        value = normal * params[8:9, :WIDE] + params[6:7, :WIDE]
        out[rows, :] = value
        out_low[rows, :] = low(value)
        for at, (source, target) in enumerate(outs):
            copy(source.at[rows], target.at[rows], row_sem.at[at])
    for at, (source, _) in enumerate(outs):
        wait_all(source, row_sem.at[at])
    wait_all(slope, slope_sem)
    wait_all(act, act_sem)


def load_rows(pairs, sem):
    for at, (start, size) in enumerate(chunks(pairs[0][0].shape[0])):
        for source, target in pairs:
            rows = pl.ds(start, size)
            copy(source.at[rows], target.at[rows], sem.at[at])


def norm_step(grad, hat, scale, gain, out, out_ref, sums, sums_ref, waits, sem, out_sem, sums_sem):
    totals = [0.0, 0.0, 0.0]
    for at, (start, size) in enumerate(chunks(grad.shape[0])):
        rows = pl.ds(start, size)
        for array in waits:
            wait_all(array.at[rows], sem.at[at])
        value, hat_rows = full(grad[rows, :]), hat[rows, :]
        grad_in = norm_backward(value, hat_rows, scale[rows, :][:, :1], gain)
        out[rows, :] = grad_in
        copy(out.at[rows], out_ref.at[rows], out_sem)
        for number, part in enumerate((value * hat_rows, value, full(low(grad_in)))):
            totals[number] += jnp.sum(part, axis=0, keepdims=True)
    sums[...] = jnp.zeros_like(sums)
    for number in range(3):
        sums[number : number + 1, :] = totals[number]
    copy(sums, sums_ref, sums_sem)


def down_backward(depth, extra, pos_ref, params_ref, grad_ref, hat_ref, scale_ref, act_ref, *refs):
    second_ref, sums_ref, near_ref, far_ref = refs[extra : extra + 4]
    params, sums, grad, hat, scale, second, act, held, *sems = refs[extra + 4 :]
    params_sem, sums_sem, row_sem, act_sem, out_sem, held_sem = sems
    place = Place(pos_ref)
    copy(params_ref.at[:, pl.ds(0, WIDE)], params, params_sem)
    load_rows([(grad_ref, grad), (hat_ref, hat), (scale_ref, scale)], row_sem)
    for tile in range(4):
        copy(act_ref.at[tile], act.at[tile], act_sem.at[tile])
    wait_all(params, params_sem)
    norm_step(
        grad, hat, scale, params[8:9, :], second, second_ref, sums, sums_ref, (grad, hat, scale), row_sem, out_sem, sums_sem
    )
    grad_low = low(second[...])
    for tile in range(4):
        wait_all(act.at[tile], act_sem.at[tile])

    levels = depth // 4

    def tile_step(tile, carry):
        held[pl.ds(tile * levels, levels)] = low(t_mm(act[tile], grad_low)).reshape((levels,) + held.shape[1:])
        return carry

    for start in (0, 2):
        lax.fori_loop(start, start + 2, tile_step, 0)
        store_rows(place, pl.ds(start * levels, 2 * levels), held, (near_ref, far_ref), held_sem)
    wait_all(second, out_sem)
    wait_all(sums, sums_sem)
    wait_all(held, held_sem)


def up_backward(
    depth, extra, pos_ref, params_ref, second_ref, slope_ref, first_low_ref, hat_ref, scale_ref, *refs
):
    parts, refs = refs[:10], refs[10 + extra :]
    first_in_ref, sums_ref, up_grad_ref, near_ref, far_ref = refs[:5]
    params, sums, up_grad, up, down, slope, total, first_low, hat, scale, held, *sems = refs[5:]
    params_sem, sums_sem, up_grad_sem, up_sem, down_sem, slope_sem, second_sem, first_sem, row_sem, out_sem, held_sem = sems
    place = Place(pos_ref)
    copy(second_ref, total, second_sem)
    load_unit(place, parts, 1, down, down_sem, True)
    copy(slope_ref, slope, slope_sem)
    levels = depth // 4
    wait_all(total, second_sem)
    grad_low = low(total[...])
    wait_all(down, down_sem)
    wait_all(slope, slope_sem)
    load_unit(place, parts, 0, up, up_sem, False)
    copy(first_low_ref, first_low, first_sem)
    load_rows([(hat_ref, hat), (scale_ref, scale)], row_sem)
    copy(params_ref.at[:, pl.ds(0, WIDE)], params, params_sem)

    def pre_step(tile, carry):
        weight = down[pl.ds(tile * levels, levels)].reshape(WIDE, WIDE)
        grad = low(mm_t(grad_low, weight) * full(slope[tile]))
        slope[tile] = grad
        up_grad[:, pl.ds(pl.multiple_of(tile * WIDE, WIDE), WIDE)] = jnp.sum(
            full(grad), axis=0, keepdims=True
        )
        return carry

    lax.fori_loop(0, 4, pre_step, 0)
    copy(up_grad, up_grad_ref, up_grad_sem)
    wait_all(first_low, first_sem)
    for tile in range(4):
        wait_all(up.at[tile], up_sem.at[tile])

    def tile_step(tile, carry):
        held[tile] = low(t_mm(first_low[...], slope[tile])).reshape(held.shape[1:])
        total[...] += mm_t(slope[tile], up[tile].reshape(WIDE, WIDE))
        store_columns(place, tile, held.at[tile], (near_ref, far_ref), held_sem)
        return carry

    lax.fori_loop(0, 4, tile_step, 0)
    wait_all(params, params_sem)
    norm_step(
        total, hat, scale, params[7:8, :], total, first_in_ref, sums, sums_ref, (hat, scale), row_sem, out_sem, sums_sem
    )
    wait_all(total, out_sem)
    wait_all(sums, sums_sem)
    wait_all(up_grad, up_grad_sem)
    wait_all(held, held_sem)


def attention_backward(depth, seqs, extra, pos_ref, grad_ref, qkv_ref, probs_ref, *refs):
    parts, refs = refs[:10], refs[10 + extra :]
    grads_ref = refs[0]
    weight, grad, qkv, probs, ctx_grad, grads, weight_sem, grad_sem, qkv_sem, probs_sem, out_sem = refs[1:]
    place = Place(pos_ref)
    copy(grad_ref, grad, grad_sem)
    load_block(place, 3, parts, weight, weight_sem)
    copy(qkv_ref, qkv, qkv_sem)
    copy(probs_ref, probs, probs_sem)
    tokens = grad.shape[0]
    slots = tokens // seqs
    wait_all(grad, grad_sem)
    wait_all(weight, weight_sem)
    from_out = low(mm_t(low(grad[...]), weight[...].reshape(WIDE, WIDE)))
    for pair in range(PAIRS):
        ctx_grad[pair] = from_out[:, pair * PAIR : (pair + 1) * PAIR]
    wait_all(qkv, qkv_sem)
    wait_all(probs, probs_sem)
    lane = lax.broadcasted_iota(jnp.int32, (KEYS, PAIR), 1)

    def pair_step(step, carry):
        seq, pair = step // PAIRS, lax.rem(step, PAIRS)
        start = pl.multiple_of(seq * slots, 16)
        rows, key_rows = pl.ds(start, slots), pl.ds(start, KEYS)
        q = qkv[pair, rows, :]
        out_grad = ctx_grad[pair, rows, :]
        weights = probs[seq, pair]
        probs_grad = mm_t(out_grad, head_masks(qkv[2 * PAIRS + pair, key_rows, :], lane))
        halves = []
        for half in range(2):
            lanes = slice(half * KEYS, (half + 1) * KEYS)
            weight_part, grad_part = full(weights[:, lanes]), probs_grad[:, lanes]
            dot = jnp.sum(weight_part * grad_part, axis=-1, keepdims=True)
            halves.append(low(weight_part * (grad_part - dot)))
        scores_grad = jnp.concatenate(halves, 1)
        q_grad = mm(scores_grad, head_masks(qkv[PAIRS + pair, key_rows, :], lane)) * HEAD_DIM**-0.5
        grads[pair, rows, :] = low(q_grad)
        k_grad = t_mm(q, scores_grad) * HEAD_DIM**-0.5
        v_grad = t_mm(out_grad, weights)
        for at, value in ((PAIRS, k_grad), (2 * PAIRS, v_grad)):
            value = jnp.concatenate([value[:HEAD_DIM, :KEYS], value[HEAD_DIM:, KEYS:]], 0)
            grads[at + pair, key_rows, :] = low(value.T)
            grads[at + pair, pl.ds(pl.multiple_of(start + KEYS, 16), slots - KEYS), :] = jnp.zeros(
                (slots - KEYS, PAIR), BF16
            )
        for at in range(3):
            copy(grads.at[at * PAIRS + pair, rows], grads_ref.at[at * PAIRS + pair, rows], out_sem)
        return carry

    lax.fori_loop(0, seqs * PAIRS, pair_step, 0, unroll=2)
    wait_all(grads, out_sem)


def qkv_weights(
    depth, up_size, width, with_states, extra, pos_ref, down_sums_ref, up_sums_ref, up_bias_ref, grad_ref, grads_ref, ctx_ref, x_ref,
    *refs,
):
    parts, refs = refs[: 10 * with_states], refs[10 * with_states + extra :]
    outs, refs = refs[:2], refs[2:]
    if with_states:
        x_grad_ref, *refs = refs
        *refs, weight, weight_sem, out_sem = refs
    down_sums, up_sums, up_bias, bias_sem, *refs = refs
    grad, grads, ctx, x_low, held, sums, block_rows, small, grad_sem, grads_sem, ctx_sem, x_sem, held_sem, small_sem = refs
    place = Place(pos_ref)
    copy(x_ref, x_low, x_sem)
    for block in range(3):
        panels = pl.ds(block * PAIRS, PAIRS)
        copy(grads_ref.at[panels], grads.at[panels], grads_sem.at[block])
    copy(ctx_ref, ctx, ctx_sem)
    copy(grad_ref, grad, grad_sem)
    if with_states:
        for block in range(3):
            load_block(place, block, parts, weight.at[block], weight_sem.at[block])
    biases = ((down_sums_ref, down_sums), (up_sums_ref, up_sums), (up_bias_ref, up_bias))
    for at, (source, target) in enumerate(biases):
        copy(source, target, bias_sem.at[at])
    wait_all(x_low, x_sem)
    for block in range(3):
        wait_all(grads.at[pl.ds(block * PAIRS, PAIRS)], grads_sem.at[block])

    def block_step(block, carry):
        part = side_by_side(grads, block)
        sums[pl.ds(block, 1), :] = jnp.sum(full(part), axis=0, keepdims=True)
        held[block] = low(t_mm(x_low[...], part)).reshape(held.shape[1:])
        store_columns(place, block, held.at[block], outs, held_sem)
        return carry

    lax.fori_loop(0, 3, block_step, 0)
    sums[1:2, :] = sums[2:3, :]
    for at, (_, target) in enumerate(biases):
        wait_all(target, bias_sem.at[at])
    block_rows[...] = jnp.zeros_like(block_rows)
    for shard in range(2 * depth):
        lanes = slice(shard * width, (shard + 1) * width)
        block_rows[0:1, :up_size] = up_bias[:, shard * up_size : (shard + 1) * up_size]
        block_rows[1:3, :width] = sums[0:2, lanes]
        for row, (ref, at) in enumerate(
            ((up_sums, 2), (up_sums, 1), (down_sums, 2), (down_sums, 1), (up_sums, 0), (down_sums, 0))
        ):
            block_rows[3 + row : 4 + row, :width] = ref[at : at + 1, lanes]
        small[shard // 2, shard % 2] = low(block_rows[...])
    rows = held.shape[3]
    for out in outs:
        for far_row in range(2):
            for far_side in range(2):
                for path in range(2):
                    target = sum_place(out, path, far_row, far_side).at[:, pl.ds(rows, SMALL)]
                    copy(small.at[:, flip(place.row, far_row)], target, small_sem)
    wait_all(ctx, ctx_sem)
    wait_all(grad, grad_sem)
    held[3] = low(t_mm(side_by_side(ctx, 0), low(grad[...]))).reshape(held.shape[1:])
    store_columns(place, 3, held.at[3], outs, held_sem)
    if with_states:
        for block in range(3):
            wait_all(weight.at[block], weight_sem.at[block])

        def state_step(block, carry):
            grad[...] += mm_t(side_by_side(grads, block), weight[block].reshape(WIDE, WIDE))
            return carry

        lax.fori_loop(0, 3, state_step, 0)
        copy(grad, x_grad_ref, out_sem)
        wait_all(grad, out_sem)
    wait_all(held, held_sem)
    for _ in range(8):
        wait_all(small, small_sem)


def qkv_backward(depth, extra, pos_ref, grad_ref, grads_ref, *refs):
    parts, refs = refs[:10], refs[10 + extra :]
    x_grad_ref, total, weight, grads, weight_sem, grads_sem, grad_sem, out_sem = refs
    place = Place(pos_ref)
    copy(grads_ref, grads, grads_sem)
    for block in range(3):
        load_block(place, block, parts, weight.at[block], weight_sem.at[block])
    copy(grad_ref, total, grad_sem)
    wait_all(grads, grads_sem)
    for block in range(3):
        wait_all(weight.at[block], weight_sem.at[block])
    wait_all(total, grad_sem)

    def block_step(block, carry):
        total[...] += mm_t(side_by_side(grads, block), weight[block].reshape(WIDE, WIDE))
        return carry

    lax.fori_loop(0, 3, block_step, 0)
    copy(total, x_grad_ref, out_sem)
    wait_all(total, out_sem)


def finish_first(extra, pos_ref, *refs):
    core, side = pos_ref[0], pos_ref[1]
    quarters, refs = refs[:8], refs[8 + extra :]
    qkv_ref, out_ref, up_bias_ref, biases_ref, gains_ref = refs
    rows = qkv_ref.shape[1]
    for layer in range(LAYERS):
        for far in range(4):
            at_core, at_side = flip(core, far // 2), flip(side, far % 2)
            half = at_core * HALF
            blocks = []
            for block in range(2):
                start = block * (rows + SMALL)
                if layer:
                    blocks.append(full(quarters[4 + far][start : start + rows + SMALL, :]))
                else:
                    blocks.append(full(quarters[far][block]))
            if far == 0:
                small = blocks[0][rows:, :]
                up_bias_ref[layer : layer + 1, :] = small[0:1, : up_bias_ref.shape[1]]
                biases_ref[:, layer] = small[1:7, : biases_ref.shape[2]]
                gains_ref[layer] = small[7:9, : gains_ref.shape[2]]
            lanes = pl.ds(pl.multiple_of(at_side * (2 * WIDE) + half, HALF), HALF)
            qkv_ref[layer, :, lanes] = blocks[0][:rows, :]
            last = blocks[1][:rows, :]

            @pl.when(at_side == 0)
            def _():
                qkv_ref[layer, :, pl.ds(pl.multiple_of(WIDE + half, HALF), HALF)] = last

            @pl.when(at_side == 1)
            def _():
                out_ref[layer, :, half_lanes(at_core)] = last


def finish_second(extra, pos_ref, *refs):
    core, side = pos_ref[0], pos_ref[1]
    quarters, (up_ref, down_ref) = refs[:8], refs[8 + extra :]
    rows = up_ref.shape[1]
    for layer in range(LAYERS):
        for far in range(4):
            at_core, at_side = flip(core, far // 2), flip(side, far % 2)
            blocks = []
            for block in range(4):
                start = 2 * (rows + SMALL) + block * rows
                if layer:
                    blocks.append(full(quarters[4 + far][block]))
                else:
                    blocks.append(full(quarters[far][start : start + rows, :]))
            for block in range(2):
                lanes = pl.ds(
                    pl.multiple_of(at_side * (2 * WIDE) + block * WIDE + at_core * HALF, HALF), HALF
                )
                up_ref[layer, :, lanes] = blocks[block]
                down_rows = pl.ds(pl.multiple_of((at_side * 2 + block) * rows, rows), rows)
                down_ref[layer, down_rows, half_lanes(at_core)] = blocks[2 + block]


def prepare(
    pos_ref, qkv_ref, out_ref, up_ref, down_ref, up_bias_ref, biases_ref, gains_ref,
    first_group, second_group, third_group, rows_of, sem,
):
    core, side = pos_ref[0], pos_ref[1]
    rows = out_ref.shape[1]
    up_size, width = up_bias_ref.shape[1], biases_ref.shape[2]
    for layer in range(LAYERS):
        for block in range(2):
            at = side * 2 + block
            lanes = pl.ds(pl.multiple_of(at * WIDE + core * HALF, HALF), HALF)
            if layer == 0:
                target = first_group.at[block, 0, pl.ds(0, rows)]
                up, down = second_group.at[block, 0], second_group.at[block, 1]
            else:
                target, up, down = (third_group.at[block, unit] for unit in range(3))
            if block == 0:
                pltpu.make_async_copy(qkv_ref.at[layer, :, lanes], target, sem.at[layer, 0, 0]).start()
            else:

                @pl.when(side == 0)
                def _():
                    lanes = pl.ds(pl.multiple_of(WIDE + core * HALF, HALF), HALF)
                    pltpu.make_async_copy(qkv_ref.at[layer, :, lanes], target, sem.at[layer, 0, 1]).start()

                @pl.when(side == 1)
                def _():
                    pltpu.make_async_copy(
                        out_ref.at[layer, :, half_lanes(core)], target, sem.at[layer, 0, 1]
                    ).start()

            pltpu.make_async_copy(up_ref.at[layer, :, lanes], up, sem.at[layer, 1, block]).start()
            down_rows = pl.ds(pl.multiple_of(at * rows, rows), rows)
            pltpu.make_async_copy(
                down_ref.at[layer, down_rows, half_lanes(core)], down, sem.at[layer, 2, block]
            ).start()
    for layer in range(LAYERS):
        rows_of[...] = jnp.zeros_like(rows_of)
        rows_of[0:1, :up_size] = full(up_bias_ref[layer : layer + 1, :])
        rows_of[1:7, :width] = full(biases_ref[:, layer])
        rows_of[7:9, :width] = full(gains_ref[layer])
        first_group[layer, 0, rows : rows + SMALL, :] = low(rows_of[...])
    for layer in range(LAYERS):
        for block in range(2):
            for unit in range(3):
                if layer:
                    part = third_group.at[block, unit]
                elif unit:
                    part = second_group.at[block, unit - 1]
                else:
                    part = first_group.at[block, 0, pl.ds(0, rows)]
                wait_all(part, sem.at[layer, unit, block])


def columns_of(depth, pos_ref, *refs):
    level, out = pos_ref[3], refs[-1]
    for path in range(2):
        for far_level, piece in enumerate(refs[:depth]):
            out[path, lax.rem(level + depth - far_level, depth)] = piece[path]


def split_columns(sizes, column_ref, *refs):
    start = 0
    for size, out in zip(sizes, refs[-len(sizes) :]):
        for path in range(2):
            out[path] = column_ref[:, path, start : start + size]
        start += size


def add_up(jobs, *refs):
    start, out = 0, sum(sum(counts) for counts, _ in jobs)
    for counts, form in jobs:
        row = 0
        for at, count in enumerate(counts):
            total = full(refs[start][...])
            for ref in refs[start + 1 : start + count]:
                total = total + full(ref[...])
            if form == "joined":
                refs[out][at] = low(total)
            elif form == "beside":
                refs[out][:, at] = low(total)
            elif form == "rows":
                refs[out][:, row : row + total.shape[1], :] = low(total)
                row += total.shape[1]
            else:
                refs[out + at][...] = low(total)
            start += count
        out += 1 if form else len(counts)


def add_up_far(depth, count, pos_ref, *refs):
    inputs, outs = refs[: 2 * count], refs[2 * count :]
    step = pl.program_id(0)
    for path in range(2):
        total = full(inputs[path * count][...])
        for ref in inputs[path * count + 1 : (path + 1) * count]:
            total = total + full(ref[...])
        for at in range(depth):

            @pl.when(step == at)
            def _():
                outs[at][path] = total[0].astype(outs[at].dtype)


def add_all(*refs):
    total = full(refs[0][...])
    for ref in refs[1:-1]:
        total = total + full(ref[...])
    refs[-1][...] = low(total)


def spread(depth, up_size, width, path, pos_ref, near_ref, far_ref, params_ref, small, sem):
    place = Place(pos_ref)
    rows = near_ref.shape[3] - SMALL
    for far_row, part in enumerate((near_ref.at[path], far_ref.at[path])):
        for level in range(depth):
            pltpu.make_async_copy(
                part.at[level, 0, pl.ds(rows, SMALL)], small.at[far_row, level], sem
            ).start()
    wait_all(small, sem)
    ups, others = 0.0, 0.0
    for far_row in range(2):
        for level in range(depth):
            shard = place.shard(level, far_row)
            block = full(small[far_row, level])
            up = jnp.concatenate([block, jnp.zeros((SMALL, 4 * WIDE - HALF), F32)], 1)
            ups += pltpu.roll(up, shard * up_size, 1)
            other = jnp.concatenate([block[:, :128], jnp.zeros((SMALL, WIDE - 128), F32)], 1)
            others += pltpu.roll(other, shard * width, 1)
    params_ref[...] = ups
    params_ref[1:9, :WIDE] = others[1:9]


VMEM = pltpu.MemorySpace.VMEM
SMEM = pltpu.MemorySpace.SMEM
ANY = pl.ANY
F32 = jnp.float32
BF16 = jnp.bfloat16


def call(kernel, spaces, outs, scratch, cost, after=(), limit=VMEM_LIMIT):
    run = pl.pallas_call(
        kernel,
        in_specs=[pl.BlockSpec(memory_space=space) for space in spaces + [ANY] * len(after)],
        out_specs=[pl.BlockSpec(memory_space=space) for _, _, space in outs],
        out_shape=[jax.ShapeDtypeStruct(shape, dtype) for shape, dtype, _ in outs],
        scratch_shapes=scratch,
        compiler_params=pltpu.CompilerParams(vmem_limit_bytes=limit),
        cost_estimate=pl.CostEstimate(flops=int(cost * COST), bytes_accessed=0, transcendentals=0),
    )
    return lambda *args: run(*args, *after)


def pass_through(*refs):
    pass


def tie(values, after):
    count = len(values)
    return pl.pallas_call(
        pass_through,
        in_specs=[pl.BlockSpec(memory_space=ANY)] * (count + len(after)),
        out_specs=[pl.BlockSpec(memory_space=ANY)] * count,
        out_shape=[jax.ShapeDtypeStruct(value.shape, value.dtype) for value in values],
        input_output_aliases={at: at for at in range(count)},
    )(*values, *after)


DMA = pltpu.SemaphoreType.DMA


class Sizes:
    def __init__(self, tokens, seqs, shards, rows, up_size, width):
        self.tokens, self.seqs, self.shards, self.rows = tokens, seqs, shards, rows
        self.up_size, self.width = up_size, width
        self.depth = shards // 2
        self.slots = tokens // seqs

    def columns(self, count):
        return pltpu.VMEM((count, self.depth, 2, self.rows, WIDE), BF16)

    def by_rows(self):
        return pltpu.VMEM((self.depth, 2, 4, self.rows, WIDE), BF16)

    def unit_grad(self, more=0):
        return [((2, 2, 2, self.depth, self.rows + more, HALF), BF16, ANY)] * 2


def run_attention_forward(z, pos, counts, x, group, params, after=()):
    t = z.tokens
    rows = [((t, WIDE), F32), ((t, WIDE), BF16), ((t, WIDE), F32), ((t, 128), F32)]
    panels = [((PAIRS, t, PAIR), BF16), ((3 * PAIRS, t, PAIR), BF16)]
    probs = ((z.seqs, PAIRS, z.slots, 2 * KEYS), BF16)
    return call(
        functools.partial(attention_forward, z.depth, z.seqs, len(after)),
        [SMEM, SMEM] + [ANY] * 12,
        [(*out, ANY) for out in rows + panels + [probs]],
        [
            pltpu.VMEM((t, WIDE), x.dtype),
            pltpu.VMEM((SMALL, WIDE), F32),
            *[pltpu.VMEM(*out) for out in rows + panels],
            z.columns(4),
            pltpu.VMEM(*probs),
            DMA,
            DMA,
            DMA((4,)),
            DMA,
            DMA,
            DMA((4,)),
            DMA,
        ],
        21,
        after,
    )(pos, counts, x, params, *group)


def run_mlp_forward(z, pos, first, group, params, after=()):
    t = z.tokens
    rows = [((t, WIDE), F32), ((t, WIDE), BF16), ((t, WIDE), F32), ((t, 128), F32)]
    tiles = [((4, t, WIDE), BF16)] * 2
    return call(
        functools.partial(mlp_forward, z.depth, len(after)),
        [SMEM] + [ANY] * 12,
        [(*out, ANY) for out in rows + tiles],
        [
            pltpu.VMEM((SMALL, 4 * WIDE), F32),
            *[pltpu.VMEM(*out) for out in rows],
            z.columns(4),
            z.by_rows(),
            pltpu.VMEM((2, t, WIDE), F32),
            pltpu.VMEM((t, WIDE), BF16),
            *[pltpu.VMEM(*out) for out in tiles],
            DMA,
            DMA,
            DMA((4,)),
            DMA((4,)),
            DMA,
            DMA,
            DMA,
        ],
        20,
        after,
    )(pos, first, params, *group)


def run_down_backward(z, pos, grad, hat, scale, params, act, after=()):
    t = z.tokens
    return call(
        functools.partial(down_backward, z.depth, len(after)),
        [SMEM] + [ANY] * 5,
        [
            ((t, WIDE), F32, ANY),
            ((8, WIDE), F32, ANY),
            *z.unit_grad(),
        ],
        [
            pltpu.VMEM((SMALL, WIDE), F32),
            pltpu.VMEM((8, WIDE), F32),
            pltpu.VMEM((t, WIDE), grad.dtype),
            pltpu.VMEM((t, WIDE), F32),
            pltpu.VMEM((t, 128), F32),
            pltpu.VMEM((t, WIDE), F32),
            pltpu.VMEM((4, t, WIDE), BF16),
            z.by_rows(),
            DMA,
            DMA,
            DMA((4,)),
            DMA((4,)),
            DMA,
            DMA,
        ],
        10,
        after,
    )(pos, params, grad, hat, scale, act)


def run_up_backward(z, pos, second, group, slope, first_low, hat, scale, params, after=()):
    t = z.tokens
    return call(
        functools.partial(up_backward, z.depth, len(after)),
        [SMEM] + [ANY] * 16,
        [
            ((t, WIDE), F32, ANY),
            ((8, WIDE), F32, ANY),
            ((1, 4 * WIDE), F32, ANY),
            *z.unit_grad(),
        ],
        [
            pltpu.VMEM((SMALL, WIDE), F32),
            pltpu.VMEM((8, WIDE), F32),
            pltpu.VMEM((1, 4 * WIDE), F32),
            z.columns(4),
            z.by_rows(),
            pltpu.VMEM((4, t, WIDE), BF16),
            pltpu.VMEM((t, WIDE), F32),
            pltpu.VMEM((t, WIDE), BF16),
            pltpu.VMEM((t, WIDE), F32),
            pltpu.VMEM((t, 128), F32),
            z.columns(4),
            DMA,
            DMA,
            DMA,
            DMA((4,)),
            DMA,
            DMA,
            DMA,
            DMA,
            DMA((4,)),
            DMA,
            DMA,
        ],
        19,
        after,
    )(pos, params, second, slope, first_low, hat, scale, *group)


def run_attention_backward(z, pos, grad, group, qkv, probs, after=()):
    t = z.tokens
    return call(
        functools.partial(attention_backward, z.depth, z.seqs, len(after)),
        [SMEM] + [ANY] * 13,
        [((3 * PAIRS, t, PAIR), BF16, ANY)],
        [
            pltpu.VMEM((z.depth, 2, z.rows, WIDE), BF16),
            pltpu.VMEM((t, WIDE), F32),
            pltpu.VMEM((3 * PAIRS, t, PAIR), BF16),
            pltpu.VMEM((z.seqs, PAIRS, z.slots, 2 * KEYS), BF16),
            pltpu.VMEM((PAIRS, t, PAIR), BF16),
            pltpu.VMEM((3 * PAIRS, t, PAIR), BF16),
            DMA,
            DMA,
            DMA,
            DMA,
            DMA,
        ],
        13,
        after,
    )(pos, grad, qkv, probs, *group)[0]


def run_qkv_weights(z, pos, grad, grads, ctx, x_low, down_sums, up_sums, up_bias, group=(), after=()):
    t = z.tokens
    more = [z.columns(3), DMA((3,)), DMA] if group else []
    return call(
        functools.partial(qkv_weights, z.depth, z.up_size, z.width, bool(group), len(after)),
        [SMEM] + [ANY] * (7 + len(group)),
        z.unit_grad(SMALL) + ([((t, WIDE), F32, ANY)] if group else []),
        [
            pltpu.VMEM((8, WIDE), F32),
            pltpu.VMEM((8, WIDE), F32),
            pltpu.VMEM((1, 4 * WIDE), F32),
            DMA((3,)),
            pltpu.VMEM((t, WIDE), F32),
            pltpu.VMEM((3 * PAIRS, t, PAIR), BF16),
            pltpu.VMEM((PAIRS, t, PAIR), BF16),
            pltpu.VMEM((t, WIDE), BF16),
            z.columns(4),
            pltpu.VMEM((8, WIDE), F32),
            pltpu.VMEM((SMALL, HALF), F32),
            pltpu.VMEM((z.depth, 2, SMALL, HALF), BF16),
            DMA,
            DMA((3,)),
            DMA,
            DMA,
            DMA,
            DMA,
            *more,
        ],
        8,
        after,
    )(pos, down_sums, up_sums, up_bias, grad, grads, ctx, x_low, *group)


def run_qkv_backward(z, pos, grad, grads, group, after=()):
    t = z.tokens
    return call(
        functools.partial(qkv_backward, z.depth, len(after)),
        [SMEM] + [ANY] * 12,
        [((t, WIDE), F32, ANY)],
        [
            pltpu.VMEM((t, WIDE), F32),
            z.columns(3),
            pltpu.VMEM((3 * PAIRS, t, PAIR), BF16),
            DMA((3,)),
            DMA,
            DMA,
            DMA,
        ],
        6,
        after,
    )(pos, grad, grads, *group)[0]


def run_finish_first(z, pos, quarters, after=()):
    r = z.rows
    return call(
        functools.partial(finish_first, len(after)),
        [SMEM] + [VMEM] * (4 * LAYERS),
        [
            ((LAYERS, r, 3 * WIDE), F32, VMEM),
            ((LAYERS, r, WIDE), F32, VMEM),
            ((LAYERS, z.up_size), F32, VMEM),
            ((6, LAYERS, z.width), F32, VMEM),
            ((LAYERS, 2, z.width), F32, VMEM),
        ],
        [],
        3,
        after,
        limit=SMALL_LIMIT,
    )(pos, *quarters)


def run_finish_second(z, pos, quarters, after=()):
    r = z.rows
    return call(
        functools.partial(finish_second, len(after)),
        [SMEM] + [VMEM] * (4 * LAYERS),
        [
            ((LAYERS, r, 4 * WIDE), F32, VMEM),
            ((LAYERS, 4 * r, WIDE), F32, VMEM),
        ],
        [],
        5,
        after,
        limit=SMALL_LIMIT,
    )(pos, *quarters)


def run_prepare(z, pos, *arrays):
    r = z.rows
    return call(
        prepare,
        [SMEM] + [ANY] * 4 + [VMEM] * 3,
        [
            ((2, 1, r + SMALL, HALF), BF16, VMEM),
            ((2, 2, r, HALF), BF16, VMEM),
            ((2, 3, r, HALF), BF16, VMEM),
        ],
        [
            pltpu.VMEM((SMALL, HALF), F32),
            DMA((LAYERS, 3, 2)),
        ],
        1,
        limit=SMALL_LIMIT,
    )(pos, *arrays)


def run_columns_of(pos, pieces):
    depth, shape = len(pieces), pieces[0].shape
    return call(
        functools.partial(columns_of, depth),
        [SMEM] + [VMEM] * depth,
        [((2, depth) + shape[1:], BF16, VMEM)],
        [],
        2,
    )(pos, *pieces)[0]


def run_split_columns(column, sizes):
    depth, _, _, *rest = column.shape
    outs = [((2, depth, size, *rest), BF16, VMEM) for size in sizes]
    return call(functools.partial(split_columns, sizes), [VMEM], outs, [], 2)(column)


def add_specs(sums, size, place):
    specs = []
    for parts in sums:
        for array, lead in parts:
            rest = array.shape[len(lead) + 1 :]
            specs.append(
                pl.BlockSpec(
                    (None,) * len(lead) + (size,) + rest,
                    lambda *at, lead=lead, rest=len(rest): lead + (place(*at),) + (0,) * rest,
                )
            )
    return specs


def run_add_up(jobs):
    specs, arrays, outs, out_specs = [], [], [], []
    for sums, form in jobs:
        array, lead = sums[0][0]
        depth, *rest = array.shape[len(lead) :]
        size, count = depth // 2, len(sums)
        specs += add_specs(sums, size, lambda step: step)
        arrays += [array for parts in sums for array, _ in parts]
        if form == "joined":
            outs.append((count, depth, *rest))
            out_specs.append(pl.BlockSpec((count, size, *rest), lambda step: (0, step, 0, 0)))
        elif form == "rows":
            rows = sum(parts[0][0].shape[-2] for parts in sums)
            outs.append((depth, rows, HALF))
            out_specs.append(pl.BlockSpec((size, rows, HALF), lambda step: (step, 0, 0)))
        elif form == "beside":
            outs.append((depth, count, *rest))
            out_specs.append(pl.BlockSpec((size, count, *rest), lambda step: (step, 0, 0, 0)))
        else:
            outs += [(depth, *rest)] * count
            out_specs += [
                pl.BlockSpec((size, *rest), lambda step, zeros=(0,) * len(rest): (step,) + zeros)
            ] * count
    results = list(
        pl.pallas_call(
            functools.partial(add_up, [([len(parts) for parts in sums], form) for sums, form in jobs]),
            grid=(2,),
            in_specs=specs,
            out_specs=out_specs,
            out_shape=[jax.ShapeDtypeStruct(out, BF16) for out in outs],
            compiler_params=pltpu.CompilerParams(vmem_limit_bytes=SMALL_LIMIT),
            cost_estimate=pl.CostEstimate(flops=int(3 * COST), bytes_accessed=0, transcendentals=0),
        )(*arrays)
    )
    grouped = []
    for sums, form in jobs:
        count = 1 if form else len(sums)
        grouped.append(results[:count])
        results = results[count:]
    return grouped


def run_add_up_far(pos, sums):
    array, lead = sums[0][0]
    depth, *rest = array.shape[len(lead) :]
    outs = [jax.ShapeDtypeStruct((2, *rest), F32 if at == 0 else BF16) for at in range(depth)]
    return pl.pallas_call(
        functools.partial(add_up_far, depth, len(sums[0])),
        grid_spec=pltpu.PrefetchScalarGridSpec(
            num_scalar_prefetch=1,
            grid=(depth,),
            in_specs=add_specs(sums, 1, lambda step, pos_ref: lax.rem(pos_ref[3] + step, depth)),
            out_specs=[pl.BlockSpec(out.shape, lambda step, pos_ref: (0, 0, 0)) for out in outs],
        ),
        out_shape=outs,
        compiler_params=pltpu.CompilerParams(vmem_limit_bytes=SMALL_LIMIT),
        cost_estimate=pl.CostEstimate(flops=int(3 * COST), bytes_accessed=0, transcendentals=0),
    )(pos, *[array for parts in sums for array, _ in parts])


def run_add_all(arrays):
    return call(add_all, [VMEM] * len(arrays), [(arrays[0].shape, BF16, VMEM)], [], 1, limit=SMALL_LIMIT)(*arrays)[0]


def run_spread(z, pos, near, far, path):
    return call(
        functools.partial(spread, z.depth, z.up_size, z.width, path),
        [SMEM, ANY, ANY],
        [((SMALL, 4 * WIDE), F32, VMEM)],
        [pltpu.VMEM((2, z.depth, SMALL, HALF), BF16), DMA],
        2,
        limit=SMALL_LIMIT,
    )(pos, near, far)[0]


class Links:
    def __init__(self, rep_size, fsdp_size):
        self.rep_size, self.fsdp_size = rep_size, fsdp_size
        self.depth = fsdp_size // 2
        rep_at, fsdp_at = lax.axis_index("rep"), lax.axis_index("fsdp")
        self.core, self.side = rep_at % 2, (rep_at // 2) % 2
        self.row, self.level = fsdp_at % 2, fsdp_at // 2

    def permute(self, value, target):
        pairs = []
        for rep_at in range(self.rep_size):
            for fsdp_at in range(self.fsdp_size):
                to_rep, to_fsdp = target(rep_at, fsdp_at)
                pairs.append((rep_at * self.fsdp_size + fsdp_at, to_rep * self.fsdp_size + to_fsdp))
        return lax.ppermute(value, AXES, pairs)

    def other_core(self, value):
        return self.permute(value, lambda r, f: (r ^ 1, f))

    def other_side(self, value):
        return self.permute(value, lambda r, f: (r ^ 2, f))

    def other_row(self, value):
        return self.permute(value, lambda r, f: (r, f ^ 1))

    def level_up(self, value, step):
        return self.permute(value, lambda r, f: (r, ((f // 2 + step) % self.depth) * 2 + f % 2))

    def levels(self):
        return [list(range(row, self.fsdp_size, 2)) for row in range(2)]


class Gather:
    def __init__(self, name, links, columns):
        self.name, self.links, self.live, self.moving = name, links, [columns], []

    def scope(self, stage):
        return jax.named_scope("gather_" + self.name + "_" + stage)

    def first(self):
        with self.scope("first"):
            self.moving = [self.links.other_row(self.live[0]), self.links.other_side(self.live[0])]

    def second(self):
        self.live += self.moving
        with self.scope("second"):
            rows, sides = self.live[1:3]
            self.moving = [self.links.other_side(rows[0]), self.links.other_row(sides[1])]
        with self.scope("cores"):
            self.moving += [self.links.other_core(part) for part in self.live[:3]]

    def last(self):
        self.live += self.moving[:2]
        self.far = self.moving[2:]
        with self.scope("last"):
            self.moving = [self.links.other_core(part) for part in self.live[3:5]]

    def arrays(self):
        return self.live + self.far + self.moving


class Sum:
    def __init__(self, name, links, near, far):
        self.name, self.links, self.near, self.sends = name, links, near, [far]
        self.hops = ((links.other_row, links.other_side), (links.other_side, links.other_row))

    def scope(self, stage):
        return jax.named_scope("sum_" + self.name + "_" + stage)

    def cores(self):
        with self.scope("cores"):
            self.moving = [self.links.other_core(self.sends[0])]

    def at(self, far):
        return [[(array, lead + (far,)) for array, lead in parts] for parts in self.parts]

    def came(self):
        self.parts = [[(self.near, (path,)), (self.moving[0], (path,))] for path in range(2)]
        return [(self.at(1), None)]

    def first(self):
        with self.scope("first"):
            self.moving = [self.hops[path][0](self.sends[path]) for path in range(2)]


class Second:
    def __init__(self, name, links, sums):
        self.name, self.links, self.sums = name, links, sums

    def came(self):
        for one in self.sums:
            one.parts = [parts + [(move, ())] for parts, move in zip(one.at(0), one.moving)]
        return [([one.at(1)[path] for one in self.sums], "joined") for path in range(2)]

    def second(self):
        with jax.named_scope("sum_" + self.name + "_second"):
            self.moving = [hops[1](send) for hops, send in zip(self.sums[0].hops, self.sends)]


def add(*steps):
    jobs = [step.came() for step in steps]
    with jax.named_scope("add_" + "_".join(step.name for step in steps)):
        outs = run_add_up([job for step_jobs in jobs for job in step_jobs])
    for step, step_jobs in zip(steps, jobs):
        step.sends = [out for group in outs[: len(step_jobs)] for out in group]
        outs = outs[len(step_jobs) :]


class Share:
    def __init__(self, name, links, second):
        self.name, self.links, self.second = name, links, second

    def scope(self):
        return jax.named_scope("share_" + self.name)

    def parts(self):
        return [
            one.at(0)[path] + [(self.second.moving[path], (unit,))]
            for unit, one in enumerate(self.second.sums)
            for path in range(2)
        ]

    def came(self):
        return [(self.parts(), "beside")]

    def scatter(self):
        with self.scope():
            self.sends = [
                lax.psum_scatter(
                    self.sends[0], "fsdp", scatter_dimension=0, axis_index_groups=self.links.levels()
                )
            ]

    def add_far(self, pos):
        with self.scope():
            self.kept, *self.sends = run_add_up_far(pos, self.parts())

    def levels(self):
        with self.scope():
            self.moving = [self.links.level_up(send, at + 1) for at, send in enumerate(self.sends)]

    def after_levels(self):
        with self.scope():
            self.sends = [run_add_all([self.kept] + self.moving)]

    def copies(self):
        if self.links.rep_size > 4:
            groups = [list(range(first, self.links.rep_size, 4)) for first in range(4)]
            self.sends = [lax.psum(self.sends[0], "rep", axis_index_groups=groups)]

    def sides(self):
        with self.scope():
            self.sends += [self.links.other_side(self.sends[0])]

    def last(self):
        with self.scope():
            self.moving = [self.links.other_core(send) for send in self.sends]

    def quarters(self):
        return self.sends + self.moving


class Mixed(Share):
    def __init__(self, name, links, seconds):
        super().__init__(name, links, None)
        self.seconds = seconds

    def came(self):
        parts = []
        for self.second in self.seconds:
            parts += self.parts()
        return [(parts, "rows")]


def order(steps, after=()):
    names = ("live", "moving", "sends")
    held = [(step, name) for step in steps for name in (names[:2] if hasattr(step, "live") else names[2:])]
    values = [value for step, name in held for value in getattr(step, name)]
    values = list(tie(values, list(after)))
    token = min(values, key=lambda value: value.size)
    for step, name in held:
        size = len(getattr(step, name))
        setattr(step, name, values[:size])
        values = values[size:]
    return [token]


def shards(
    rep_size, fsdp_size, hidden, region_counts, w_qkv, w_out, w_up, w_down, bias_up, biases, norm_gains, cotangent
):
    links = Links(rep_size, fsdp_size)
    z = Sizes(
        hidden.shape[0], region_counts.shape[0], fsdp_size, w_qkv.shape[1], bias_up.shape[1], biases.shape[2]
    )
    pos = jnp.stack([links.core, links.side, links.row, links.level]).astype(jnp.int32)
    quarters = run_prepare(
        z, pos, w_qkv, w_out, w_up, w_down, bias_up, jnp.transpose(biases, (1, 0, 2)), norm_gains
    )
    kept, groups, params = [], [None] * 4, [None] * 2

    def run_first(layer, states, after):
        return run_attention_forward(z, pos, region_counts, states, groups[2 * layer], params[layer], after)

    def run_second(layer, first, after):
        return run_mlp_forward(z, pos, first, groups[2 * layer + 1], params[layer], after)

    def columns(name, quarter, after=()):
        with jax.named_scope("columns_" + name):
            if after:
                quarter = tie([quarter], list(after))[0]
            pieces = [quarter] + [links.level_up(quarter, step) for step in range(1, links.depth)]
            return run_columns_of(pos, pieces)

    first_0 = Gather("first0", links, columns("first0", quarters[0]))
    first_0.first()
    second_0 = Gather("second0", links, columns("second0", quarters[1], first_0.live))

    order([first_0])
    first_0.second()

    second_0.first()
    order([first_0])
    first_0.last()
    with jax.named_scope("columns_third"):
        third = tie([quarters[2]], first_0.live[1:3])[0]
        third = lax.all_gather(third, "fsdp", axis_index_groups=links.levels())
    params = [run_spread(z, pos, *first_0.live[:2], layer) for layer in range(LAYERS)]
    groups[0] = first_0.arrays()
    one = run_first(0, hidden, params[1:])

    order([second_0], one[3:4])
    second_0.second()
    with jax.named_scope("columns_third"):
        third = run_split_columns(third, (1, 2))
    first_1, second_1 = (Gather(name, links, part) for name, part in zip(("first1", "second1"), third))

    first_1.first()

    order([second_0, second_1])
    second_0.last()
    second_1.first()
    groups[1] = second_0.arrays()
    two = run_second(0, one[0], ())
    kept.append((hidden, one, two))

    order([first_1], two[3:4])
    first_1.second()

    order([first_1, second_1])
    first_1.last()
    second_1.second()
    groups[2] = first_1.arrays()
    one = run_first(1, two[0], ())

    order([second_1], one[3:4])
    second_1.last()
    groups[3] = second_1.arrays()
    low_states = two[1]
    two = run_second(1, one[0], ())
    kept.append((low_states, one, two))
    output = two[1]

    def run_down(layer, gradient, after):
        _, _, hat, scale, act, _ = kept[layer][2]
        return run_down_backward(z, pos, gradient, hat, scale, params[layer], act, after)

    def run_up(layer, second, after):
        _, first_low, hat, scale, *_ = kept[layer][1]
        return run_up_backward(
            z, pos, second, groups[2 * layer + 1], kept[layer][2][5], first_low, hat, scale, params[layer], after
        )

    def run_attention(layer, first_in, after):
        qkv, probs = kept[layer][1][5:7]
        return run_attention_backward(z, pos, first_in, groups[2 * layer], qkv, probs, after)

    def run_weights(layer, first_in, grads, small, group, after):
        return run_qkv_weights(z, pos, first_in, grads, kept[layer][1][4], kept[layer][0], *small, group, after)

    def run_states(layer, first_in, grads, after):
        return run_qkv_backward(z, pos, first_in, grads, groups[2 * layer], after)

    second, down_sums, near, far = run_down(1, cotangent, ())
    down_1 = Sum("down1", links, near, far)

    token = order([down_1])
    down_1.cores()
    first_in, up_sums, up_bias, near, far = run_up(1, second, token)
    up_1 = Sum("up1", links, near, far)

    add(down_1)
    token = order([down_1, up_1])
    down_1.first()
    up_1.cores()
    grads = run_attention(1, first_in, token)

    add(up_1)
    token = order([up_1], [grads] + down_1.moving)
    up_1.first()
    near, far, gradient = run_weights(1, first_in, grads, (down_sums, up_sums, up_bias), groups[2], token)
    first_1 = Sum("first1", links, near, far)

    second_1 = Second("second1", links, [up_1, down_1])
    add(second_1)
    token = order([second_1, first_1], [gradient])
    second_1.second()
    first_1.cores()
    second, down_sums, near, far = run_down(0, gradient, token)
    down_0 = Sum("down0", links, near, far)

    share_second_1 = Share("second1", links, second_1)
    order([down_0], second_1.moving + first_1.moving)
    down_0.cores()
    add(first_1, share_second_1)
    order([first_1, share_second_1])
    first_1.first()
    share_second_1.scatter()
    add(down_0)
    token = order([down_0])
    down_0.first()
    first_in, up_sums, up_bias, near, far = run_up(0, second, token)
    up_0 = Sum("up0", links, near, far)

    first_second_1 = Second("first1", links, [first_1])
    order([up_0], first_1.moving + down_0.moving)
    up_0.cores()
    add(first_second_1)
    order([first_second_1])
    first_second_1.second()
    add(up_0)
    token = order([up_0])
    up_0.first()
    grads = run_attention(0, first_in, token)

    second_0 = Second("second0", links, [up_0, down_0])
    add(second_0)
    token = order([second_0], [grads] + first_second_1.moving)
    second_0.second()
    near, far = run_weights(0, first_in, grads, (down_sums, up_sums, up_bias), (), token)
    first_0 = Sum("first0", links, near, far)

    mixed = Mixed("mixed", links, [first_second_1, second_0])
    order([first_0], second_0.moving)
    first_0.cores()
    add(mixed)
    order([mixed])
    mixed.scatter()
    add(first_0)
    token = order([first_0])
    first_0.first()
    gradient = run_states(0, first_in, grads, token)

    first_second_0 = Second("first0", links, [first_0])
    first_0.moving = list(tie(first_0.moving, [gradient]))
    add(first_second_0)
    order([first_second_0])
    first_second_0.second()

    share_first_0 = Share("first0", links, first_second_0)
    share_first_0.add_far(pos)
    mixed.copies()
    share_second_1.copies()
    order([share_first_0, mixed, share_second_1])
    share_first_0.levels()
    mixed.sides()
    share_second_1.sides()

    share_first_0.after_levels()
    share_first_0.copies()
    order([share_first_0, mixed, share_second_1])
    share_first_0.sides()
    mixed.last()
    share_second_1.last()

    order([share_first_0], mixed.moving + share_second_1.moving)
    share_first_0.last()
    up_grad, down_grad = run_finish_second(z, pos, mixed.quarters() + share_second_1.quarters())
    qkv_grad, out_grad, up_bias_grad, biases_grad, gains_grad = run_finish_first(
        z, pos, share_first_0.quarters() + mixed.quarters(), [up_grad]
    )
    biases_grad = jnp.transpose(biases_grad, (1, 0, 2))
    return output, gradient, qkv_grad, out_grad, up_grad, down_grad, up_bias_grad, biases_grad, gains_grad


def solution(mesh):
    in_specs = (
        P(("rep", "fsdp"), None),
        P(("rep", "fsdp")),
        P(None, "fsdp", None),
        P(None, "fsdp", None),
        P(None, "fsdp", None),
        P(None, "fsdp", None),
        P(None, "fsdp"),
        P(None, None, "fsdp"),
        P(None, None, "fsdp"),
        P(("rep", "fsdp"), None),
    )
    out_specs = (
        P(("rep", "fsdp"), None),
        P(("rep", "fsdp"), None),
        P(None, "fsdp", None),
        P(None, "fsdp", None),
        P(None, "fsdp", None),
        P(None, "fsdp", None),
        P(None, "fsdp"),
        P(None, None, "fsdp"),
        P(None, None, "fsdp"),
    )
    local = functools.partial(shards, mesh.shape["rep"], mesh.shape["fsdp"])
    return jax.shard_map(local, mesh=mesh, in_specs=in_specs, out_specs=out_specs, check_vma=False)
```

```python
import functools

import jax
import jax.numpy as jnp
from jax import lax
from jax.experimental import pallas as pl
from jax.experimental.pallas import tpu as pltpu
from jax.sharding import PartitionSpec as P

HEADS = 12
HEAD_DIM = 64
LAYERS = 2
TEXT = 128
KEYS = 256
WIDE = 768
HALF = WIDE // 2
PAIR = 2 * HEAD_DIM
PAIRS = HEADS // 2
EPSILON = 1e-12
MASKED = -1000000000.0
AXES = ("rep", "fsdp")
COST = 1.15e9
SMALL = 16
VMEM_LIMIT = 64 * 1024 * 1024
SMALL_LIMIT = VMEM_LIMIT


def low(value):
    return value.astype(jnp.bfloat16)


def full(value):
    return value.astype(jnp.float32)


def mm(left, right):
    return jnp.dot(left, right, preferred_element_type=jnp.float32)


def mm_t(left, right):
    return lax.dot_general(
        left, right, (((1,), (1,)), ((), ())), preferred_element_type=jnp.float32
    )


def t_mm(left, right):
    return lax.dot_general(
        left, right, (((0,), (0,)), ((), ())), preferred_element_type=jnp.float32
    )


def flip(at, by):
    return 1 - at if by else at


class Place:
    def __init__(self, pos_ref):
        self.core, self.side = pos_ref[0], pos_ref[1]
        self.row, self.level = pos_ref[2], pos_ref[3]

    def shard(self, level, far_row):
        return level * 2 + flip(self.row, far_row)


def half_lanes(at):
    return pl.ds(pl.multiple_of(at * HALF, HALF), HALF)


def part_of(arrays, path, far_core, far_side, far_row):
    arrays = arrays[5 * far_core : 5 * far_core + 5]
    if far_side and far_row:
        return arrays[3 + path]
    return arrays[2 * far_side + far_row].at[path]


def load_unit(place, arrays, unit, whole, sems, by_rows):
    rows = pl.ds(0, whole.shape[3])
    for far_side in range(2):
        for path in range(2):
            block = flip(place.side, far_side) * 2 + path
            for far_core in range(2):
                lanes = half_lanes(flip(place.core, far_core))
                for far_row in range(2):
                    row = flip(place.row, far_row)
                    part = part_of(arrays, path, far_core, far_side, far_row).at[:, unit, rows]
                    if by_rows:
                        copy(part, whole.at[:, row, block, :, lanes], sems)
                    else:
                        copy(part, whole.at[block, :, row, :, lanes], sems.at[block])


def load_block(place, block, arrays, whole, sem):
    path = block % 2
    rows = pl.ds(0, whole.shape[2])
    needed_side = place.side if block // 2 == 0 else 1 - place.side
    for far_side in range(2):

        @pl.when(needed_side == far_side)
        def _():
            for far_core in range(2):
                lanes = half_lanes(flip(place.core, far_core))
                for far_row in range(2):
                    part = part_of(arrays, path, far_core, far_side, far_row).at[:, 0, rows]
                    copy(part, whole.at[:, flip(place.row, far_row), :, lanes], sem)


def copy(source, target, sem):
    pltpu.make_async_copy(source, target, sem).start()


def wait_all(ref, sem):
    pltpu.make_async_copy(ref, ref, sem).wait()


def either(choice, one, other):
    return other + choice * (one - other)


def either(choice, one, other):
    return other + choice * (one - other)


def sum_place(out, block, far_row, far_side):
    path = block % 2
    return out.at[path, either(path, far_side, far_row), either(path, far_row, far_side)]


def side_distance(place, block):
    return either(place.side, 1 - block // 2, block // 2)


def store_columns(place, block, held, outs, sem):
    rows = pl.ds(0, held.shape[2])
    far_side = side_distance(place, block)
    for far_core, out in enumerate(outs):
        lanes = half_lanes(flip(place.core, far_core))
        for far_row in range(2):
            source = held.at[:, flip(place.row, far_row), :, lanes]
            copy(source, sum_place(out, block, far_row, far_side).at[:, rows], sem)


def store_rows(place, levels, held, outs, sem):
    for far_core, out in enumerate(outs):
        lanes = half_lanes(flip(place.core, far_core))
        for block in range(4):
            far_side = side_distance(place, block)
            for far_row in range(2):
                source = held.at[levels, flip(place.row, far_row), block, :, lanes]
                copy(source, sum_place(out, block, far_row, far_side).at[levels], sem)


def chunks(rows):
    edges = [rows // 16 * at // 4 * 16 for at in range(4)] + [rows]
    return [(start, end - start) for start, end in zip(edges, edges[1:])]


def normalize(value):
    centered = value - jnp.mean(value, axis=-1, keepdims=True)
    scale = lax.rsqrt(jnp.mean(centered * centered, axis=-1, keepdims=True) + EPSILON)
    return centered * scale, scale


def norm_backward(grad, hat, scale, gain):
    direct = grad * gain
    return (
        direct
        - jnp.mean(direct, axis=-1, keepdims=True)
        - hat * jnp.mean(direct * hat, axis=-1, keepdims=True)
    ) * scale


def gelu_and_slope(value):
    size = jnp.abs(value) * 0.7071067811865476
    t = 1.0 / (1.0 + 0.3275911 * size)
    series = t * (
        0.127414796
        + t * (-0.142248368 + t * (0.7107068705 + t * (-0.7265760135 + t * 0.5307027145)))
    )
    bell = jnp.exp(-0.5 * value * value)
    tail = series * bell
    below = jnp.where(value >= 0, 1.0 - tail, tail)
    return value * below, below + value * bell * 0.3989422804014327


def head_masks(value, lane):
    none = jnp.zeros_like(value)
    return jnp.concatenate(
        [jnp.where(lane < HEAD_DIM, value, none), jnp.where(lane < HEAD_DIM, none, value)], 0
    )


def side_by_side(ref, block):
    return jnp.concatenate([ref[block * PAIRS + pair] for pair in range(PAIRS)], 1)


def attention_forward(depth, seqs, extra, pos_ref, counts_ref, x_ref, params_ref, *refs):
    parts, refs = refs[:10], refs[10 + extra :]
    first_out, first_low_out, hat_out, scale_out, ctx_out, qkv_out, probs_ref = refs[:7]
    x, params, first, first_low, hat, scale, ctx, qkv, weight, held, *sems = refs[7:]
    x_sem, params_sem, row_sem, ctx_sem, qkv_sem, weight_sem, held_sem = sems
    place = Place(pos_ref)
    copy(x_ref, x, x_sem)
    load_unit(place, parts, 0, weight, weight_sem, False)
    copy(params_ref.at[:, pl.ds(0, WIDE)], params, params_sem)
    tokens = x.shape[0]
    slots = tokens // seqs
    wait_all(x, x_sem)
    x_low = low(x[...])
    wait_all(params, params_sem)

    for block in range(3):
        wait_all(weight.at[block], weight_sem.at[block])

    def project(block, carry):
        out = mm(x_low, weight[block].reshape(WIDE, WIDE))
        bias = params[pl.ds(1 + block // 2, 1), :]
        out = low(out + jnp.where(block == 1, jnp.zeros_like(bias), bias))
        for pair in range(PAIRS):
            qkv[block * PAIRS + pair] = out[:, pair * PAIR : (pair + 1) * PAIR]
        return carry

    lax.fori_loop(0, 3, project, 0)
    copy(qkv, qkv_out, qkv_sem)
    lane = lax.broadcasted_iota(jnp.int32, (KEYS, PAIR), 1)
    key = lax.broadcasted_iota(jnp.int32, (slots, KEYS), 1)

    def pair_step(step, carry):
        seq, pair = step // PAIRS, lax.rem(step, PAIRS)
        rows = pl.ds(pl.multiple_of(seq * slots, 16), slots)
        key_rows = pl.ds(pl.multiple_of(seq * slots, 16), KEYS)
        valid = key < TEXT + counts_ref[seq]
        q = qkv[pair, rows, :] * jnp.bfloat16(HEAD_DIM**-0.5)
        scores = mm_t(q, head_masks(qkv[PAIRS + pair, key_rows, :], lane))
        halves = []
        for half in range(2):
            part = jnp.where(valid, scores[:, half * KEYS : (half + 1) * KEYS], MASKED)
            part = jnp.exp(part - jnp.max(part, axis=-1, keepdims=True))
            halves.append(low(part * (1.0 / jnp.sum(part, axis=-1, keepdims=True))))
        probs = jnp.concatenate(halves, 1)
        held[seq, pair] = probs
        copy(held.at[seq, pair], probs_ref.at[seq, pair], held_sem)
        ctx[pair, rows, :] = low(mm(probs, head_masks(qkv[2 * PAIRS + pair, key_rows, :], lane)))
        return carry

    lax.fori_loop(0, seqs * PAIRS, pair_step, 0, unroll=2)
    copy(ctx, ctx_out, ctx_sem)
    wait_all(weight.at[3], weight_sem.at[3])
    first[...] = mm(side_by_side(ctx, 0), weight[3].reshape(WIDE, WIDE))
    outs = ((first, first_out), (first_low, first_low_out), (hat, hat_out), (scale, scale_out))
    for start, size in chunks(tokens):
        rows = pl.ds(start, size)
        normal, factor = normalize(full(x[rows, :]) + (first[rows, :] + params[3:4, :]))
        hat[rows, :] = normal
        scale[rows, :] = jnp.broadcast_to(factor, (size, 128))
        value = normal * params[7:8, :] + params[4:5, :]
        first[rows, :] = value
        first_low[rows, :] = low(value)
        for at, (source, target) in enumerate(outs):
            copy(source.at[rows], target.at[rows], row_sem.at[at])
    for at, (source, _) in enumerate(outs):
        wait_all(source, row_sem.at[at])
    wait_all(ctx, ctx_sem)
    wait_all(qkv, qkv_sem)
    wait_all(held, held_sem)


def mlp_forward(depth, extra, pos_ref, first_ref, params_ref, *refs):
    parts, refs = refs[:10], refs[10 + extra :]
    out_out, out_low_out, hat_out, scale_out, act_ref, slope_ref = refs[:6]
    params, out, out_low, hat, scale, up, down, pre, first_low, act, slope, *sems = refs[6:]
    params_sem, first_sem, row_sem, up_sem, down_sem, act_sem, slope_sem = sems
    place = Place(pos_ref)
    copy(first_ref, out, first_sem)
    load_unit(place, parts, 0, up, up_sem, False)
    copy(params_ref, params, params_sem)
    load_unit(place, parts, 1, down, down_sem, True)
    tokens = out.shape[0]
    half = tokens // 2
    levels = depth // 4
    wait_all(out, first_sem)
    first_low[...] = low(out[...])
    act[3, half:, :] = jnp.zeros((half, WIDE), BF16)
    for tile in range(4):
        wait_all(up.at[tile], up_sem.at[tile])
    pre[0] = mm(first_low[...], up[0].reshape(WIDE, WIDE))
    wait_all(params, params_sem)
    out[...] += params[5:6, :WIDE]
    wait_all(down, down_sem)

    def half_rows(step):
        return pl.ds(pl.multiple_of(lax.rem(step, 2) * half, 16), half)

    def below(step):
        tile, rows = step // 2, half_rows(step)
        weight = down[pl.ds(tile * levels, levels)].reshape(WIDE, WIDE)
        out[rows, :] += mm(act[tile, rows, :], weight)

    def half_step(step, carry):
        tile, rows = step // 2, half_rows(step)
        slot, later = lax.rem(tile, 2), lax.rem(tile + 1, 4)
        bias = params[0:1, pl.ds(pl.multiple_of(tile * WIDE, WIDE), WIDE)]
        below(lax.rem(step + 7, 8))
        pre[1 - slot, rows, :] = mm(first_low[rows, :], up[later].reshape(WIDE, WIDE))
        gelu, rise = gelu_and_slope(pre[slot, rows, :] + bias)
        act[tile, rows, :] = low(gelu)
        slope[tile, rows, :] = low(rise)
        copy(slope.at[tile, rows], slope_ref.at[tile, rows], slope_sem)
        copy(act.at[tile, rows], act_ref.at[tile, rows], act_sem)
        return carry

    lax.fori_loop(0, 8, half_step, 0)
    below(7)
    outs = ((out, out_out), (out_low, out_low_out), (hat, hat_out), (scale, scale_out))
    for start, size in chunks(tokens):
        rows = pl.ds(start, size)
        normal, factor = normalize(out[rows, :])
        hat[rows, :] = normal
        scale[rows, :] = jnp.broadcast_to(factor, (size, 128))
        value = normal * params[8:9, :WIDE] + params[6:7, :WIDE]
        out[rows, :] = value
        out_low[rows, :] = low(value)
        for at, (source, target) in enumerate(outs):
            copy(source.at[rows], target.at[rows], row_sem.at[at])
    for at, (source, _) in enumerate(outs):
        wait_all(source, row_sem.at[at])
    wait_all(slope, slope_sem)
    wait_all(act, act_sem)


def load_rows(pairs, sem):
    for at, (start, size) in enumerate(chunks(pairs[0][0].shape[0])):
        for source, target in pairs:
            rows = pl.ds(start, size)
            copy(source.at[rows], target.at[rows], sem.at[at])


def norm_step(grad, hat, scale, gain, out, out_ref, sums, sums_ref, waits, sem, out_sem, sums_sem):
    totals = [0.0, 0.0, 0.0]
    for at, (start, size) in enumerate(chunks(grad.shape[0])):
        rows = pl.ds(start, size)
        for array in waits:
            wait_all(array.at[rows], sem.at[at])
        value, hat_rows = full(grad[rows, :]), hat[rows, :]
        grad_in = norm_backward(value, hat_rows, scale[rows, :][:, :1], gain)
        out[rows, :] = grad_in
        copy(out.at[rows], out_ref.at[rows], out_sem)
        for number, part in enumerate((value * hat_rows, value, full(low(grad_in)))):
            totals[number] += jnp.sum(part, axis=0, keepdims=True)
    sums[...] = jnp.zeros_like(sums)
    for number in range(3):
        sums[number : number + 1, :] = totals[number]
    copy(sums, sums_ref, sums_sem)


def down_backward(depth, extra, pos_ref, params_ref, grad_ref, hat_ref, scale_ref, act_ref, *refs):
    second_ref, sums_ref, near_ref, far_ref = refs[extra : extra + 4]
    params, sums, grad, hat, scale, second, act, held, *sems = refs[extra + 4 :]
    params_sem, sums_sem, row_sem, act_sem, out_sem, held_sem = sems
    place = Place(pos_ref)
    copy(params_ref.at[:, pl.ds(0, WIDE)], params, params_sem)
    load_rows([(grad_ref, grad), (hat_ref, hat), (scale_ref, scale)], row_sem)
    for tile in range(4):
        copy(act_ref.at[tile], act.at[tile], act_sem.at[tile])
    wait_all(params, params_sem)
    norm_step(
        grad, hat, scale, params[8:9, :], second, second_ref, sums, sums_ref, (grad, hat, scale), row_sem, out_sem, sums_sem
    )
    grad_low = low(second[...])
    for tile in range(4):
        wait_all(act.at[tile], act_sem.at[tile])

    levels = depth // 4

    def tile_step(tile, carry):
        held[pl.ds(tile * levels, levels)] = low(t_mm(act[tile], grad_low)).reshape((levels,) + held.shape[1:])
        return carry

    for start in (0, 2):
        lax.fori_loop(start, start + 2, tile_step, 0)
        store_rows(place, pl.ds(start * levels, 2 * levels), held, (near_ref, far_ref), held_sem)
    wait_all(second, out_sem)
    wait_all(sums, sums_sem)
    wait_all(held, held_sem)


def up_backward(
    depth, extra, pos_ref, params_ref, second_ref, slope_ref, first_low_ref, hat_ref, scale_ref, *refs
):
    parts, refs = refs[:10], refs[10 + extra :]
    first_in_ref, sums_ref, up_grad_ref, near_ref, far_ref = refs[:5]
    params, sums, up_grad, up, down, slope, total, first_low, hat, scale, held, *sems = refs[5:]
    params_sem, sums_sem, up_grad_sem, up_sem, down_sem, slope_sem, second_sem, first_sem, row_sem, out_sem, held_sem = sems
    place = Place(pos_ref)
    copy(second_ref, total, second_sem)
    load_unit(place, parts, 1, down, down_sem, True)
    copy(slope_ref, slope, slope_sem)
    levels = depth // 4
    wait_all(total, second_sem)
    grad_low = low(total[...])
    wait_all(down, down_sem)
    wait_all(slope, slope_sem)
    load_unit(place, parts, 0, up, up_sem, False)
    copy(first_low_ref, first_low, first_sem)
    load_rows([(hat_ref, hat), (scale_ref, scale)], row_sem)
    copy(params_ref.at[:, pl.ds(0, WIDE)], params, params_sem)

    def pre_step(tile, carry):
        weight = down[pl.ds(tile * levels, levels)].reshape(WIDE, WIDE)
        grad = low(mm_t(grad_low, weight) * full(slope[tile]))
        slope[tile] = grad
        up_grad[:, pl.ds(pl.multiple_of(tile * WIDE, WIDE), WIDE)] = jnp.sum(
            full(grad), axis=0, keepdims=True
        )
        return carry

    lax.fori_loop(0, 4, pre_step, 0)
    copy(up_grad, up_grad_ref, up_grad_sem)
    wait_all(first_low, first_sem)
    for tile in range(4):
        wait_all(up.at[tile], up_sem.at[tile])

    def tile_step(tile, carry):
        held[tile] = low(t_mm(first_low[...], slope[tile])).reshape(held.shape[1:])
        total[...] += mm_t(slope[tile], up[tile].reshape(WIDE, WIDE))
        store_columns(place, tile, held.at[tile], (near_ref, far_ref), held_sem)
        return carry

    lax.fori_loop(0, 4, tile_step, 0)
    wait_all(params, params_sem)
    norm_step(
        total, hat, scale, params[7:8, :], total, first_in_ref, sums, sums_ref, (hat, scale), row_sem, out_sem, sums_sem
    )
    wait_all(total, out_sem)
    wait_all(sums, sums_sem)
    wait_all(up_grad, up_grad_sem)
    wait_all(held, held_sem)


def attention_backward(depth, seqs, extra, pos_ref, grad_ref, qkv_ref, probs_ref, *refs):
    parts, refs = refs[:10], refs[10 + extra :]
    grads_ref = refs[0]
    weight, grad, qkv, probs, ctx_grad, grads, weight_sem, grad_sem, qkv_sem, probs_sem, out_sem = refs[1:]
    place = Place(pos_ref)
    copy(grad_ref, grad, grad_sem)
    load_block(place, 3, parts, weight, weight_sem)
    copy(qkv_ref, qkv, qkv_sem)
    copy(probs_ref, probs, probs_sem)
    tokens = grad.shape[0]
    slots = tokens // seqs
    wait_all(grad, grad_sem)
    wait_all(weight, weight_sem)
    from_out = low(mm_t(low(grad[...]), weight[...].reshape(WIDE, WIDE)))
    for pair in range(PAIRS):
        ctx_grad[pair] = from_out[:, pair * PAIR : (pair + 1) * PAIR]
    wait_all(qkv, qkv_sem)
    wait_all(probs, probs_sem)
    lane = lax.broadcasted_iota(jnp.int32, (KEYS, PAIR), 1)

    def pair_step(step, carry):
        seq, pair = step // PAIRS, lax.rem(step, PAIRS)
        start = pl.multiple_of(seq * slots, 16)
        rows, key_rows = pl.ds(start, slots), pl.ds(start, KEYS)
        q = qkv[pair, rows, :]
        out_grad = ctx_grad[pair, rows, :]
        weights = probs[seq, pair]
        probs_grad = mm_t(out_grad, head_masks(qkv[2 * PAIRS + pair, key_rows, :], lane))
        halves = []
        for half in range(2):
            lanes = slice(half * KEYS, (half + 1) * KEYS)
            weight_part, grad_part = full(weights[:, lanes]), probs_grad[:, lanes]
            dot = jnp.sum(weight_part * grad_part, axis=-1, keepdims=True)
            halves.append(low(weight_part * (grad_part - dot)))
        scores_grad = jnp.concatenate(halves, 1)
        q_grad = mm(scores_grad, head_masks(qkv[PAIRS + pair, key_rows, :], lane)) * HEAD_DIM**-0.5
        grads[pair, rows, :] = low(q_grad)
        k_grad = t_mm(q, scores_grad) * HEAD_DIM**-0.5
        v_grad = t_mm(out_grad, weights)
        for at, value in ((PAIRS, k_grad), (2 * PAIRS, v_grad)):
            value = jnp.concatenate([value[:HEAD_DIM, :KEYS], value[HEAD_DIM:, KEYS:]], 0)
            grads[at + pair, key_rows, :] = low(value.T)
            grads[at + pair, pl.ds(pl.multiple_of(start + KEYS, 16), slots - KEYS), :] = jnp.zeros(
                (slots - KEYS, PAIR), BF16
            )
        for at in range(3):
            copy(grads.at[at * PAIRS + pair, rows], grads_ref.at[at * PAIRS + pair, rows], out_sem)
        return carry

    lax.fori_loop(0, seqs * PAIRS, pair_step, 0, unroll=6)
    wait_all(grads, out_sem)


def qkv_weights(
    depth, up_size, width, with_states, extra, pos_ref, down_sums_ref, up_sums_ref, up_bias_ref, grad_ref, grads_ref, ctx_ref, x_ref,
    *refs,
):
    parts, refs = refs[: 10 * with_states], refs[10 * with_states + extra :]
    outs, refs = refs[:2], refs[2:]
    if with_states:
        x_grad_ref, *refs = refs
        *refs, weight, weight_sem, out_sem = refs
    down_sums, up_sums, up_bias, bias_sem, *refs = refs
    grad, grads, ctx, x_low, held, sums, block_rows, small, grad_sem, grads_sem, ctx_sem, x_sem, held_sem, small_sem = refs
    place = Place(pos_ref)
    copy(x_ref, x_low, x_sem)
    for block in range(3):
        panels = pl.ds(block * PAIRS, PAIRS)
        copy(grads_ref.at[panels], grads.at[panels], grads_sem.at[block])
    copy(ctx_ref, ctx, ctx_sem)
    copy(grad_ref, grad, grad_sem)
    if with_states:
        for block in range(3):
            load_block(place, block, parts, weight.at[block], weight_sem.at[block])
    biases = ((down_sums_ref, down_sums), (up_sums_ref, up_sums), (up_bias_ref, up_bias))
    for at, (source, target) in enumerate(biases):
        copy(source, target, bias_sem.at[at])
    wait_all(x_low, x_sem)
    for block in range(3):
        wait_all(grads.at[pl.ds(block * PAIRS, PAIRS)], grads_sem.at[block])

    def block_step(block, carry):
        part = side_by_side(grads, block)
        sums[pl.ds(block, 1), :] = jnp.sum(full(part), axis=0, keepdims=True)
        held[block] = low(t_mm(x_low[...], part)).reshape(held.shape[1:])
        store_columns(place, block, held.at[block], outs, held_sem)
        return carry

    lax.fori_loop(0, 3, block_step, 0)
    sums[1:2, :] = sums[2:3, :]
    for at, (_, target) in enumerate(biases):
        wait_all(target, bias_sem.at[at])
    block_rows[...] = jnp.zeros_like(block_rows)
    for shard in range(2 * depth):
        lanes = slice(shard * width, (shard + 1) * width)
        block_rows[0:1, :up_size] = up_bias[:, shard * up_size : (shard + 1) * up_size]
        block_rows[1:3, :width] = sums[0:2, lanes]
        for row, (ref, at) in enumerate(
            ((up_sums, 2), (up_sums, 1), (down_sums, 2), (down_sums, 1), (up_sums, 0), (down_sums, 0))
        ):
            block_rows[3 + row : 4 + row, :width] = ref[at : at + 1, lanes]
        small[shard // 2, shard % 2] = low(block_rows[...])
    rows = held.shape[3]
    for out in outs:
        for far_row in range(2):
            for far_side in range(2):
                for path in range(2):
                    target = sum_place(out, path, far_row, far_side).at[:, pl.ds(rows, SMALL)]
                    copy(small.at[:, flip(place.row, far_row)], target, small_sem)
    wait_all(ctx, ctx_sem)
    wait_all(grad, grad_sem)
    held[3] = low(t_mm(side_by_side(ctx, 0), low(grad[...]))).reshape(held.shape[1:])
    store_columns(place, 3, held.at[3], outs, held_sem)
    if with_states:
        for block in range(3):
            wait_all(weight.at[block], weight_sem.at[block])

        def state_step(block, carry):
            grad[...] += mm_t(side_by_side(grads, block), weight[block].reshape(WIDE, WIDE))
            return carry

        lax.fori_loop(0, 3, state_step, 0)
        copy(grad, x_grad_ref, out_sem)
        wait_all(grad, out_sem)
    wait_all(held, held_sem)
    for _ in range(8):
        wait_all(small, small_sem)


def qkv_backward(depth, extra, pos_ref, grad_ref, grads_ref, *refs):
    parts, refs = refs[:10], refs[10 + extra :]
    x_grad_ref, total, weight, grads, weight_sem, grads_sem, grad_sem, out_sem = refs
    place = Place(pos_ref)
    copy(grads_ref, grads, grads_sem)
    for block in range(3):
        load_block(place, block, parts, weight.at[block], weight_sem.at[block])
    copy(grad_ref, total, grad_sem)
    wait_all(grads, grads_sem)
    for block in range(3):
        wait_all(weight.at[block], weight_sem.at[block])
    wait_all(total, grad_sem)

    def block_step(block, carry):
        total[...] += mm_t(side_by_side(grads, block), weight[block].reshape(WIDE, WIDE))
        return carry

    lax.fori_loop(0, 3, block_step, 0)
    copy(total, x_grad_ref, out_sem)
    wait_all(total, out_sem)


def finish_first(extra, pos_ref, *refs):
    core, side = pos_ref[0], pos_ref[1]
    quarters, refs = refs[:8], refs[8 + extra :]
    qkv_ref, out_ref, up_bias_ref, biases_ref, gains_ref = refs
    rows = qkv_ref.shape[1]
    for layer in range(LAYERS):
        for far in range(4):
            at_core, at_side = flip(core, far // 2), flip(side, far % 2)
            half = at_core * HALF
            blocks = []
            for block in range(2):
                start = block * (rows + SMALL)
                if layer:
                    blocks.append(full(quarters[4 + far][start : start + rows + SMALL, :]))
                else:
                    blocks.append(full(quarters[far][block]))
            if far == 0:
                small = blocks[0][rows:, :]
                up_bias_ref[layer : layer + 1, :] = small[0:1, : up_bias_ref.shape[1]]
                biases_ref[:, layer] = small[1:7, : biases_ref.shape[2]]
                gains_ref[layer] = small[7:9, : gains_ref.shape[2]]
            lanes = pl.ds(pl.multiple_of(at_side * (2 * WIDE) + half, HALF), HALF)
            qkv_ref[layer, :, lanes] = blocks[0][:rows, :]
            last = blocks[1][:rows, :]

            @pl.when(at_side == 0)
            def _():
                qkv_ref[layer, :, pl.ds(pl.multiple_of(WIDE + half, HALF), HALF)] = last

            @pl.when(at_side == 1)
            def _():
                out_ref[layer, :, half_lanes(at_core)] = last


def finish_second(extra, pos_ref, *refs):
    core, side = pos_ref[0], pos_ref[1]
    quarters, (up_ref, down_ref) = refs[:8], refs[8 + extra :]
    rows = up_ref.shape[1]
    for layer in range(LAYERS):
        for far in range(4):
            at_core, at_side = flip(core, far // 2), flip(side, far % 2)
            blocks = []
            for block in range(4):
                start = 2 * (rows + SMALL) + block * rows
                if layer:
                    blocks.append(full(quarters[4 + far][block]))
                else:
                    blocks.append(full(quarters[far][start : start + rows, :]))
            for block in range(2):
                lanes = pl.ds(
                    pl.multiple_of(at_side * (2 * WIDE) + block * WIDE + at_core * HALF, HALF), HALF
                )
                up_ref[layer, :, lanes] = blocks[block]
                down_rows = pl.ds(pl.multiple_of((at_side * 2 + block) * rows, rows), rows)
                down_ref[layer, down_rows, half_lanes(at_core)] = blocks[2 + block]


def prepare(
    pos_ref, qkv_ref, out_ref, up_ref, down_ref, up_bias_ref, biases_ref, gains_ref,
    first_group, second_group, third_group, rows_of, sem,
):
    core, side = pos_ref[0], pos_ref[1]
    rows = out_ref.shape[1]
    up_size, width = up_bias_ref.shape[1], biases_ref.shape[2]
    for layer in range(LAYERS):
        for block in range(2):
            at = side * 2 + block
            lanes = pl.ds(pl.multiple_of(at * WIDE + core * HALF, HALF), HALF)
            if layer == 0:
                target = first_group.at[block, 0, pl.ds(0, rows)]
                up, down = second_group.at[block, 0], second_group.at[block, 1]
            else:
                target, up, down = (third_group.at[block, unit] for unit in range(3))
            if block == 0:
                pltpu.make_async_copy(qkv_ref.at[layer, :, lanes], target, sem.at[layer, 0, 0]).start()
            else:

                @pl.when(side == 0)
                def _():
                    lanes = pl.ds(pl.multiple_of(WIDE + core * HALF, HALF), HALF)
                    pltpu.make_async_copy(qkv_ref.at[layer, :, lanes], target, sem.at[layer, 0, 1]).start()

                @pl.when(side == 1)
                def _():
                    pltpu.make_async_copy(
                        out_ref.at[layer, :, half_lanes(core)], target, sem.at[layer, 0, 1]
                    ).start()

            pltpu.make_async_copy(up_ref.at[layer, :, lanes], up, sem.at[layer, 1, block]).start()
            down_rows = pl.ds(pl.multiple_of(at * rows, rows), rows)
            pltpu.make_async_copy(
                down_ref.at[layer, down_rows, half_lanes(core)], down, sem.at[layer, 2, block]
            ).start()
    for layer in range(LAYERS):
        rows_of[...] = jnp.zeros_like(rows_of)
        rows_of[0:1, :up_size] = full(up_bias_ref[layer : layer + 1, :])
        rows_of[1:7, :width] = full(biases_ref[:, layer])
        rows_of[7:9, :width] = full(gains_ref[layer])
        first_group[layer, 0, rows : rows + SMALL, :] = low(rows_of[...])
    for layer in range(LAYERS):
        for block in range(2):
            for unit in range(3):
                if layer:
                    part = third_group.at[block, unit]
                elif unit:
                    part = second_group.at[block, unit - 1]
                else:
                    part = first_group.at[block, 0, pl.ds(0, rows)]
                wait_all(part, sem.at[layer, unit, block])


def columns_of(depth, pos_ref, *refs):
    level, out = pos_ref[3], refs[-1]
    for path in range(2):
        for far_level, piece in enumerate(refs[:depth]):
            out[path, lax.rem(level + depth - far_level, depth)] = piece[path]


def split_columns(sizes, column_ref, *refs):
    start = 0
    for size, out in zip(sizes, refs[-len(sizes) :]):
        for path in range(2):
            out[path] = column_ref[:, path, start : start + size]
        start += size


def add_up(jobs, *refs):
    start, out = 0, sum(sum(counts) for counts, _ in jobs)
    for counts, form in jobs:
        row = 0
        for at, count in enumerate(counts):
            total = full(refs[start][...])
            for ref in refs[start + 1 : start + count]:
                total = total + full(ref[...])
            if form == "joined":
                refs[out][at] = low(total)
            elif form == "beside":
                refs[out][:, at] = low(total)
            elif form == "rows":
                refs[out][:, row : row + total.shape[1], :] = low(total)
                row += total.shape[1]
            else:
                refs[out + at][...] = low(total)
            start += count
        out += 1 if form else len(counts)


def add_up_far(depth, count, pos_ref, *refs):
    inputs, outs = refs[: 2 * count], refs[2 * count :]
    step = pl.program_id(0)
    for path in range(2):
        total = full(inputs[path * count][...])
        for ref in inputs[path * count + 1 : (path + 1) * count]:
            total = total + full(ref[...])
        for at in range(depth):

            @pl.when(step == at)
            def _():
                outs[at][path] = total[0].astype(outs[at].dtype)


def add_all(*refs):
    total = full(refs[0][...])
    for ref in refs[1:-1]:
        total = total + full(ref[...])
    refs[-1][...] = low(total)


def spread(depth, up_size, width, path, pos_ref, near_ref, far_ref, params_ref, small, sem):
    place = Place(pos_ref)
    rows = near_ref.shape[3] - SMALL
    for far_row, part in enumerate((near_ref.at[path], far_ref.at[path])):
        for level in range(depth):
            pltpu.make_async_copy(
                part.at[level, 0, pl.ds(rows, SMALL)], small.at[far_row, level], sem
            ).start()
    wait_all(small, sem)
    ups, others = 0.0, 0.0
    for far_row in range(2):
        for level in range(depth):
            shard = place.shard(level, far_row)
            block = full(small[far_row, level])
            up = jnp.concatenate([block, jnp.zeros((SMALL, 4 * WIDE - HALF), F32)], 1)
            ups += pltpu.roll(up, shard * up_size, 1)
            other = jnp.concatenate([block[:, :128], jnp.zeros((SMALL, WIDE - 128), F32)], 1)
            others += pltpu.roll(other, shard * width, 1)
    params_ref[...] = ups
    params_ref[1:9, :WIDE] = others[1:9]


VMEM = pltpu.MemorySpace.VMEM
SMEM = pltpu.MemorySpace.SMEM
ANY = pl.ANY
F32 = jnp.float32
BF16 = jnp.bfloat16


def call(kernel, spaces, outs, scratch, cost, after=(), limit=VMEM_LIMIT):
    run = pl.pallas_call(
        kernel,
        in_specs=[pl.BlockSpec(memory_space=space) for space in spaces + [ANY] * len(after)],
        out_specs=[pl.BlockSpec(memory_space=space) for _, _, space in outs],
        out_shape=[jax.ShapeDtypeStruct(shape, dtype) for shape, dtype, _ in outs],
        scratch_shapes=scratch,
        compiler_params=pltpu.CompilerParams(vmem_limit_bytes=limit),
        cost_estimate=pl.CostEstimate(flops=int(cost * COST), bytes_accessed=0, transcendentals=0),
    )
    return lambda *args: run(*args, *after)


def pass_through(*refs):
    pass


def tie(values, after):
    count = len(values)
    return pl.pallas_call(
        pass_through,
        in_specs=[pl.BlockSpec(memory_space=ANY)] * (count + len(after)),
        out_specs=[pl.BlockSpec(memory_space=ANY)] * count,
        out_shape=[jax.ShapeDtypeStruct(value.shape, value.dtype) for value in values],
        input_output_aliases={at: at for at in range(count)},
    )(*values, *after)


DMA = pltpu.SemaphoreType.DMA


class Sizes:
    def __init__(self, tokens, seqs, shards, rows, up_size, width):
        self.tokens, self.seqs, self.shards, self.rows = tokens, seqs, shards, rows
        self.up_size, self.width = up_size, width
        self.depth = shards // 2
        self.slots = tokens // seqs

    def columns(self, count):
        return pltpu.VMEM((count, self.depth, 2, self.rows, WIDE), BF16)

    def by_rows(self):
        return pltpu.VMEM((self.depth, 2, 4, self.rows, WIDE), BF16)

    def unit_grad(self, more=0):
        return [((2, 2, 2, self.depth, self.rows + more, HALF), BF16, ANY)] * 2


def run_attention_forward(z, pos, counts, x, group, params, after=()):
    t = z.tokens
    rows = [((t, WIDE), F32), ((t, WIDE), BF16), ((t, WIDE), F32), ((t, 128), F32)]
    panels = [((PAIRS, t, PAIR), BF16), ((3 * PAIRS, t, PAIR), BF16)]
    probs = ((z.seqs, PAIRS, z.slots, 2 * KEYS), BF16)
    return call(
        functools.partial(attention_forward, z.depth, z.seqs, len(after)),
        [SMEM, SMEM] + [ANY] * 12,
        [(*out, ANY) for out in rows + panels + [probs]],
        [
            pltpu.VMEM((t, WIDE), x.dtype),
            pltpu.VMEM((SMALL, WIDE), F32),
            *[pltpu.VMEM(*out) for out in rows + panels],
            z.columns(4),
            pltpu.VMEM(*probs),
            DMA,
            DMA,
            DMA((4,)),
            DMA,
            DMA,
            DMA((4,)),
            DMA,
        ],
        21,
        after,
    )(pos, counts, x, params, *group)


def run_mlp_forward(z, pos, first, group, params, after=()):
    t = z.tokens
    rows = [((t, WIDE), F32), ((t, WIDE), BF16), ((t, WIDE), F32), ((t, 128), F32)]
    tiles = [((4, t, WIDE), BF16)] * 2
    return call(
        functools.partial(mlp_forward, z.depth, len(after)),
        [SMEM] + [ANY] * 12,
        [(*out, ANY) for out in rows + tiles],
        [
            pltpu.VMEM((SMALL, 4 * WIDE), F32),
            *[pltpu.VMEM(*out) for out in rows],
            z.columns(4),
            z.by_rows(),
            pltpu.VMEM((2, t, WIDE), F32),
            pltpu.VMEM((t, WIDE), BF16),
            *[pltpu.VMEM(*out) for out in tiles],
            DMA,
            DMA,
            DMA((4,)),
            DMA((4,)),
            DMA,
            DMA,
            DMA,
        ],
        20,
        after,
    )(pos, first, params, *group)


def run_down_backward(z, pos, grad, hat, scale, params, act, after=()):
    t = z.tokens
    return call(
        functools.partial(down_backward, z.depth, len(after)),
        [SMEM] + [ANY] * 5,
        [
            ((t, WIDE), F32, ANY),
            ((8, WIDE), F32, ANY),
            *z.unit_grad(),
        ],
        [
            pltpu.VMEM((SMALL, WIDE), F32),
            pltpu.VMEM((8, WIDE), F32),
            pltpu.VMEM((t, WIDE), grad.dtype),
            pltpu.VMEM((t, WIDE), F32),
            pltpu.VMEM((t, 128), F32),
            pltpu.VMEM((t, WIDE), F32),
            pltpu.VMEM((4, t, WIDE), BF16),
            z.by_rows(),
            DMA,
            DMA,
            DMA((4,)),
            DMA((4,)),
            DMA,
            DMA,
        ],
        10,
        after,
    )(pos, params, grad, hat, scale, act)


def run_up_backward(z, pos, second, group, slope, first_low, hat, scale, params, after=()):
    t = z.tokens
    return call(
        functools.partial(up_backward, z.depth, len(after)),
        [SMEM] + [ANY] * 16,
        [
            ((t, WIDE), F32, ANY),
            ((8, WIDE), F32, ANY),
            ((1, 4 * WIDE), F32, ANY),
            *z.unit_grad(),
        ],
        [
            pltpu.VMEM((SMALL, WIDE), F32),
            pltpu.VMEM((8, WIDE), F32),
            pltpu.VMEM((1, 4 * WIDE), F32),
            z.columns(4),
            z.by_rows(),
            pltpu.VMEM((4, t, WIDE), BF16),
            pltpu.VMEM((t, WIDE), F32),
            pltpu.VMEM((t, WIDE), BF16),
            pltpu.VMEM((t, WIDE), F32),
            pltpu.VMEM((t, 128), F32),
            z.columns(4),
            DMA,
            DMA,
            DMA,
            DMA((4,)),
            DMA,
            DMA,
            DMA,
            DMA,
            DMA((4,)),
            DMA,
            DMA,
        ],
        19,
        after,
    )(pos, params, second, slope, first_low, hat, scale, *group)


def run_attention_backward(z, pos, grad, group, qkv, probs, after=()):
    t = z.tokens
    return call(
        functools.partial(attention_backward, z.depth, z.seqs, len(after)),
        [SMEM] + [ANY] * 13,
        [((3 * PAIRS, t, PAIR), BF16, ANY)],
        [
            pltpu.VMEM((z.depth, 2, z.rows, WIDE), BF16),
            pltpu.VMEM((t, WIDE), F32),
            pltpu.VMEM((3 * PAIRS, t, PAIR), BF16),
            pltpu.VMEM((z.seqs, PAIRS, z.slots, 2 * KEYS), BF16),
            pltpu.VMEM((PAIRS, t, PAIR), BF16),
            pltpu.VMEM((3 * PAIRS, t, PAIR), BF16),
            DMA,
            DMA,
            DMA,
            DMA,
            DMA,
        ],
        13,
        after,
    )(pos, grad, qkv, probs, *group)[0]


def run_qkv_weights(z, pos, grad, grads, ctx, x_low, down_sums, up_sums, up_bias, group=(), after=()):
    t = z.tokens
    more = [z.columns(3), DMA((3,)), DMA] if group else []
    return call(
        functools.partial(qkv_weights, z.depth, z.up_size, z.width, bool(group), len(after)),
        [SMEM] + [ANY] * (7 + len(group)),
        z.unit_grad(SMALL) + ([((t, WIDE), F32, ANY)] if group else []),
        [
            pltpu.VMEM((8, WIDE), F32),
            pltpu.VMEM((8, WIDE), F32),
            pltpu.VMEM((1, 4 * WIDE), F32),
            DMA((3,)),
            pltpu.VMEM((t, WIDE), F32),
            pltpu.VMEM((3 * PAIRS, t, PAIR), BF16),
            pltpu.VMEM((PAIRS, t, PAIR), BF16),
            pltpu.VMEM((t, WIDE), BF16),
            z.columns(4),
            pltpu.VMEM((8, WIDE), F32),
            pltpu.VMEM((SMALL, HALF), F32),
            pltpu.VMEM((z.depth, 2, SMALL, HALF), BF16),
            DMA,
            DMA((3,)),
            DMA,
            DMA,
            DMA,
            DMA,
            *more,
        ],
        8,
        after,
    )(pos, down_sums, up_sums, up_bias, grad, grads, ctx, x_low, *group)


def run_qkv_backward(z, pos, grad, grads, group, after=()):
    t = z.tokens
    return call(
        functools.partial(qkv_backward, z.depth, len(after)),
        [SMEM] + [ANY] * 12,
        [((t, WIDE), F32, ANY)],
        [
            pltpu.VMEM((t, WIDE), F32),
            z.columns(3),
            pltpu.VMEM((3 * PAIRS, t, PAIR), BF16),
            DMA((3,)),
            DMA,
            DMA,
            DMA,
        ],
        6,
        after,
    )(pos, grad, grads, *group)[0]


def run_finish_first(z, pos, quarters, after=()):
    r = z.rows
    return call(
        functools.partial(finish_first, len(after)),
        [SMEM] + [VMEM] * (4 * LAYERS),
        [
            ((LAYERS, r, 3 * WIDE), F32, VMEM),
            ((LAYERS, r, WIDE), F32, VMEM),
            ((LAYERS, z.up_size), F32, VMEM),
            ((6, LAYERS, z.width), F32, VMEM),
            ((LAYERS, 2, z.width), F32, VMEM),
        ],
        [],
        3,
        after,
        limit=SMALL_LIMIT,
    )(pos, *quarters)


def run_finish_second(z, pos, quarters, after=()):
    r = z.rows
    return call(
        functools.partial(finish_second, len(after)),
        [SMEM] + [VMEM] * (4 * LAYERS),
        [
            ((LAYERS, r, 4 * WIDE), F32, VMEM),
            ((LAYERS, 4 * r, WIDE), F32, VMEM),
        ],
        [],
        5,
        after,
        limit=SMALL_LIMIT,
    )(pos, *quarters)


def run_prepare(z, pos, *arrays):
    r = z.rows
    return call(
        prepare,
        [SMEM] + [ANY] * 4 + [VMEM] * 3,
        [
            ((2, 1, r + SMALL, HALF), BF16, VMEM),
            ((2, 2, r, HALF), BF16, VMEM),
            ((2, 3, r, HALF), BF16, VMEM),
        ],
        [
            pltpu.VMEM((SMALL, HALF), F32),
            DMA((LAYERS, 3, 2)),
        ],
        1,
        limit=SMALL_LIMIT,
    )(pos, *arrays)


def run_columns_of(pos, pieces):
    depth, shape = len(pieces), pieces[0].shape
    return call(
        functools.partial(columns_of, depth),
        [SMEM] + [VMEM] * depth,
        [((2, depth) + shape[1:], BF16, VMEM)],
        [],
        2,
    )(pos, *pieces)[0]


def run_split_columns(column, sizes):
    depth, _, _, *rest = column.shape
    outs = [((2, depth, size, *rest), BF16, VMEM) for size in sizes]
    return call(functools.partial(split_columns, sizes), [VMEM], outs, [], 2)(column)


def add_specs(sums, size, place):
    specs = []
    for parts in sums:
        for array, lead in parts:
            rest = array.shape[len(lead) + 1 :]
            specs.append(
                pl.BlockSpec(
                    (None,) * len(lead) + (size,) + rest,
                    lambda *at, lead=lead, rest=len(rest): lead + (place(*at),) + (0,) * rest,
                )
            )
    return specs


def run_add_up(jobs):
    specs, arrays, outs, out_specs = [], [], [], []
    for sums, form in jobs:
        array, lead = sums[0][0]
        depth, *rest = array.shape[len(lead) :]
        size, count = depth // 2, len(sums)
        specs += add_specs(sums, size, lambda step: step)
        arrays += [array for parts in sums for array, _ in parts]
        if form == "joined":
            outs.append((count, depth, *rest))
            out_specs.append(pl.BlockSpec((count, size, *rest), lambda step: (0, step, 0, 0)))
        elif form == "rows":
            rows = sum(parts[0][0].shape[-2] for parts in sums)
            outs.append((depth, rows, HALF))
            out_specs.append(pl.BlockSpec((size, rows, HALF), lambda step: (step, 0, 0)))
        elif form == "beside":
            outs.append((depth, count, *rest))
            out_specs.append(pl.BlockSpec((size, count, *rest), lambda step: (step, 0, 0, 0)))
        else:
            outs += [(depth, *rest)] * count
            out_specs += [
                pl.BlockSpec((size, *rest), lambda step, zeros=(0,) * len(rest): (step,) + zeros)
            ] * count
    results = list(
        pl.pallas_call(
            functools.partial(add_up, [([len(parts) for parts in sums], form) for sums, form in jobs]),
            grid=(2,),
            in_specs=specs,
            out_specs=out_specs,
            out_shape=[jax.ShapeDtypeStruct(out, BF16) for out in outs],
            compiler_params=pltpu.CompilerParams(vmem_limit_bytes=SMALL_LIMIT),
            cost_estimate=pl.CostEstimate(flops=int(3 * COST), bytes_accessed=0, transcendentals=0),
        )(*arrays)
    )
    grouped = []
    for sums, form in jobs:
        count = 1 if form else len(sums)
        grouped.append(results[:count])
        results = results[count:]
    return grouped


def run_add_up_far(pos, sums):
    array, lead = sums[0][0]
    depth, *rest = array.shape[len(lead) :]
    outs = [jax.ShapeDtypeStruct((2, *rest), F32 if at == 0 else BF16) for at in range(depth)]
    return pl.pallas_call(
        functools.partial(add_up_far, depth, len(sums[0])),
        grid_spec=pltpu.PrefetchScalarGridSpec(
            num_scalar_prefetch=1,
            grid=(depth,),
            in_specs=add_specs(sums, 1, lambda step, pos_ref: lax.rem(pos_ref[3] + step, depth)),
            out_specs=[pl.BlockSpec(out.shape, lambda step, pos_ref: (0, 0, 0)) for out in outs],
        ),
        out_shape=outs,
        compiler_params=pltpu.CompilerParams(vmem_limit_bytes=SMALL_LIMIT),
        cost_estimate=pl.CostEstimate(flops=int(3 * COST), bytes_accessed=0, transcendentals=0),
    )(pos, *[array for parts in sums for array, _ in parts])


def run_add_all(arrays):
    return call(add_all, [VMEM] * len(arrays), [(arrays[0].shape, BF16, VMEM)], [], 1, limit=SMALL_LIMIT)(*arrays)[0]


def run_spread(z, pos, near, far, path):
    return call(
        functools.partial(spread, z.depth, z.up_size, z.width, path),
        [SMEM, ANY, ANY],
        [((SMALL, 4 * WIDE), F32, VMEM)],
        [pltpu.VMEM((2, z.depth, SMALL, HALF), BF16), DMA],
        2,
        limit=SMALL_LIMIT,
    )(pos, near, far)[0]


class Links:
    def __init__(self, rep_size, fsdp_size):
        self.rep_size, self.fsdp_size = rep_size, fsdp_size
        self.depth = fsdp_size // 2
        rep_at, fsdp_at = lax.axis_index("rep"), lax.axis_index("fsdp")
        self.core, self.side = rep_at % 2, (rep_at // 2) % 2
        self.row, self.level = fsdp_at % 2, fsdp_at // 2

    def permute(self, value, target):
        pairs = []
        for rep_at in range(self.rep_size):
            for fsdp_at in range(self.fsdp_size):
                to_rep, to_fsdp = target(rep_at, fsdp_at)
                pairs.append((rep_at * self.fsdp_size + fsdp_at, to_rep * self.fsdp_size + to_fsdp))
        return lax.ppermute(value, AXES, pairs)

    def other_core(self, value):
        return self.permute(value, lambda r, f: (r ^ 1, f))

    def other_side(self, value):
        return self.permute(value, lambda r, f: (r ^ 2, f))

    def other_row(self, value):
        return self.permute(value, lambda r, f: (r, f ^ 1))

    def level_up(self, value, step):
        return self.permute(value, lambda r, f: (r, ((f // 2 + step) % self.depth) * 2 + f % 2))

    def levels(self):
        return [list(range(row, self.fsdp_size, 2)) for row in range(2)]


class Gather:
    def __init__(self, name, links, columns):
        self.name, self.links, self.live, self.moving = name, links, [columns], []

    def scope(self, stage):
        return jax.named_scope("gather_" + self.name + "_" + stage)

    def first(self):
        with self.scope("first"):
            self.moving = [self.links.other_row(self.live[0]), self.links.other_side(self.live[0])]

    def second(self):
        self.live += self.moving
        with self.scope("second"):
            rows, sides = self.live[1:3]
            self.moving = [self.links.other_side(rows[0]), self.links.other_row(sides[1])]
        with self.scope("cores"):
            self.moving += [self.links.other_core(part) for part in self.live[:3]]

    def last(self):
        self.live += self.moving[:2]
        self.far = self.moving[2:]
        with self.scope("last"):
            self.moving = [self.links.other_core(part) for part in self.live[3:5]]

    def arrays(self):
        return self.live + self.far + self.moving


class Sum:
    def __init__(self, name, links, near, far):
        self.name, self.links, self.near, self.sends = name, links, near, [far]
        self.hops = ((links.other_row, links.other_side), (links.other_side, links.other_row))

    def scope(self, stage):
        return jax.named_scope("sum_" + self.name + "_" + stage)

    def cores(self):
        with self.scope("cores"):
            self.moving = [self.links.other_core(self.sends[0])]

    def at(self, far):
        return [[(array, lead + (far,)) for array, lead in parts] for parts in self.parts]

    def came(self):
        self.parts = [[(self.near, (path,)), (self.moving[0], (path,))] for path in range(2)]
        return [(self.at(1), None)]

    def first(self):
        with self.scope("first"):
            self.moving = [self.hops[path][0](self.sends[path]) for path in range(2)]


class Second:
    def __init__(self, name, links, sums):
        self.name, self.links, self.sums = name, links, sums

    def came(self):
        for one in self.sums:
            one.parts = [parts + [(move, ())] for parts, move in zip(one.at(0), one.moving)]
        return [([one.at(1)[path] for one in self.sums], "joined") for path in range(2)]

    def second(self):
        with jax.named_scope("sum_" + self.name + "_second"):
            self.moving = [hops[1](send) for hops, send in zip(self.sums[0].hops, self.sends)]


def add(*steps):
    jobs = [step.came() for step in steps]
    with jax.named_scope("add_" + "_".join(step.name for step in steps)):
        outs = run_add_up([job for step_jobs in jobs for job in step_jobs])
    for step, step_jobs in zip(steps, jobs):
        step.sends = [out for group in outs[: len(step_jobs)] for out in group]
        outs = outs[len(step_jobs) :]


class Share:
    def __init__(self, name, links, second):
        self.name, self.links, self.second = name, links, second

    def scope(self):
        return jax.named_scope("share_" + self.name)

    def parts(self):
        return [
            one.at(0)[path] + [(self.second.moving[path], (unit,))]
            for unit, one in enumerate(self.second.sums)
            for path in range(2)
        ]

    def came(self):
        return [(self.parts(), "beside")]

    def scatter(self):
        with self.scope():
            self.sends = [
                lax.psum_scatter(
                    self.sends[0], "fsdp", scatter_dimension=0, axis_index_groups=self.links.levels()
                )
            ]

    def add_far(self, pos):
        with self.scope():
            self.kept, *self.sends = run_add_up_far(pos, self.parts())

    def levels(self):
        with self.scope():
            self.moving = [self.links.level_up(send, at + 1) for at, send in enumerate(self.sends)]

    def after_levels(self):
        with self.scope():
            self.sends = [run_add_all([self.kept] + self.moving)]

    def copies(self):
        if self.links.rep_size > 4:
            groups = [list(range(first, self.links.rep_size, 4)) for first in range(4)]
            self.sends = [lax.psum(self.sends[0], "rep", axis_index_groups=groups)]

    def sides(self):
        with self.scope():
            self.sends += [self.links.other_side(self.sends[0])]

    def last(self):
        with self.scope():
            self.moving = [self.links.other_core(send) for send in self.sends]

    def quarters(self):
        return self.sends + self.moving


class Mixed(Share):
    def __init__(self, name, links, seconds):
        super().__init__(name, links, None)
        self.seconds = seconds

    def came(self):
        parts = []
        for self.second in self.seconds:
            parts += self.parts()
        return [(parts, "rows")]


def order(steps, after=()):
    names = ("live", "moving", "sends")
    held = [(step, name) for step in steps for name in (names[:2] if hasattr(step, "live") else names[2:])]
    values = [value for step, name in held for value in getattr(step, name)]
    values = list(tie(values, list(after)))
    token = min(values, key=lambda value: value.size)
    for step, name in held:
        size = len(getattr(step, name))
        setattr(step, name, values[:size])
        values = values[size:]
    return [token]


def shards(
    rep_size, fsdp_size, hidden, region_counts, w_qkv, w_out, w_up, w_down, bias_up, biases, norm_gains, cotangent
):
    links = Links(rep_size, fsdp_size)
    z = Sizes(
        hidden.shape[0], region_counts.shape[0], fsdp_size, w_qkv.shape[1], bias_up.shape[1], biases.shape[2]
    )
    pos = jnp.stack([links.core, links.side, links.row, links.level]).astype(jnp.int32)
    quarters = run_prepare(
        z, pos, w_qkv, w_out, w_up, w_down, bias_up, jnp.transpose(biases, (1, 0, 2)), norm_gains
    )
    kept, groups, params = [], [None] * 4, [None] * 2

    def run_first(layer, states, after):
        return run_attention_forward(z, pos, region_counts, states, groups[2 * layer], params[layer], after)

    def run_second(layer, first, after):
        return run_mlp_forward(z, pos, first, groups[2 * layer + 1], params[layer], after)

    def columns(name, quarter, after=()):
        with jax.named_scope("columns_" + name):
            if after:
                quarter = tie([quarter], list(after))[0]
            pieces = [quarter] + [links.level_up(quarter, step) for step in range(1, links.depth)]
            return run_columns_of(pos, pieces)

    first_0 = Gather("first0", links, columns("first0", quarters[0]))
    first_0.first()
    second_0 = Gather("second0", links, columns("second0", quarters[1], first_0.live))

    order([first_0])
    first_0.second()

    second_0.first()
    order([first_0])
    first_0.last()
    with jax.named_scope("columns_third"):
        third = tie([quarters[2]], first_0.live[1:3])[0]
        third = lax.all_gather(third, "fsdp", axis_index_groups=links.levels())
    params = [run_spread(z, pos, *first_0.live[:2], layer) for layer in range(LAYERS)]
    groups[0] = first_0.arrays()
    one = run_first(0, hidden, params[1:])

    order([second_0], one[3:4])
    second_0.second()
    with jax.named_scope("columns_third"):
        third = run_split_columns(third, (1, 2))
    first_1, second_1 = (Gather(name, links, part) for name, part in zip(("first1", "second1"), third))

    first_1.first()

    order([second_0, second_1])
    second_0.last()
    second_1.first()
    groups[1] = second_0.arrays()
    two = run_second(0, one[0], ())
    kept.append((hidden, one, two))

    order([first_1], two[3:4])
    first_1.second()

    order([first_1, second_1])
    first_1.last()
    second_1.second()
    groups[2] = first_1.arrays()
    one = run_first(1, two[0], ())

    order([second_1], one[3:4])
    second_1.last()
    groups[3] = second_1.arrays()
    low_states = two[1]
    two = run_second(1, one[0], ())
    kept.append((low_states, one, two))
    output = two[1]

    def run_down(layer, gradient, after):
        _, _, hat, scale, act, _ = kept[layer][2]
        return run_down_backward(z, pos, gradient, hat, scale, params[layer], act, after)

    def run_up(layer, second, after):
        _, first_low, hat, scale, *_ = kept[layer][1]
        return run_up_backward(
            z, pos, second, groups[2 * layer + 1], kept[layer][2][5], first_low, hat, scale, params[layer], after
        )

    def run_attention(layer, first_in, after):
        qkv, probs = kept[layer][1][5:7]
        return run_attention_backward(z, pos, first_in, groups[2 * layer], qkv, probs, after)

    def run_weights(layer, first_in, grads, small, group, after):
        return run_qkv_weights(z, pos, first_in, grads, kept[layer][1][4], kept[layer][0], *small, group, after)

    def run_states(layer, first_in, grads, after):
        return run_qkv_backward(z, pos, first_in, grads, groups[2 * layer], after)

    second, down_sums, near, far = run_down(1, cotangent, ())
    down_1 = Sum("down1", links, near, far)

    token = order([down_1])
    down_1.cores()
    first_in, up_sums, up_bias, near, far = run_up(1, second, token)
    up_1 = Sum("up1", links, near, far)

    add(down_1)
    token = order([down_1, up_1])
    down_1.first()
    up_1.cores()
    grads = run_attention(1, first_in, token)

    add(up_1)
    token = order([up_1], [grads] + down_1.moving)
    up_1.first()
    near, far, gradient = run_weights(1, first_in, grads, (down_sums, up_sums, up_bias), groups[2], token)
    first_1 = Sum("first1", links, near, far)

    second_1 = Second("second1", links, [up_1, down_1])
    add(second_1)
    token = order([second_1, first_1], [gradient])
    second_1.second()
    first_1.cores()
    second, down_sums, near, far = run_down(0, gradient, token)
    down_0 = Sum("down0", links, near, far)

    share_second_1 = Share("second1", links, second_1)
    order([down_0], second_1.moving + first_1.moving)
    down_0.cores()
    add(first_1, share_second_1)
    order([first_1, share_second_1])
    first_1.first()
    share_second_1.scatter()
    add(down_0)
    token = order([down_0])
    down_0.first()
    first_in, up_sums, up_bias, near, far = run_up(0, second, token)
    up_0 = Sum("up0", links, near, far)

    first_second_1 = Second("first1", links, [first_1])
    order([up_0], first_1.moving + down_0.moving)
    up_0.cores()
    add(first_second_1)
    order([first_second_1])
    first_second_1.second()
    add(up_0)
    token = order([up_0])
    up_0.first()
    grads = run_attention(0, first_in, token)

    second_0 = Second("second0", links, [up_0, down_0])
    add(second_0)
    token = order([second_0], [grads] + first_second_1.moving)
    second_0.second()
    near, far = run_weights(0, first_in, grads, (down_sums, up_sums, up_bias), (), token)
    first_0 = Sum("first0", links, near, far)

    mixed = Mixed("mixed", links, [first_second_1, second_0])
    order([first_0], second_0.moving)
    first_0.cores()
    add(mixed)
    order([mixed])
    mixed.scatter()
    add(first_0)
    token = order([first_0])
    first_0.first()
    gradient = run_states(0, first_in, grads, token)

    first_second_0 = Second("first0", links, [first_0])
    first_0.moving = list(tie(first_0.moving, [gradient]))
    add(first_second_0)
    order([first_second_0])
    first_second_0.second()

    share_first_0 = Share("first0", links, first_second_0)
    share_first_0.add_far(pos)
    mixed.copies()
    share_second_1.copies()
    order([share_first_0, mixed, share_second_1])
    share_first_0.levels()
    mixed.sides()
    share_second_1.sides()

    share_first_0.after_levels()
    share_first_0.copies()
    order([share_first_0, mixed, share_second_1])
    share_first_0.sides()
    mixed.last()
    share_second_1.last()

    order([share_first_0], mixed.moving + share_second_1.moving)
    share_first_0.last()
    up_grad, down_grad = run_finish_second(z, pos, mixed.quarters() + share_second_1.quarters())
    qkv_grad, out_grad, up_bias_grad, biases_grad, gains_grad = run_finish_first(
        z, pos, share_first_0.quarters() + mixed.quarters(), [up_grad]
    )
    biases_grad = jnp.transpose(biases_grad, (1, 0, 2))
    return output, gradient, qkv_grad, out_grad, up_grad, down_grad, up_bias_grad, biases_grad, gains_grad


def solution(mesh):
    in_specs = (
        P(("rep", "fsdp"), None),
        P(("rep", "fsdp")),
        P(None, "fsdp", None),
        P(None, "fsdp", None),
        P(None, "fsdp", None),
        P(None, "fsdp", None),
        P(None, "fsdp"),
        P(None, None, "fsdp"),
        P(None, None, "fsdp"),
        P(("rep", "fsdp"), None),
    )
    out_specs = (
        P(("rep", "fsdp"), None),
        P(("rep", "fsdp"), None),
        P(None, "fsdp", None),
        P(None, "fsdp", None),
        P(None, "fsdp", None),
        P(None, "fsdp", None),
        P(None, "fsdp"),
        P(None, None, "fsdp"),
        P(None, None, "fsdp"),
    )
    local = functools.partial(shards, mesh.shape["rep"], mesh.shape["fsdp"])
    return jax.shard_map(local, mesh=mesh, in_specs=in_specs, out_specs=out_specs, check_vma=False)
```
